128 devices in a mesh: dp: 8 (over y_lo, z), ctx: 8 (over x, y_hi), tp: 2 (over core).
Axes of the slice: x: 4, y: 4 (y_hi: 2, y_lo: 2; y = y_hi * 2 + y_lo), z: 4, core: 2. Of those that a mesh axis runs over, the one named last changes fastest.
Arguments:
- block_input: bfloat16 [8192, 2048], P(('dp', 'ctx')), may hold values from -6 to 6
- out_cotangent: bfloat16 [8192, 2048], P(('dp', 'ctx')), may hold values from -6 to 6
- token_order: int32 [8, 1024], P('dp', 'ctx'), may hold values from 0 to 1023, each once within a row
- seq_lengths: int32 [8, 4], P('dp'), may hold values from 1 to 768, 1024 in all within a row
- w_qkv: float32 [2048, 3, 2048], P(('dp', 'ctx'), None, 'tp'), may hold values from -0.125 to 0.125
- w_out: float32 [2, 1024, 2048], P('tp', ('dp', 'ctx')), may hold values from -1 to 1
- w_fc1: float32 [2048, 8192], P(('dp', 'ctx'), 'tp'), may hold values from -0.125 to 0.125
- w_fc2: float32 [2, 4096, 2048], P('tp', ('dp', 'ctx')), may hold values from -0.0625 to 0.0625
- vectors: float32 [11, 2048], replicated, may hold values from -0.9 to 1.3, as said below
- mom1_qkv: float32 [2048, 3, 2048], P(('dp', 'ctx'), None, 'tp'), may hold values from -32 to 32
- mom1_out: float32 [2, 1024, 2048], P('tp', ('dp', 'ctx')), may hold values from -4 to 4
- mom1_fc1: float32 [2048, 8192], P(('dp', 'ctx'), 'tp'), may hold values from -16 to 16
- mom1_fc2: float32 [2, 4096, 2048], P('tp', ('dp', 'ctx')), may hold values from -32 to 32
- mom1_vec: float32 [11, 2048], replicated, may hold values from -64 to 64
- mom2_qkv: float32 [2048, 3, 2048], P(('dp', 'ctx'), None, 'tp'), may hold values from 54.0672 to 860.16
- mom2_out: float32 [2, 1024, 2048], P('tp', ('dp', 'ctx')), may hold values from 3.328 to 53.76
- mom2_fc1: float32 [2048, 8192], P(('dp', 'ctx'), 'tp'), may hold values from 13.1072 to 212.992
- mom2_fc2: float32 [2, 4096, 2048], P('tp', ('dp', 'ctx')), may hold values from 77.0048 to 1228.8
- mom2_vec: float32 [11, 2048], replicated, may hold values from 212.992 to 3440.64
Outputs:
- block_output: bfloat16 [8192, 2048], P(('dp', 'ctx'))
- input_grad: float32 [8192, 2048], P(('dp', 'ctx'))
- new_w_qkv: float32 [2048, 3, 2048], P(('dp', 'ctx'), None, 'tp')
- new_w_out: float32 [2, 1024, 2048], P('tp', ('dp', 'ctx'))
- new_w_fc1: float32 [2048, 8192], P(('dp', 'ctx'), 'tp')
- new_w_fc2: float32 [2, 4096, 2048], P('tp', ('dp', 'ctx'))
- new_vectors: float32 [11, 2048], replicated
- new_mom1_qkv: float32 [2048, 3, 2048], P(('dp', 'ctx'), None, 'tp')
- new_mom1_out: float32 [2, 1024, 2048], P('tp', ('dp', 'ctx'))
- new_mom1_fc1: float32 [2048, 8192], P(('dp', 'ctx'), 'tp')
- new_mom1_fc2: float32 [2, 4096, 2048], P('tp', ('dp', 'ctx'))
- new_mom1_vec: float32 [11, 2048], replicated
- new_mom2_qkv: float32 [2048, 3, 2048], P(('dp', 'ctx'), None, 'tp')
- new_mom2_out: float32 [2, 1024, 2048], P('tp', ('dp', 'ctx'))
- new_mom2_fc1: float32 [2048, 8192], P(('dp', 'ctx'), 'tp')
- new_mom2_fc2: float32 [2, 4096, 2048], P('tp', ('dp', 'ctx'))
- new_mom2_vec: float32 [11, 2048], replicated
The draws below stay inside these ranges and needn't reach their ends.
Inputs may be any that keep to these rules, and one draw needn't show every extreme that they name: `token_order`: each row holds every number of 0 to 1023 once. `seq_lengths`: each row sums to 1024; its largest entry is 768. `vectors`: row 9 lies near one.
All inputs are finite; a program needn't handle non-finite values.
Results may differ from the reference program's by a relative error of at most 0.02.
Values may be sent and summed in bfloat16 or wider, within the bound.
No kernel may reach another device: no remote copies, remote signals or barrier semaphores. Data moves between devices by JAX's collectives and lax.ppermute only.
A program may use at most 256 MiB of HBM per device.

```python
import math
import jax
import jax.numpy as jnp
import numpy as np
from jax import lax

D = 2048
FF = 8192
HD = 64
ROT = 32
TOK_DEV = 128
SEQS = 4
STEP = 10
VECS = 11
GROUP = 1024
LONGEST = 768
TOKENS = 8192
KEFF = 64
N_DP = 8
N_CTX = 8
N_TP = 2


def draw_vectors(key, part):
    key = jax.random.fold_in(key, 11)
    base = jnp.clip(0.3 * jax.random.normal(key, (VECS, D), jnp.float32), -0.9, 0.9)
    row_index = jnp.arange(VECS)[:, None]
    return jnp.where(row_index == 9, 1.0 + 0.3 * base, base)


def shard_levels(key, extent, split, smallest, largest):
    factor_of = 1.0
    for dim, shards_of in split:
        heights = jax.random.uniform(jax.random.fold_in(jax.random.fold_in(key, 6), dim), (shards_of,), jnp.float32, smallest / len(split), largest / len(split))
        factor_of = factor_of * jnp.repeat(jnp.exp(heights), extent[dim] // shards_of).reshape((-1,) + (1,) * (len(extent) - 1 - dim))
    return factor_of


def length_profile(count, total, limit, slope):
    weights = [(1 << 20) // math.isqrt(standing ** slope) + 1 for standing in range(2, count + 1)]
    rest, holding = total - limit - (count - 1), [1] * (count - 1)
    while rest > 0:
        free = [i for i in range(count - 1) if holding[i] < limit]
        mass, remaining = sum([weights[i] for i in free]), rest
        for i in free:
            addition = min(limit - holding[i], max(1, remaining * weights[i] // mass), rest)
            holding[i] = holding[i] + addition
            rest = rest - addition
    return np.array([limit] + holding)


def ragged(stream_key, count, total, bound, skew):
    if count == 2:
        one = jax.random.randint(stream_key, (), max(1, total - bound), min(bound, total - 1) + 1)
        return jnp.stack([one, total - one])
    lengths = jnp.asarray(length_profile(count, total, bound, skew), jnp.int32)
    pairs = (count - 1) // 2
    donor, taker = lengths[1:1 + 2 * pairs:2], lengths[2:2 + 2 * pairs:2]
    slack = jnp.minimum(donor - 1, bound - taker)
    passed = jax.random.randint(jax.random.fold_in(stream_key, 1), (pairs,), 0, 1 << 20) % (slack + 1)
    lengths = lengths.at[1:1 + 2 * pairs:2].set(donor - passed).at[2:2 + 2 * pairs:2].set(taker + passed)
    return lengths[jax.random.permutation(jax.random.fold_in(stream_key, 2), count)]


def gaussian(own_key, shape, width, most, cuts=(), kind=jnp.bfloat16):
    values = jax.random.normal(own_key, shape, jnp.float32) * width
    if len(cuts) > 0:
        values = shard_levels(own_key, shape, cuts, -0.22, 0.18) * values
    return jnp.clip(values, min=-most, max=most).astype(kind)


def setup_inputs(seed: int = 0) -> dict:
    arg_keys = jax.random.split(jax.random.key(seed), 20)
    return {
        "block_input": gaussian(arg_keys[0], (TOKENS, D), 1.0, 6.0, ((0, 64),)),
        "out_cotangent": gaussian(arg_keys[1], (TOKENS, D), 1.0, 6.0, ((0, 64),)),
        "token_order": jax.vmap(lambda own: jax.random.permutation(own, GROUP))(jax.random.split(arg_keys[2], N_DP)).reshape((N_DP, GROUP)).astype(jnp.int32),
        "seq_lengths": jax.vmap(lambda own: ragged(own, SEQS, GROUP, LONGEST, 2))(jax.random.split(arg_keys[3], N_DP)).reshape((N_DP, SEQS)).astype(jnp.int32),
        "w_qkv": gaussian(arg_keys[4], (D, 3, D), D ** -0.5, 0.125, ((0, 64), (2, 2)), jnp.float32),
        "w_out": gaussian(arg_keys[5], (N_TP, D // N_TP, D), (D // KEFF) ** -0.5, 1.0, ((0, 2), (1, 64)), jnp.float32),
        "w_fc1": gaussian(arg_keys[6], (D, FF), D ** -0.5, 0.125, ((0, 64), (1, 2)), jnp.float32),
        "w_fc2": gaussian(arg_keys[7], (N_TP, FF // N_TP, D), FF ** -0.5, 0.0625, ((0, 2), (1, 64)), jnp.float32),
        "vectors": draw_vectors(jax.random.fold_in(arg_keys[19], 71), 0),
        "mom1_qkv": gaussian(arg_keys[9], (D, 3, D), (0.055 * TOKENS ** 0.5), 32.0, ((0, 64), (2, 2)), jnp.float32),
        "mom1_out": gaussian(arg_keys[10], (N_TP, D // N_TP, D), (0.11 * (TOKENS * KEFF ** -1) ** 0.5), 4.0, ((0, 2), (1, 64)), jnp.float32),
        "mom1_fc1": gaussian(arg_keys[11], (D, FF), (0.0275 * TOKENS ** 0.5), 16.0, ((0, 64), (1, 2)), jnp.float32),
        "mom1_fc2": gaussian(arg_keys[12], (N_TP, FF // N_TP, D), (0.066 * TOKENS ** 0.5), 32.0, ((0, 2), (1, 64)), jnp.float32),
        "mom1_vec": gaussian(arg_keys[13], (VECS, D), (0.11 * TOKENS ** 0.5), 64.0, (), jnp.float32),
        "mom2_qkv": jnp.clip(jnp.exp(math.log(860.16) - 2.7668907 * jax.random.uniform(arg_keys[14], (D, 3, D), jnp.float32) ** shard_levels(arg_keys[14], (D, 3, D), ((0, 64), (2, 2)), -0.2, 0.2)), 54.0672, 860.16),
        "mom2_out": jnp.clip(jnp.exp(math.log(53.76) - 2.7821581 * jax.random.uniform(arg_keys[15], (N_TP, D // N_TP, D), jnp.float32) ** shard_levels(arg_keys[15], (N_TP, D // N_TP, D), ((0, 2), (1, 64)), -0.2, 0.2)), 3.328, 53.76),
        "mom2_fc1": jnp.clip(jnp.exp(math.log(212.992) - 2.78809295 * jax.random.uniform(arg_keys[16], (D, FF), jnp.float32) ** shard_levels(arg_keys[16], (D, FF), ((0, 64), (1, 2)), -0.2, 0.2)), 13.1072, 212.992),
        "mom2_fc2": jnp.clip(jnp.exp(math.log(1228.8) - 2.7699257 * jax.random.uniform(arg_keys[17], (N_TP, FF // N_TP, D), jnp.float32) ** shard_levels(arg_keys[17], (N_TP, FF // N_TP, D), ((0, 2), (1, 64)), -0.2, 0.2)), 77.0048, 1228.8),
        "mom2_vec": jnp.clip(jnp.exp(jax.random.uniform(arg_keys[18], (VECS, D), jnp.float32, math.log(212.992), math.log(3440.64))), 212.992, 3440.64),
    }


@jax.custom_vjp
def low(v):
    return lax.optimization_barrier(v.astype(jnp.bfloat16)).astype(jnp.float32)

@jax.custom_vjp
def low_back(v):
    return v

def low_keep(v):
    return (low(v), None)

def low_pass(kept, grad):
    return (grad,)

def back_keep(v):
    return (v, None)

def back_low(kept, grad):
    return (low(grad),)
low.defvjp(low_keep, low_pass)
low_back.defvjp(back_keep, back_low)
NORM_EPS = 1e-05
SCORE_SCALE = 0.125
MASKED = -1e+30
ROPE_BASE = 10000.0
BETA_ONE = 0.9
BETA_TWO = 0.95
ADAM_EPS = 1e-08
WEIGHT_DECAY = 0.1
HIGHEST = lax.Precision.HIGHEST

def places(order_row, length_row):
    seq_ends = jnp.cumsum(length_row).astype(jnp.int32)
    seq_starts = (seq_ends - length_row).astype(jnp.int32)
    inside = (order_row[:, None] >= seq_starts[None, :]) & (order_row[:, None] < seq_ends[None, :])
    doc_ids = lax.optimization_barrier(jnp.sum((order_row[:, None] >= seq_ends[None, :]).astype(jnp.int32), axis=1))
    seq_first = lax.optimization_barrier(jnp.sum(jnp.where(inside, seq_starts[None, :], 0), axis=1))
    return (doc_ids.astype(jnp.int32), (order_row - seq_first).astype(jnp.int32))

def angles(positions):
    half_rot = ROT // 2
    inverse = ROPE_BASE ** (-(2.0 * jnp.arange(half_rot, dtype=jnp.float32)) / ROT)
    rotation = positions.astype(jnp.float32)[:, None] * inverse[None, :]
    return (jnp.cos(rotation)[:, None, :], jnp.sin(rotation)[:, None, :])

def rotate(features, cos_table, sin_table):
    half_rot = ROT // 2
    first_half = features[..., :half_rot]
    second = features[..., half_rot:ROT]
    return jnp.concatenate([first_half * cos_table - second * sin_table, second * cos_table + first_half * sin_table, features[..., ROT:]], axis=-1)

def layer_group(weights, x_group, doc_ids, positions):
    w_qkv, w_out, w_fc1, w_fc2, vectors = weights
    group_rows = x_group.shape[0]
    heads = D // HD
    row_mean = lax.optimization_barrier(jnp.mean(x_group, axis=-1, keepdims=True))
    centered = x_group - row_mean
    row_var = lax.optimization_barrier(jnp.mean(centered * centered, axis=-1, keepdims=True))
    normed = low(centered * lax.rsqrt(row_var + NORM_EPS) * vectors[9] + vectors[10])
    projected = jnp.einsum('nd,dcf->ncf', normed, low(w_qkv), precision=HIGHEST) + vectors[0:3][None]
    projected = low_back(projected)
    cos_table, sin_table = angles(positions)
    query = low(rotate(projected[:, 0].reshape(group_rows, heads, HD), cos_table, sin_table))
    key_rot = low(rotate(projected[:, 1].reshape(group_rows, heads, HD), cos_table, sin_table))
    value = low(projected[:, 2].reshape(group_rows, heads, HD))
    attn_mask = (doc_ids[:, None] == doc_ids[None, :]) & (positions[None, :] <= positions[:, None])

    def one_head(pieces):
        query_head, key_head, value_head = pieces
        scores = low_back(jnp.dot(query_head, key_head.T, precision=HIGHEST) * SCORE_SCALE)
        scores = jnp.where(attn_mask, scores, MASKED)
        row_top = lax.optimization_barrier(jnp.max(scores, axis=-1, keepdims=True))
        attn_probs = jnp.where(attn_mask, jnp.exp(scores - row_top), 0.0)
        attn_probs = attn_probs / lax.optimization_barrier(jnp.sum(attn_probs, axis=-1, keepdims=True))
        return jnp.dot(low(attn_probs), value_head, precision=HIGHEST)
    mixed = lax.map(jax.checkpoint(one_head), (query.transpose(1, 0, 2), key_rot.transpose(1, 0, 2), value.transpose(1, 0, 2)))
    attended = low(low_back(mixed.transpose(1, 0, 2).reshape(group_rows, D)))
    branch = jnp.dot(attended, low(w_out), precision=HIGHEST)
    hidden = low_back(jnp.dot(normed, low(w_fc1), precision=HIGHEST) + vectors[3:3 + FF // D].reshape(FF))
    active = low(jax.nn.gelu(hidden, approximate=True))
    branch = branch + jnp.dot(active, low(w_fc2), precision=HIGHEST)
    return x_group + branch + vectors[7] + vectors[8]

def adam_update(weight, gradient, moment_one, moment_two, step_rate):
    moment_one = BETA_ONE * moment_one + (1.0 - BETA_ONE) * gradient
    moment_two = BETA_TWO * moment_two + (1.0 - BETA_TWO) * gradient * gradient
    first_hat = moment_one / (1.0 - BETA_ONE ** STEP)
    second_hat = moment_two / (1.0 - BETA_TWO ** STEP)
    weight = weight - step_rate * (first_hat / (jnp.sqrt(second_hat) + ADAM_EPS) + WEIGHT_DECAY * weight)
    return (weight, moment_one, moment_two)

def reference(block_input, out_cotangent, token_order, seq_lengths, w_qkv, w_out, w_fc1, w_fc2, vectors, mom1_qkv, mom1_out, mom1_fc1, mom1_fc2, mom1_vec, mom2_qkv, mom2_out, mom2_fc1, mom2_fc2, mom2_vec):
    group_size = TOK_DEV * N_CTX
    doc_ids, positions = jax.vmap(places)(token_order, seq_lengths)
    inputs = block_input.astype(jnp.float32).reshape(N_DP, group_size, D)

    def forward(mat_qkv, mat_out, mat_fc1, mat_fc2, vec_table, x_all):
        weights = (mat_qkv, mat_out.reshape(D, D), mat_fc1, mat_fc2.reshape(FF, D), vec_table)

        def one_group(pieces):
            return layer_group(weights, pieces[0], pieces[1], pieces[2])
        return lax.map(jax.checkpoint(one_group), (x_all, doc_ids, positions))
    result, pullback = jax.vjp(forward, w_qkv, w_out, w_fc1, w_fc2, vectors, inputs)
    grads = pullback(out_cotangent.astype(jnp.float32).reshape(N_DP, group_size, D))
    new_qkv = adam_update(w_qkv, grads[0], mom1_qkv, mom2_qkv, 2.0 / math.sqrt(D))
    new_out = adam_update(w_out, grads[1], mom1_out, mom2_out, 16.0 / math.sqrt(D))
    new_fc1 = adam_update(w_fc1, grads[2], mom1_fc1, mom2_fc1, 2.0 / math.sqrt(D))
    new_fc2 = adam_update(w_fc2, grads[3], mom1_fc2, mom2_fc2, 2.0 / math.sqrt(FF))
    new_vec = adam_update(vectors, grads[4], mom1_vec, mom2_vec, 0.2)
    return (result.reshape(N_DP * group_size, D).astype(jnp.bfloat16), grads[5].reshape(N_DP * group_size, D), new_qkv[0], new_out[0], new_fc1[0], new_fc2[0], new_vec[0], new_qkv[1], new_out[1], new_fc1[1], new_fc2[1], new_vec[1], new_qkv[2], new_out[2], new_fc1[2], new_fc2[2], new_vec[2])
```

```python
import math

import jax
import jax.numpy as jnp
from jax import lax
from jax.experimental import pallas as pl
from jax.experimental.pallas import tpu as pltpu
from jax.sharding import PartitionSpec as P

D = 2048
FF = 8192
HD = 64
ROT = 32
STEP = 10

NORM_EPS = 1e-05
SCORE_SCALE = 0.125
MASKED = -1e30
ROPE_BASE = 10000.0
BETA_ONE = 0.9
BETA_TWO = 0.95
ADAM_EPS = 1e-08
WEIGHT_DECAY = 0.1

N_DP = 8
N_CTX = 8
N_TP = 2
TEAM = N_CTX * N_TP
GROUP = 1024
HALF_ROWS = 64
FEAT = D // TEAM
HIDDEN = FF // TEAM
QKV = 3 * FEAT
Q_BLOCK = 256

BF = jnp.bfloat16
F32 = jnp.float32


def adam_update(weight, gradient, moment_one, moment_two, step_rate):
    moment_one = BETA_ONE * moment_one + (1.0 - BETA_ONE) * gradient
    moment_two = BETA_TWO * moment_two + (1.0 - BETA_TWO) * gradient * gradient
    first_hat = moment_one / (1.0 - BETA_ONE**STEP)
    second_hat = moment_two / (1.0 - BETA_TWO**STEP)
    weight = weight - step_rate * (
        first_hat / (jnp.sqrt(second_hat) + ADAM_EPS) + WEIGHT_DECAY * weight
    )
    return (weight, moment_one, moment_two)


def gelu_and_slope(hidden):
    root = math.sqrt(2.0 / math.pi)
    square = hidden * hidden
    bent = jnp.tanh(root * (hidden + 0.044715 * hidden * square))
    value = 0.5 * hidden * (1.0 + bent)
    slope = 0.5 * (1.0 + bent) + 0.5 * hidden * (1.0 - bent * bent) * root * (
        1.0 + 3.0 * 0.044715 * square
    )
    return (value, slope)


def dot(left, right, dims):
    return lax.dot_general(left, right, (dims, ((), ())), preferred_element_type=F32)


def attention_kernel(
    pre_ref,
    dattn_ref,
    cos_ref,
    sin_ref,
    tok_ref,
    start_ref,
    key_tok_ref,
    attended_ref,
    dpre_ref,
    sums_ref,
    key_scr,
    value_scr,
    dkey_scr,
    dvalue_scr,
):
    step = pl.program_id(0)
    lane = lax.broadcasted_iota(jnp.int32, (1, FEAT), 1)
    early = (lane % HD) < (ROT // 2)
    first_head = lane < HD

    def partner(value):
        return jnp.where(
            early,
            pltpu.roll(value, FEAT - ROT // 2, axis=1),
            pltpu.roll(value, ROT // 2, axis=1),
        )

    @pl.when(step == 0)
    def _():
        key = pre_ref[:, FEAT : 2 * FEAT]
        key_scr[...] = (key * cos_ref[...] + partner(key) * sin_ref[...]).astype(BF)
        value_scr[...] = pre_ref[:, 2 * FEAT :].astype(BF)
        dkey_scr[...] = jnp.zeros_like(dkey_scr)
        dvalue_scr[...] = jnp.zeros_like(dvalue_scr)
        sums_ref[...] = jnp.zeros_like(sums_ref)

    rows = pl.ds(step * Q_BLOCK, Q_BLOCK)
    cos_rows = cos_ref[rows, :]
    sin_rows = sin_ref[rows, :]
    query = pre_ref[rows, :FEAT]
    query = (query * cos_rows + partner(query) * sin_rows).astype(BF) * jnp.asarray(SCORE_SCALE, BF)
    dattn = dattn_ref[rows, :]
    key = key_scr[...]
    value = value_scr[...]
    tok = tok_ref[rows, :]
    start = start_ref[rows, :]
    key_tok = key_tok_ref[...]
    mask = (key_tok <= tok) & (key_tok >= start)
    zero = jnp.zeros((), BF)
    out_parts = []
    dquery_parts = []
    for head in range(2):
        inside = first_head if head == 0 else jnp.logical_not(first_head)
        query_h = jnp.where(inside, query, zero)
        dattn_h = jnp.where(inside, dattn, zero)
        scores = dot(query_h, key, ((1,), (1,)))
        scores = jnp.where(mask, scores, MASKED)
        top = jnp.max(scores, axis=1, keepdims=True)
        probs = jnp.exp(scores - top)
        probs = probs * (1.0 / jnp.sum(probs, axis=1, keepdims=True))
        probs_b = probs.astype(BF)
        out = dot(probs_b, value, ((1,), (0,)))
        delta = jnp.sum(
            jnp.where(inside, out, 0.0) * dattn_h.astype(F32), axis=1, keepdims=True
        )
        dprobs = dot(dattn_h, value, ((1,), (1,)))
        dscore = (probs * (dprobs - delta)).astype(BF)
        dquery_parts.append(dot(dscore, key, ((1,), (0,))))
        dkey_scr[...] += dot(dscore, query_h, ((0,), (0,)))
        dvalue_scr[...] += dot(probs_b, dattn_h, ((0,), (0,)))
        out_parts.append(out)
    attended_ref[rows, :] = jnp.where(first_head, out_parts[0], out_parts[1]).astype(BF)
    dquery = jnp.where(first_head, dquery_parts[0], dquery_parts[1]) * SCORE_SCALE
    dquery = (dquery * cos_rows - partner(dquery) * sin_rows).astype(BF)
    dpre_ref[rows, :FEAT] = dquery
    sums_ref[0:1, :FEAT] += jnp.sum(dquery.astype(F32), axis=0, keepdims=True)

    @pl.when(step == pl.num_programs(0) - 1)
    def _():
        dkey = dkey_scr[...]
        dkey = (dkey * cos_ref[...] - partner(dkey) * sin_ref[...]).astype(BF)
        dvalue = dvalue_scr[...].astype(BF)
        dpre_ref[:, FEAT : 2 * FEAT] = dkey
        dpre_ref[:, 2 * FEAT :] = dvalue
        sums_ref[0:1, FEAT : 2 * FEAT] = jnp.sum(dkey.astype(F32), axis=0, keepdims=True)
        sums_ref[0:1, 2 * FEAT :] = jnp.sum(dvalue.astype(F32), axis=0, keepdims=True)


def attention(pre, dattn, cos_table, sin_table, tok, start):
    tokens = pre.shape[0]
    whole = pl.BlockSpec(memory_space=pltpu.VMEM)
    return pl.pallas_call(
        attention_kernel,
        grid=(tokens // Q_BLOCK,),
        out_shape=(
            jax.ShapeDtypeStruct((tokens, FEAT), BF),
            jax.ShapeDtypeStruct((tokens, QKV), BF),
            jax.ShapeDtypeStruct((8, QKV), F32),
        ),
        in_specs=[whole] * 7,
        out_specs=(whole, whole, whole),
        scratch_shapes=[
            pltpu.VMEM((tokens, FEAT), BF),
            pltpu.VMEM((tokens, FEAT), BF),
            pltpu.VMEM((tokens, FEAT), F32),
            pltpu.VMEM((tokens, FEAT), F32),
        ],
        compiler_params=pltpu.CompilerParams(vmem_limit_bytes=40 * 2**20),
        cost_estimate=pl.CostEstimate(
            flops=7 * 2 * 2 * tokens * tokens * HD,
            bytes_accessed=8 * 2**20,
            transcendentals=2 * tokens * tokens,
        ),
    )(pre, dattn, cos_table, sin_table, tok[:, None], start[:, None], tok[None, :])


def swap(value):
    return lax.ppermute(value, "tp", [(0, 1), (1, 0)])


def spread(value, axis, count):
    return lax.all_to_all(
        jnp.broadcast_to(value[None], (count,) + value.shape), axis, 0, 0, tiled=True
    )


def transposed(value):
    pairs = [(a * N_CTX + b, b * N_CTX + a) for a in range(N_DP) for b in range(N_CTX)]
    return lax.ppermute(value, ("dp", "ctx"), pairs)


def shards(
    block_input,
    out_cotangent,
    token_order,
    seq_lengths,
    w_qkv,
    w_out,
    w_fc1,
    w_fc2,
    vectors,
    mom1_qkv,
    mom1_out,
    mom1_fc1,
    mom1_fc2,
    mom1_vec,
    mom2_qkv,
    mom2_out,
    mom2_fc1,
    mom2_fc2,
    mom2_vec,
):
    ctx_rank = lax.axis_index("ctx")
    tp_rank = lax.axis_index("tp")
    team_rank = ctx_rank * N_TP + tp_rank
    own_d = D // (N_DP * N_CTX)
    out_rows = w_out.shape[1]
    fc2_rows = w_fc2.shape[1]

    columns = jnp.concatenate(
        [w_qkv[:, part].reshape(own_d, N_CTX, FEAT) for part in range(3)]
        + [w_fc1.reshape(own_d, N_CTX, HIDDEN)],
        axis=2,
    ).astype(BF)
    columns = lax.all_to_all(columns.transpose(1, 0, 2), "ctx", 0, 0, tiled=True)
    columns = columns.reshape(N_CTX * own_d, QKV + HIDDEN)
    w_in = lax.all_gather(columns, "dp", axis=0, tiled=True)
    rows = transposed(jnp.concatenate([w_out[0], w_fc2[0]], axis=0).astype(BF))
    rows = lax.all_gather(rows, "dp", axis=0, tiled=False)
    w_back = jnp.concatenate(
        [rows[:, :out_rows].reshape(FEAT, D), rows[:, out_rows:].reshape(HIDDEN, D)], axis=0
    )

    def half(value, axis=0):
        return lax.dynamic_slice_in_dim(value, tp_rank * HALF_ROWS, HALF_ROWS, axis)

    x_own = half(block_input).astype(F32)
    dy_own = half(out_cotangent)
    tok_own = half(token_order[0])
    row_mean = jnp.mean(x_own, axis=-1, keepdims=True)
    centered = x_own - row_mean
    inv_std = lax.rsqrt(jnp.mean(centered * centered, axis=-1, keepdims=True) + NORM_EPS)
    normal_x = centered * inv_std
    norm_gain = vectors[9]
    norm_shift = vectors[10]
    normed_own = (normal_x * norm_gain + norm_shift).astype(BF)

    def whole_group(value):
        mine = spread(value, "ctx", N_CTX)
        mine = mine.reshape((N_CTX * HALF_ROWS,) + value.shape[1:])
        return jnp.concatenate([mine, swap(mine)], axis=0)

    normed = whole_group(normed_own)
    tok = whole_group(tok_own)
    dy = whole_group(dy_own)

    ends = jnp.cumsum(seq_lengths[0])
    starts = ends - seq_lengths[0]
    inside = (tok[:, None] >= starts[None, :]) & (tok[:, None] < ends[None, :])
    first = jnp.sum(jnp.where(inside, starts[None, :], 0), axis=1)
    position = (tok - first).astype(F32)
    lane = jnp.arange(FEAT) % HD
    inverse = ROPE_BASE ** (-(2.0 * (lane % (ROT // 2)).astype(F32)) / ROT)
    inverse = jnp.where(lane < ROT, inverse, 0.0)
    rotation = position[:, None] * inverse[None, :]
    cos_table = jnp.cos(rotation)
    sin_table = jnp.sin(rotation) * jnp.where(lane < ROT // 2, -1.0, 1.0)

    bias_qkv = lax.dynamic_slice(vectors, (0, tp_rank * (D // N_TP) + ctx_rank * FEAT), (3, FEAT))
    bias_fc1 = lax.dynamic_slice_in_dim(
        vectors[3:7].reshape(FF), tp_rank * (FF // N_TP) + ctx_rank * HIDDEN, HIDDEN
    )
    pre = dot(normed, w_in, ((1,), (0,)))
    back = dot(dy, w_back, ((1,), (1,)))
    hidden = pre[:, QKV:] + bias_fc1
    pre_qkv = pre[:, :QKV] + bias_qkv.reshape(QKV)
    active, slope = gelu_and_slope(hidden)
    active = active.astype(BF)
    dhid = (back[:, FEAT:] * slope).astype(BF)
    dattn = back[:, :FEAT].astype(BF)
    attended, dpre, dpre_sums = attention(pre_qkv, dattn, cos_table, sin_table, tok, first)

    grad_fc1 = dot(normed, dhid, ((0,), (0,))).astype(BF)
    grad_fc1 = lax.psum_scatter(grad_fc1, "dp", scatter_dimension=0, tiled=True)
    grad_fc2 = dot(active, dy, ((0,), (0,))).astype(BF)
    grad_fc2 = lax.psum_scatter(grad_fc2, "dp", scatter_dimension=0, tiled=True)
    grad_out = dot(attended, dy, ((0,), (0,))).astype(BF)
    grad_qkv = dot(normed, dpre, ((0,), (0,))).astype(BF)

    def summed(value):
        pieces = value.reshape((N_DP, value.shape[0] // N_DP) + value.shape[1:])
        pieces = lax.all_to_all(pieces, "dp", 0, 0, tiled=True)
        return jnp.sum(pieces.astype(F32), axis=0)

    grad_qkv = summed(grad_qkv).astype(BF)
    grad_out = summed(grad_out).astype(BF)
    back_rows = transposed(jnp.concatenate([grad_out, grad_fc2], axis=0)).astype(F32)
    sum_out = back_rows[None, :out_rows]
    sum_fc2 = back_rows[None, out_rows:]
    back_columns = jnp.concatenate([grad_qkv, grad_fc1], axis=1)
    back_columns = back_columns.reshape(N_CTX, own_d, QKV + HIDDEN)
    back_columns = lax.all_to_all(back_columns, "ctx", 0, 0, tiled=True).astype(F32)
    sum_qkv = jnp.stack(
        [
            back_columns[:, :, part * FEAT : (part + 1) * FEAT]
            .transpose(1, 0, 2)
            .reshape(own_d, N_CTX * FEAT)
            for part in range(3)
        ],
        axis=1,
    )
    sum_fc1 = back_columns[:, :, QKV:].transpose(1, 0, 2).reshape(own_d, N_CTX * HIDDEN)

    def to_owner(left, right, dims):
        rows_half = N_CTX * HALF_ROWS
        theirs = dot(left[rows_half:], right, dims).astype(BF)
        mine = dot(left[:rows_half], right, dims)
        mine = (mine + swap(theirs).astype(F32)).astype(BF)
        mine = mine.reshape(N_CTX, HALF_ROWS, D)
        return jnp.sum(lax.all_to_all(mine, "ctx", 0, 0, tiled=True).astype(F32), axis=0)

    def both_halves(value):
        other = swap(value)
        first_core = tp_rank == 0
        return jnp.concatenate(
            [jnp.where(first_core, value, other), jnp.where(first_core, other, value)], axis=0
        )

    branch = to_owner(jnp.concatenate([attended, active], axis=1), w_back, ((1,), (0,)))
    block_output = both_halves((x_own + branch + vectors[7] + vectors[8]).astype(BF))
    normed_grad = to_owner(jnp.concatenate([dpre, dhid], axis=1), w_in, ((1,), (1,)))
    scaled_grad = normed_grad * norm_gain
    input_grad = dy_own.astype(F32) + inv_std * (
        scaled_grad
        - jnp.mean(scaled_grad, axis=-1, keepdims=True)
        - normal_x * jnp.mean(scaled_grad * normal_x, axis=-1, keepdims=True)
    )
    input_grad = both_halves(input_grad)

    dy_sum = jnp.sum(dy.astype(F32), axis=0)
    dy_sum = lax.dynamic_slice_in_dim(dy_sum, team_rank * FEAT, FEAT)
    norm_terms = jnp.stack([jnp.sum(normed_grad * normal_x, axis=0), jnp.sum(normed_grad, axis=0)])
    norm_terms = norm_terms.reshape(2, TEAM, FEAT).transpose(1, 0, 2)
    norm_terms = jnp.sum(lax.all_to_all(norm_terms, ("ctx", "tp"), 0, 0, tiled=True), axis=0)
    terms = jnp.concatenate(
        [
            dpre_sums[0],
            jnp.sum(dhid.astype(F32), axis=0),
            dy_sum,
            norm_terms.reshape(2 * FEAT),
        ]
    )
    terms = jnp.sum(spread(terms, "dp", N_DP), axis=0)
    terms = spread(terms, ("ctx", "tp"), TEAM).reshape(N_CTX, N_TP, terms.shape[0])
    by_half = terms.transpose(1, 0, 2)
    vector_grad = jnp.concatenate(
        [by_half[:, :, part * FEAT : (part + 1) * FEAT].reshape(1, D) for part in range(3)]
        + [by_half[:, :, QKV : QKV + HIDDEN].reshape(FF // D, D)]
        + [
            terms[:, :, QKV + HIDDEN + part * FEAT : QKV + HIDDEN + (part + 1) * FEAT].reshape(1, D)
            for part in (0, 0, 1, 2)
        ],
        axis=0,
    )

    new_qkv = adam_update(w_qkv, sum_qkv, mom1_qkv, mom2_qkv, 2.0 / math.sqrt(D))
    new_out = adam_update(w_out, sum_out, mom1_out, mom2_out, 16.0 / math.sqrt(D))
    new_fc1 = adam_update(w_fc1, sum_fc1, mom1_fc1, mom2_fc1, 2.0 / math.sqrt(D))
    new_fc2 = adam_update(w_fc2, sum_fc2, mom1_fc2, mom2_fc2, 2.0 / math.sqrt(FF))
    new_vec = adam_update(vectors, vector_grad, mom1_vec, mom2_vec, 0.2)
    return (
        block_output,
        input_grad,
        new_qkv[0],
        new_out[0],
        new_fc1[0],
        new_fc2[0],
        new_vec[0],
        new_qkv[1],
        new_out[1],
        new_fc1[1],
        new_fc2[1],
        new_vec[1],
        new_qkv[2],
        new_out[2],
        new_fc1[2],
        new_fc2[2],
        new_vec[2],
    )


def solution(mesh):
    in_specs = (
        P(("dp", "ctx"), None),
        P(("dp", "ctx"), None),
        P("dp", "ctx"),
        P("dp", None),
        P(("dp", "ctx"), None, "tp"),
        P("tp", ("dp", "ctx"), None),
        P(("dp", "ctx"), "tp"),
        P("tp", ("dp", "ctx"), None),
        P(),
        P(("dp", "ctx"), None, "tp"),
        P("tp", ("dp", "ctx"), None),
        P(("dp", "ctx"), "tp"),
        P("tp", ("dp", "ctx"), None),
        P(),
        P(("dp", "ctx"), None, "tp"),
        P("tp", ("dp", "ctx"), None),
        P(("dp", "ctx"), "tp"),
        P("tp", ("dp", "ctx"), None),
        P(),
    )
    out_specs = (
        P(("dp", "ctx"), None),
        P(("dp", "ctx"), None),
        P(("dp", "ctx"), None, "tp"),
        P("tp", ("dp", "ctx"), None),
        P(("dp", "ctx"), "tp"),
        P("tp", ("dp", "ctx"), None),
        P(),
        P(("dp", "ctx"), None, "tp"),
        P("tp", ("dp", "ctx"), None),
        P(("dp", "ctx"), "tp"),
        P("tp", ("dp", "ctx"), None),
        P(),
        P(("dp", "ctx"), None, "tp"),
        P("tp", ("dp", "ctx"), None),
        P(("dp", "ctx"), "tp"),
        P("tp", ("dp", "ctx"), None),
        P(),
    )
    return jax.shard_map(shards, mesh=mesh, in_specs=in_specs, out_specs=out_specs, check_vma=False)
```

```python
import math

import jax
import jax.numpy as jnp
from jax import lax
from jax.experimental import pallas as pl
from jax.experimental.pallas import tpu as pltpu
from jax.sharding import PartitionSpec as P

D = 2048
FF = 8192
HD = 64
ROT = 32
STEP = 10

NORM_EPS = 1e-05
SCORE_SCALE = 0.125
MASKED = -1e30
ROPE_BASE = 10000.0
BETA_ONE = 0.9
BETA_TWO = 0.95
ADAM_EPS = 1e-08
WEIGHT_DECAY = 0.1

N_DP = 8
N_CTX = 8
N_TP = 2
TEAM = N_CTX * N_TP
GROUP = 1024
HALF_ROWS = 64
FEAT = D // TEAM
HIDDEN = FF // TEAM
QKV = 3 * FEAT
Q_BLOCK = 256

BF = jnp.bfloat16
F32 = jnp.float32


def adam_update(weight, gradient, moment_one, moment_two, step_rate):
    moment_one = BETA_ONE * moment_one + (1.0 - BETA_ONE) * gradient
    moment_two = BETA_TWO * moment_two + (1.0 - BETA_TWO) * gradient * gradient
    first_hat = moment_one / (1.0 - BETA_ONE**STEP)
    second_hat = moment_two / (1.0 - BETA_TWO**STEP)
    weight = weight - step_rate * (
        first_hat / (jnp.sqrt(second_hat) + ADAM_EPS) + WEIGHT_DECAY * weight
    )
    return (weight, moment_one, moment_two)


def gelu_and_slope(hidden):
    root = math.sqrt(2.0 / math.pi)
    square = hidden * hidden
    bent = jnp.tanh(root * (hidden + 0.044715 * hidden * square))
    value = 0.5 * hidden * (1.0 + bent)
    slope = 0.5 * (1.0 + bent) + 0.5 * hidden * (1.0 - bent * bent) * root * (
        1.0 + 3.0 * 0.044715 * square
    )
    return (value, slope)


def dot(left, right, dims):
    return lax.dot_general(left, right, (dims, ((), ())), preferred_element_type=F32)


def attention_kernel(
    pre_ref,
    dattn_ref,
    cos_ref,
    sin_ref,
    tok_ref,
    start_ref,
    key_tok_ref,
    attended_ref,
    dpre_ref,
    sums_ref,
    key_scr,
    value_scr,
    dkey_scr,
    dvalue_scr,
):
    step = pl.program_id(0)
    lane = lax.broadcasted_iota(jnp.int32, (1, FEAT), 1)
    early = (lane % HD) < (ROT // 2)
    first_head = lane < HD

    def partner(value):
        return jnp.where(
            early,
            pltpu.roll(value, FEAT - ROT // 2, axis=1),
            pltpu.roll(value, ROT // 2, axis=1),
        )

    @pl.when(step == 0)
    def _():
        key = pre_ref[:, FEAT : 2 * FEAT]
        key_scr[...] = (key * cos_ref[...] + partner(key) * sin_ref[...]).astype(BF)
        value_scr[...] = pre_ref[:, 2 * FEAT :].astype(BF)
        dkey_scr[...] = jnp.zeros_like(dkey_scr)
        dvalue_scr[...] = jnp.zeros_like(dvalue_scr)
        sums_ref[...] = jnp.zeros_like(sums_ref)

    rows = pl.ds(step * Q_BLOCK, Q_BLOCK)
    cos_rows = cos_ref[rows, :]
    sin_rows = sin_ref[rows, :]
    query = pre_ref[rows, :FEAT]
    query = (query * cos_rows + partner(query) * sin_rows).astype(BF) * jnp.asarray(SCORE_SCALE, BF)
    dattn = dattn_ref[rows, :]
    key = key_scr[...]
    value = value_scr[...]
    tok = tok_ref[rows, :]
    start = start_ref[rows, :]
    key_tok = key_tok_ref[...]
    mask = (key_tok <= tok) & (key_tok >= start)
    zero = jnp.zeros((), BF)
    out_parts = []
    dquery_parts = []
    for head in range(2):
        inside = first_head if head == 0 else jnp.logical_not(first_head)
        query_h = jnp.where(inside, query, zero)
        dattn_h = jnp.where(inside, dattn, zero)
        scores = dot(query_h, key, ((1,), (1,)))
        scores = jnp.where(mask, scores, MASKED)
        top = jnp.max(scores, axis=1, keepdims=True)
        probs = jnp.exp(scores - top)
        probs = probs * (1.0 / jnp.sum(probs, axis=1, keepdims=True))
        probs_b = probs.astype(BF)
        out = dot(probs_b, value, ((1,), (0,)))
        delta = jnp.sum(
            jnp.where(inside, out, 0.0) * dattn_h.astype(F32), axis=1, keepdims=True
        )
        dprobs = dot(dattn_h, value, ((1,), (1,)))
        dscore = (probs * (dprobs - delta)).astype(BF)
        dquery_parts.append(dot(dscore, key, ((1,), (0,))))
        dkey_scr[...] += dot(dscore, query_h, ((0,), (0,)))
        dvalue_scr[...] += dot(probs_b, dattn_h, ((0,), (0,)))
        out_parts.append(out)
    attended_ref[rows, :] = jnp.where(first_head, out_parts[0], out_parts[1]).astype(BF)
    dquery = jnp.where(first_head, dquery_parts[0], dquery_parts[1]) * SCORE_SCALE
    dquery = (dquery * cos_rows - partner(dquery) * sin_rows).astype(BF)
    dpre_ref[rows, :FEAT] = dquery
    sums_ref[0:1, :FEAT] += jnp.sum(dquery.astype(F32), axis=0, keepdims=True)

    @pl.when(step == pl.num_programs(0) - 1)
    def _():
        dkey = dkey_scr[...]
        dkey = (dkey * cos_ref[...] - partner(dkey) * sin_ref[...]).astype(BF)
        dvalue = dvalue_scr[...].astype(BF)
        dpre_ref[:, FEAT : 2 * FEAT] = dkey
        dpre_ref[:, 2 * FEAT :] = dvalue
        sums_ref[0:1, FEAT : 2 * FEAT] = jnp.sum(dkey.astype(F32), axis=0, keepdims=True)
        sums_ref[0:1, 2 * FEAT :] = jnp.sum(dvalue.astype(F32), axis=0, keepdims=True)


def attention(pre, dattn, cos_table, sin_table, tok, start):
    tokens = pre.shape[0]
    whole = pl.BlockSpec(memory_space=pltpu.VMEM)
    return pl.pallas_call(
        attention_kernel,
        grid=(tokens // Q_BLOCK,),
        out_shape=(
            jax.ShapeDtypeStruct((tokens, FEAT), BF),
            jax.ShapeDtypeStruct((tokens, QKV), BF),
            jax.ShapeDtypeStruct((8, QKV), F32),
        ),
        in_specs=[whole] * 7,
        out_specs=(whole, whole, whole),
        scratch_shapes=[
            pltpu.VMEM((tokens, FEAT), BF),
            pltpu.VMEM((tokens, FEAT), BF),
            pltpu.VMEM((tokens, FEAT), F32),
            pltpu.VMEM((tokens, FEAT), F32),
        ],
        compiler_params=pltpu.CompilerParams(vmem_limit_bytes=40 * 2**20),
        cost_estimate=pl.CostEstimate(
            flops=7 * 2 * 2 * tokens * tokens * HD,
            bytes_accessed=8 * 2**20,
            transcendentals=2 * tokens * tokens,
        ),
    )(pre, dattn, cos_table, sin_table, tok[:, None], start[:, None], tok[None, :])


def swap(value):
    return lax.ppermute(value, "tp", [(0, 1), (1, 0)])


PLACED = (0, 1, 3, 2, 4, 5, 7, 6)
FLIPS = (4, 3, 1)


def place_bits():
    rank = lax.axis_index("dp")
    high = (rank // 2) % 2
    return (rank // 4, high, high ^ (rank % 2))


def exchange(value, bit):
    return lax.ppermute(value, "dp", [(d, d ^ FLIPS[bit]) for d in range(N_DP)])


def gather_dp(values, order):
    bits = place_bits()
    values = [value[None, None, None] for value in values]
    for bit in order:
        first = bits[bit] == 0
        grown = []
        for value in values:
            other = exchange(value, bit)
            grown.append(
                jnp.concatenate(
                    [jnp.where(first, value, other), jnp.where(first, other, value)], axis=bit
                )
            )
        values = grown
    return [value.reshape((N_DP,) + value.shape[3:]) for value in values]


def scatter_dp(values, order):
    bits = place_bits()
    values = [value.reshape((2, 2, 2) + value.shape[1:]) for value in values]
    for bit in reversed(order):
        rest = []
        for value in values:
            kept = lax.dynamic_slice_in_dim(value, bits[bit], 1, bit)
            sent = lax.dynamic_slice_in_dim(value, 1 - bits[bit], 1, bit)
            other = exchange(sent, bit)
            rest.append((kept.astype(F32) + other.astype(F32)).astype(BF))
        values = rest
    return [value.reshape(value.shape[3:]) for value in values]


def placed(value, axis):
    shape = value.shape
    blocks = value.reshape(shape[:axis] + (N_DP, shape[axis] // N_DP) + shape[axis + 1 :])
    blocks = [lax.slice_in_dim(blocks, d, d + 1, axis=axis) for d in PLACED]
    return jnp.concatenate(blocks, axis=axis).reshape(shape)


def rows_to_team(value):
    pairs = [
        (d * N_CTX + c, PLACED[c] * N_CTX + d) for d in range(N_DP) for c in range(N_CTX)
    ]
    return lax.ppermute(value, ("dp", "ctx"), pairs)


def rows_to_owner(value):
    pairs = [
        (PLACED[c] * N_CTX + d, d * N_CTX + c) for d in range(N_DP) for c in range(N_CTX)
    ]
    return lax.ppermute(value, ("dp", "ctx"), pairs)


def spread(value, axis, count):
    return lax.all_to_all(
        jnp.broadcast_to(value[None], (count,) + value.shape), axis, 0, 0, tiled=True
    )


def shards(
    block_input,
    out_cotangent,
    token_order,
    seq_lengths,
    w_qkv,
    w_out,
    w_fc1,
    w_fc2,
    vectors,
    mom1_qkv,
    mom1_out,
    mom1_fc1,
    mom1_fc2,
    mom1_vec,
    mom2_qkv,
    mom2_out,
    mom2_fc1,
    mom2_fc2,
    mom2_vec,
):
    ctx_rank = lax.axis_index("ctx")
    tp_rank = lax.axis_index("tp")
    team_rank = tp_rank * N_CTX + ctx_rank
    own_d = D // (N_DP * N_CTX)
    half_rows = N_CTX * HALF_ROWS

    columns = jnp.concatenate(
        [w_qkv[:, part].reshape(own_d, N_CTX, FEAT) for part in range(3)]
        + [w_fc1.reshape(own_d, N_CTX, HIDDEN)],
        axis=2,
    ).astype(BF)
    columns = lax.all_to_all(columns.transpose(1, 0, 2), "ctx", 0, 0, tiled=True)
    columns = columns.reshape(N_CTX * own_d, QKV + HIDDEN)
    out_part = rows_to_team(w_out[0].astype(BF))
    fc2_part = rows_to_team(w_fc2[0].astype(BF))
    (mat_fc2,) = gather_dp([fc2_part], (2, 1, 0))
    (mat_fc1,) = gather_dp([columns[:, QKV:]], (1, 0, 2))
    mat_qkv, mat_out = gather_dp([columns[:, :QKV], out_part], (0, 2, 1))
    mat_fc2 = mat_fc2.reshape(HIDDEN, D)
    mat_out = mat_out.reshape(FEAT, D)
    mat_fc1 = mat_fc1.reshape(D, HIDDEN)
    mat_qkv = mat_qkv.reshape(D, QKV)

    def half(value, axis=0):
        return lax.dynamic_slice_in_dim(value, tp_rank * HALF_ROWS, HALF_ROWS, axis)

    x_own = placed(half(block_input), 1)
    dy_own = half(out_cotangent)
    tok_own = half(token_order[0])
    tok_pair = jnp.stack([tok_own // 32, tok_own % 32], axis=1).astype(BF)
    x_wide = jnp.concatenate([x_own, jnp.pad(tok_pair, ((0, 0), (0, 126)))], axis=1)

    def whole_group(value):
        mine = spread(value, "ctx", N_CTX).reshape(half_rows, value.shape[1])
        return jnp.concatenate([mine, swap(mine)], axis=0)

    x_wide = whole_group(x_wide)
    dy = whole_group(dy_own)
    tok_pair = x_wide[:, D : D + 2].astype(jnp.int32)
    tok = tok_pair[:, 0] * 32 + tok_pair[:, 1]

    def normal(value):
        value = value.astype(F32)
        centered = value - jnp.mean(value, axis=-1, keepdims=True)
        inv_std = lax.rsqrt(jnp.mean(centered * centered, axis=-1, keepdims=True) + NORM_EPS)
        return (centered * inv_std, inv_std)

    norm_gain = placed(vectors[9], 0)
    norm_shift = placed(vectors[10], 0)
    normal_x = normal(x_wide[:, :D])[0]
    normed = (normal_x * norm_gain + norm_shift).astype(BF)

    ends = jnp.cumsum(seq_lengths[0])
    starts = ends - seq_lengths[0]
    inside = (tok[:, None] >= starts[None, :]) & (tok[:, None] < ends[None, :])
    first = jnp.sum(jnp.where(inside, starts[None, :], 0), axis=1)
    position = (tok - first).astype(F32)
    lane = jnp.arange(FEAT) % HD
    inverse = ROPE_BASE ** (-(2.0 * (lane % (ROT // 2)).astype(F32)) / ROT)
    inverse = jnp.where(lane < ROT, inverse, 0.0)
    rotation = position[:, None] * inverse[None, :]
    cos_table = jnp.cos(rotation)
    sin_table = jnp.sin(rotation) * jnp.where(lane < ROT // 2, -1.0, 1.0)

    bias_qkv = lax.dynamic_slice(vectors, (0, team_rank * FEAT), (3, FEAT))
    bias_fc1 = lax.dynamic_slice_in_dim(vectors[3:7].reshape(FF), team_rank * HIDDEN, HIDDEN)
    dattn = dot(dy, mat_out, ((1,), (1,))).astype(BF)
    pre_qkv = dot(normed, mat_qkv, ((1,), (0,))) + bias_qkv.reshape(QKV)
    hidden = dot(normed, mat_fc1, ((1,), (0,))) + bias_fc1
    active, slope = gelu_and_slope(hidden)
    active = active.astype(BF)
    dhid = (dot(dy, mat_fc2, ((1,), (1,))) * slope).astype(BF)

    grad_fc2 = dot(active, dy, ((0,), (0,))).astype(BF)
    grad_fc1 = dot(normed, dhid, ((0,), (0,))).astype(BF)
    (grad_fc2,) = scatter_dp([grad_fc2.reshape(N_DP, HIDDEN // N_DP, D)], (2, 1, 0))
    (grad_fc1,) = scatter_dp([grad_fc1.reshape(N_DP, D // N_DP, HIDDEN)], (1, 0, 2))
    attended, dpre, dpre_sums = attention(pre_qkv, dattn, cos_table, sin_table, tok, first)
    grad_qkv = dot(normed, dpre, ((0,), (0,))).astype(BF)
    grad_out = dot(attended, dy, ((0,), (0,))).astype(BF)
    grad_qkv, grad_out = scatter_dp(
        [grad_qkv.reshape(N_DP, D // N_DP, QKV), grad_out.reshape(N_DP, FEAT // N_DP, D)],
        (0, 2, 1),
    )
    sum_out = rows_to_owner(grad_out).astype(F32)[None]
    sum_fc2 = rows_to_owner(grad_fc2).astype(F32)[None]
    back_columns = jnp.concatenate([grad_qkv, grad_fc1], axis=1)
    back_columns = back_columns.reshape(N_CTX, own_d, QKV + HIDDEN)
    back_columns = lax.all_to_all(back_columns, "ctx", 0, 0, tiled=True).astype(F32)
    sum_qkv = jnp.stack(
        [
            back_columns[:, :, part * FEAT : (part + 1) * FEAT]
            .transpose(1, 0, 2)
            .reshape(own_d, N_CTX * FEAT)
            for part in range(3)
        ],
        axis=1,
    )
    sum_fc1 = back_columns[:, :, QKV:].transpose(1, 0, 2).reshape(own_d, N_CTX * HIDDEN)

    def own_half(value):
        mine = value[:half_rows].astype(F32) + swap(value[half_rows:].astype(BF)).astype(F32)
        return mine.astype(BF).reshape(N_CTX, HALF_ROWS, D)

    def both_halves(value):
        other = swap(value)
        first_core = tp_rank == 0
        return jnp.concatenate(
            [jnp.where(first_core, value, other), jnp.where(first_core, other, value)], axis=0
        )

    normed_part = dot(dpre, mat_qkv, ((1,), (1,))) + dot(dhid, mat_fc1, ((1,), (1,)))
    branch = dot(attended, mat_out, ((1,), (0,))) + dot(active, mat_fc2, ((1,), (0,)))
    merged = jnp.concatenate([own_half(normed_part), own_half(branch)], axis=1)
    merged = lax.all_to_all(merged, "ctx", 0, 0, tiled=True).astype(F32)
    merged = jnp.sum(merged, axis=0)
    normed_grad = merged[:HALF_ROWS]
    branch = merged[HALF_ROWS:]
    block_output = half(block_input).astype(F32) + branch + vectors[7] + vectors[8]
    block_output = both_halves(block_output.astype(BF))
    own_normal, inv_std = normal(x_own)
    scaled_grad = normed_grad * norm_gain
    input_grad = inv_std * (
        scaled_grad
        - jnp.mean(scaled_grad, axis=-1, keepdims=True)
        - own_normal * jnp.mean(scaled_grad * own_normal, axis=-1, keepdims=True)
    )
    input_grad = both_halves(dy_own.astype(F32) + placed(input_grad, 1))

    norm_terms = jnp.stack(
        [jnp.sum(normed_part * normal_x, axis=0), jnp.sum(normed_part, axis=0)]
    )
    dy_sum = jnp.sum(dy.astype(F32), axis=0)
    dy_sum = lax.dynamic_slice_in_dim(dy_sum, team_rank * FEAT, FEAT)
    terms = jnp.concatenate(
        [dpre_sums[0], dy_sum, jnp.sum(dhid.astype(F32), axis=0), norm_terms.reshape(2 * D)]
    ).reshape(40, 128)
    for bit in range(3):
        terms = terms + exchange(terms, bit)
    whole = jnp.zeros((4, D), F32)
    whole = lax.dynamic_update_slice(whole, terms[:4].reshape(4, FEAT), (0, team_rank * FEAT))
    hidden_sums = lax.dynamic_update_slice_in_dim(
        jnp.zeros((FF,), F32), terms[4:8].reshape(HIDDEN), team_rank * HIDDEN, 0
    )
    whole = jnp.concatenate(
        [whole, hidden_sums.reshape(FF // D, D), terms[8:].reshape(2, D)], axis=0
    )
    for flip in (1, 2, 6):
        whole = whole + lax.ppermute(whole, "ctx", [(c, c ^ flip) for c in range(N_CTX)])
    whole = whole + swap(whole)
    vector_grad = jnp.concatenate(
        [whole[:3], whole[4:8], whole[3:4], whole[3:4], placed(whole[8:], 1)], axis=0
    )

    new_qkv = adam_update(w_qkv, sum_qkv, mom1_qkv, mom2_qkv, 2.0 / math.sqrt(D))
    new_out = adam_update(w_out, sum_out, mom1_out, mom2_out, 16.0 / math.sqrt(D))
    new_fc1 = adam_update(w_fc1, sum_fc1, mom1_fc1, mom2_fc1, 2.0 / math.sqrt(D))
    new_fc2 = adam_update(w_fc2, sum_fc2, mom1_fc2, mom2_fc2, 2.0 / math.sqrt(FF))
    new_vec = adam_update(vectors, vector_grad, mom1_vec, mom2_vec, 0.2)
    return (
        block_output,
        input_grad,
        new_qkv[0],
        new_out[0],
        new_fc1[0],
        new_fc2[0],
        new_vec[0],
        new_qkv[1],
        new_out[1],
        new_fc1[1],
        new_fc2[1],
        new_vec[1],
        new_qkv[2],
        new_out[2],
        new_fc1[2],
        new_fc2[2],
        new_vec[2],
    )


def solution(mesh):
    in_specs = (
        P(("dp", "ctx"), None),
        P(("dp", "ctx"), None),
        P("dp", "ctx"),
        P("dp", None),
        P(("dp", "ctx"), None, "tp"),
        P("tp", ("dp", "ctx"), None),
        P(("dp", "ctx"), "tp"),
        P("tp", ("dp", "ctx"), None),
        P(),
        P(("dp", "ctx"), None, "tp"),
        P("tp", ("dp", "ctx"), None),
        P(("dp", "ctx"), "tp"),
        P("tp", ("dp", "ctx"), None),
        P(),
        P(("dp", "ctx"), None, "tp"),
        P("tp", ("dp", "ctx"), None),
        P(("dp", "ctx"), "tp"),
        P("tp", ("dp", "ctx"), None),
        P(),
    )
    out_specs = (
        P(("dp", "ctx"), None),
        P(("dp", "ctx"), None),
        P(("dp", "ctx"), None, "tp"),
        P("tp", ("dp", "ctx"), None),
        P(("dp", "ctx"), "tp"),
        P("tp", ("dp", "ctx"), None),
        P(),
        P(("dp", "ctx"), None, "tp"),
        P("tp", ("dp", "ctx"), None),
        P(("dp", "ctx"), "tp"),
        P("tp", ("dp", "ctx"), None),
        P(),
        P(("dp", "ctx"), None, "tp"),
        P("tp", ("dp", "ctx"), None),
        P(("dp", "ctx"), "tp"),
        P("tp", ("dp", "ctx"), None),
        P(),
    )
    return jax.shard_map(shards, mesh=mesh, in_specs=in_specs, out_specs=out_specs, check_vma=False)
```

```python
import math

import jax
import jax.numpy as jnp
from jax import lax
from jax.experimental import pallas as pl
from jax.experimental.pallas import tpu as pltpu
from jax.sharding import PartitionSpec as P

D = 2048
FF = 8192
HD = 64
ROT = 32
STEP = 10

NORM_EPS = 1e-05
SCORE_SCALE = 0.125
MASKED = -1e30
ROPE_BASE = 10000.0
BETA_ONE = 0.9
BETA_TWO = 0.95
ADAM_EPS = 1e-08
WEIGHT_DECAY = 0.1

N_DP = 8
N_CTX = 8
N_TP = 2
TEAM = N_CTX * N_TP
GROUP = 1024
HALF_ROWS = 64
FEAT = D // TEAM
HIDDEN = FF // TEAM
QKV = 3 * FEAT
Q_BLOCK = 256
UNITS = HIDDEN // N_DP

BF = jnp.bfloat16
F32 = jnp.float32


def adam_update(weight, gradient, moment_one, moment_two, step_rate):
    moment_one = BETA_ONE * moment_one + (1.0 - BETA_ONE) * gradient
    moment_two = BETA_TWO * moment_two + (1.0 - BETA_TWO) * gradient * gradient
    first_hat = moment_one / (1.0 - BETA_ONE**STEP)
    second_hat = moment_two / (1.0 - BETA_TWO**STEP)
    weight = weight - step_rate * (
        first_hat / (jnp.sqrt(second_hat) + ADAM_EPS) + WEIGHT_DECAY * weight
    )
    return (weight, moment_one, moment_two)


def gelu_and_slope(hidden):
    root = math.sqrt(2.0 / math.pi)
    square = hidden * hidden
    bent = jnp.tanh(root * (hidden + 0.044715 * hidden * square))
    value = 0.5 * hidden * (1.0 + bent)
    slope = 0.5 * (1.0 + bent) + 0.5 * hidden * (1.0 - bent * bent) * root * (
        1.0 + 3.0 * 0.044715 * square
    )
    return (value, slope)


def dot(left, right, dims):
    return lax.dot_general(left, right, (dims, ((), ())), preferred_element_type=F32)


def attention_kernel(
    pre_ref,
    dattn_ref,
    cos_ref,
    sin_ref,
    tok_ref,
    start_ref,
    key_tok_ref,
    attended_ref,
    dpre_ref,
    sums_ref,
    key_scr,
    value_scr,
    dkey_scr,
    dvalue_scr,
):
    step = pl.program_id(0)
    lane = lax.broadcasted_iota(jnp.int32, (1, FEAT), 1)
    early = (lane % HD) < (ROT // 2)
    first_head = lane < HD

    def partner(value):
        return jnp.where(
            early,
            pltpu.roll(value, FEAT - ROT // 2, axis=1),
            pltpu.roll(value, ROT // 2, axis=1),
        )

    @pl.when(step == 0)
    def _():
        key = pre_ref[:, FEAT : 2 * FEAT]
        key_scr[...] = (key * cos_ref[...] + partner(key) * sin_ref[...]).astype(BF)
        value_scr[...] = pre_ref[:, 2 * FEAT :].astype(BF)
        dkey_scr[...] = jnp.zeros_like(dkey_scr)
        dvalue_scr[...] = jnp.zeros_like(dvalue_scr)
        sums_ref[...] = jnp.zeros_like(sums_ref)

    rows = pl.ds(step * Q_BLOCK, Q_BLOCK)
    cos_rows = cos_ref[rows, :]
    sin_rows = sin_ref[rows, :]
    query = pre_ref[rows, :FEAT]
    query = (query * cos_rows + partner(query) * sin_rows).astype(BF) * jnp.asarray(SCORE_SCALE, BF)
    dattn = dattn_ref[rows, :]
    key = key_scr[...]
    value = value_scr[...]
    tok = tok_ref[rows, :]
    start = start_ref[rows, :]
    key_tok = key_tok_ref[...]
    mask = (key_tok <= tok) & (key_tok >= start)
    zero = jnp.zeros((), BF)
    out_parts = []
    dquery_parts = []
    for head in range(2):
        inside = first_head if head == 0 else jnp.logical_not(first_head)
        query_h = jnp.where(inside, query, zero)
        dattn_h = jnp.where(inside, dattn, zero)
        scores = dot(query_h, key, ((1,), (1,)))
        scores = jnp.where(mask, scores, MASKED)
        top = jnp.max(scores, axis=1, keepdims=True)
        probs = jnp.exp(scores - top)
        probs = probs * (1.0 / jnp.sum(probs, axis=1, keepdims=True))
        probs_b = probs.astype(BF)
        out = dot(probs_b, value, ((1,), (0,)))
        delta = jnp.sum(
            jnp.where(inside, out, 0.0) * dattn_h.astype(F32), axis=1, keepdims=True
        )
        dprobs = dot(dattn_h, value, ((1,), (1,)))
        dscore = (probs * (dprobs - delta)).astype(BF)
        dquery_parts.append(dot(dscore, key, ((1,), (0,))))
        dkey_scr[...] += dot(dscore, query_h, ((0,), (0,)))
        dvalue_scr[...] += dot(probs_b, dattn_h, ((0,), (0,)))
        out_parts.append(out)
    attended_ref[rows, :] = jnp.where(first_head, out_parts[0], out_parts[1]).astype(BF)
    dquery = jnp.where(first_head, dquery_parts[0], dquery_parts[1]) * SCORE_SCALE
    dquery = (dquery * cos_rows - partner(dquery) * sin_rows).astype(BF)
    dpre_ref[rows, :FEAT] = dquery
    sums_ref[0:1, :FEAT] += jnp.sum(dquery.astype(F32), axis=0, keepdims=True)

    @pl.when(step == pl.num_programs(0) - 1)
    def _():
        dkey = dkey_scr[...]
        dkey = (dkey * cos_ref[...] - partner(dkey) * sin_ref[...]).astype(BF)
        dvalue = dvalue_scr[...].astype(BF)
        dpre_ref[:, FEAT : 2 * FEAT] = dkey
        dpre_ref[:, 2 * FEAT :] = dvalue
        sums_ref[0:1, FEAT : 2 * FEAT] = jnp.sum(dkey.astype(F32), axis=0, keepdims=True)
        sums_ref[0:1, 2 * FEAT :] = jnp.sum(dvalue.astype(F32), axis=0, keepdims=True)


def attention(pre, dattn, cos_table, sin_table, tok, start):
    tokens = pre.shape[0]
    whole = pl.BlockSpec(memory_space=pltpu.VMEM)
    return pl.pallas_call(
        attention_kernel,
        grid=(tokens // Q_BLOCK,),
        out_shape=(
            jax.ShapeDtypeStruct((tokens, FEAT), BF),
            jax.ShapeDtypeStruct((tokens, QKV), BF),
            jax.ShapeDtypeStruct((8, QKV), F32),
        ),
        in_specs=[whole] * 7,
        out_specs=(whole, whole, whole),
        scratch_shapes=[
            pltpu.VMEM((tokens, FEAT), BF),
            pltpu.VMEM((tokens, FEAT), BF),
            pltpu.VMEM((tokens, FEAT), F32),
            pltpu.VMEM((tokens, FEAT), F32),
        ],
        compiler_params=pltpu.CompilerParams(vmem_limit_bytes=40 * 2**20),
        cost_estimate=pl.CostEstimate(
            flops=7 * 2 * 2 * tokens * tokens * HD,
            bytes_accessed=8 * 2**20,
            transcendentals=2 * tokens * tokens,
        ),
    )(pre, dattn, cos_table, sin_table, tok[:, None], start[:, None], tok[None, :])


def swap(value):
    return lax.ppermute(value, "tp", [(0, 1), (1, 0)])


PLACED = (0, 1, 3, 2, 4, 5, 7, 6)
FLIPS = (4, 3, 1)
CTX_Y, CTX_A, CTX_B = 1, 2, 6
BLOCKS = (0, 1, 2, 3, 6, 7, 4, 5)


def place_bits():
    rank = lax.axis_index("dp")
    high = (rank // 2) % 2
    return (rank // 4, high, high ^ (rank % 2))


def exchange(value, bit):
    return lax.ppermute(value, "dp", [(d, d ^ FLIPS[bit]) for d in range(N_DP)])


def exchange_ctx(value, flip):
    return lax.ppermute(value, "ctx", [(c, c ^ flip) for c in range(N_CTX)])


def stage(*values):
    return lax.optimization_barrier(values)


def doubled(value, bit):
    other = exchange(value, bit)
    first = place_bits()[bit] == 0
    return jnp.concatenate(
        [jnp.where(first, value, other), jnp.where(first, other, value)], axis=bit
    )


def kept_and_sent(value, bit):
    own = place_bits()[bit]
    return (
        lax.dynamic_slice_in_dim(value, own, 1, bit),
        lax.dynamic_slice_in_dim(value, 1 - own, 1, bit),
    )


def added(left, right):
    return (left.astype(F32) + right.astype(F32)).astype(BF)


def halved(value, bit):
    kept, sent = kept_and_sent(value, bit)
    return added(kept, exchange(sent, bit))


def cube(value):
    return value.reshape((2, 2, 2, value.shape[0] // N_DP) + value.shape[1:])


def placed(value, axis):
    shape = value.shape
    blocks = value.reshape(shape[:axis] + (N_DP, shape[axis] // N_DP) + shape[axis + 1 :])
    blocks = [lax.slice_in_dim(blocks, d, d + 1, axis=axis) for d in PLACED]
    return jnp.concatenate(blocks, axis=axis).reshape(shape)


def rows_to_team(value):
    pairs = [
        (d * N_CTX + c, PLACED[c] * N_CTX + d) for d in range(N_DP) for c in range(N_CTX)
    ]
    return lax.ppermute(value, ("dp", "ctx"), pairs)


def rows_to_owner(value):
    pairs = [
        (PLACED[c] * N_CTX + d, d * N_CTX + c) for d in range(N_DP) for c in range(N_CTX)
    ]
    return lax.ppermute(value, ("dp", "ctx"), pairs)


def shards(
    block_input,
    out_cotangent,
    token_order,
    seq_lengths,
    w_qkv,
    w_out,
    w_fc1,
    w_fc2,
    vectors,
    mom1_qkv,
    mom1_out,
    mom1_fc1,
    mom1_fc2,
    mom1_vec,
    mom2_qkv,
    mom2_out,
    mom2_fc1,
    mom2_fc2,
    mom2_vec,
):
    ctx_rank = lax.axis_index("ctx")
    tp_rank = lax.axis_index("tp")
    team_rank = tp_rank * N_CTX + ctx_rank
    own_d = D // (N_DP * N_CTX)
    half_rows = N_CTX * HALF_ROWS
    lanes = QKV + HIDDEN

    def half(value):
        return lax.dynamic_slice_in_dim(value, tp_rank * HALF_ROWS, HALF_ROWS, 0)

    x_own = placed(half(block_input), 1)
    dy_own = half(out_cotangent)
    tok_own = half(token_order[0])
    tok_pair = jnp.stack([tok_own // 32, tok_own % 32], axis=1).astype(BF)
    x_wide = jnp.concatenate([x_own, jnp.pad(tok_pair, ((0, 0), (0, 126)))], axis=1)
    parts = [w_qkv[:, part].reshape(own_d, N_CTX, FEAT) for part in range(3)]
    units = placed(w_fc1, 1).reshape(own_d, N_DP, N_CTX, UNITS).transpose(0, 2, 1, 3)
    columns = jnp.concatenate(parts + [units.reshape(own_d, N_CTX, HIDDEN)], axis=2).astype(BF)
    columns = lax.all_to_all(columns.transpose(1, 0, 2), "ctx", 0, 0, tiled=True)
    columns = columns.reshape(N_CTX * own_d, lanes)
    out = rows_to_team(w_out[0].astype(BF))
    x_two = jnp.concatenate([x_wide, exchange_ctx(x_wide, CTX_Y)], axis=0)
    dy_two = jnp.concatenate([dy_own, exchange_ctx(dy_own, CTX_Y)], axis=0)
    columns, out, x_two, dy_two = stage(columns, out, x_two, dy_two)

    rows = jnp.concatenate([out, w_fc2[0].astype(BF)], axis=0)[None, None, None]
    columns = doubled(columns[None, None, None], 0)
    rows = doubled(rows, 0)
    x_four = jnp.concatenate([x_two, exchange_ctx(x_two, CTX_A)], axis=0)
    dy_four = jnp.concatenate([dy_two, exchange_ctx(dy_two, CTX_B)], axis=0)
    columns, rows, x_four, dy_four = stage(columns, rows, x_four, dy_four)

    columns = doubled(columns, 2)
    rows = doubled(rows, 1)
    x_mine = jnp.concatenate([x_four, exchange_ctx(x_four, CTX_B)], axis=0)
    dy_other = exchange_ctx(dy_four, CTX_A)
    two = 2 * HALF_ROWS
    dy_mine = jnp.concatenate(
        [dy_four[:two], dy_other[:two], dy_four[two:], dy_other[two:]], axis=0
    )
    columns, rows, x_mine, dy_mine = stage(columns, rows, x_mine, dy_mine)

    mat_in = doubled(columns, 1).reshape(D, lanes)
    rows = doubled(rows, 2).reshape(N_DP, FEAT // N_DP + UNITS, D)
    mat_out = rows[:, : FEAT // N_DP].reshape(FEAT, D)
    mat_fc2 = rows[:, FEAT // N_DP :].reshape(HIDDEN, D)
    x_wide = jnp.concatenate([x_mine, swap(x_mine)], axis=0)
    dy = jnp.concatenate([dy_mine, swap(dy_mine)], axis=0)
    tok_pair = x_wide[:, D : D + 2].astype(jnp.int32)
    tok = tok_pair[:, 0] * 32 + tok_pair[:, 1]

    def normal(value):
        value = value.astype(F32)
        centered = value - jnp.mean(value, axis=-1, keepdims=True)
        inv_std = lax.rsqrt(jnp.mean(centered * centered, axis=-1, keepdims=True) + NORM_EPS)
        return (centered * inv_std, inv_std)

    norm_gain = placed(vectors[9], 0)
    norm_shift = placed(vectors[10], 0)
    normed = (normal(x_wide[:, :D])[0] * norm_gain + norm_shift).astype(BF)

    ends = jnp.cumsum(seq_lengths[0])
    starts = ends - seq_lengths[0]
    inside = (tok[:, None] >= starts[None, :]) & (tok[:, None] < ends[None, :])
    first = jnp.sum(jnp.where(inside, starts[None, :], 0), axis=1)
    position = (tok - first).astype(F32)
    lane = jnp.arange(FEAT) % HD
    inverse = ROPE_BASE ** (-(2.0 * (lane % (ROT // 2)).astype(F32)) / ROT)
    inverse = jnp.where(lane < ROT, inverse, 0.0)
    rotation = position[:, None] * inverse[None, :]
    cos_table = jnp.cos(rotation)
    sin_table = jnp.sin(rotation) * jnp.where(lane < ROT // 2, -1.0, 1.0)
    mat_in, mat_out, mat_fc2, normed, dy, cos_table, sin_table = stage(
        mat_in, mat_out, mat_fc2, normed, dy, cos_table, sin_table
    )

    bias_qkv = lax.dynamic_slice(vectors, (0, team_rank * FEAT), (3, FEAT))
    bias_fc1 = vectors[3:7].reshape(N_TP, N_DP, N_CTX, UNITS)
    bias_fc1 = lax.dynamic_slice(bias_fc1, (tp_rank, 0, ctx_rank, 0), (1, N_DP, 1, UNITS))
    bias_fc1 = placed(bias_fc1.reshape(HIDDEN), 0)
    inner = dot(normed, mat_in, ((1,), (0,)))
    hidden = inner[:, QKV:] + bias_fc1
    pre_qkv = inner[:, :QKV] + bias_qkv.reshape(QKV)
    active, slope = gelu_and_slope(hidden)
    active = active.astype(BF)
    dhid = (dot(dy, mat_fc2, ((1,), (1,))) * slope).astype(BF)
    grad_fc2 = cube(dot(active, dy, ((0,), (0,))).astype(BF))
    grad_fc1 = cube(dot(normed, dhid, ((0,), (0,))).astype(BF))
    fc2_kept, fc2_sent = kept_and_sent(grad_fc2, 1)
    fc1_kept, fc1_sent = kept_and_sent(grad_fc1, 2)
    fc2_kept, fc2_sent, fc1_kept, fc1_sent, pre_qkv, active, dhid = stage(
        fc2_kept, fc2_sent, fc1_kept, fc1_sent, pre_qkv, active, dhid
    )

    grad_fc2 = added(fc2_kept, exchange(fc2_sent, 1))
    grad_fc1 = added(fc1_kept, exchange(fc1_sent, 2))
    dattn = dot(dy, mat_out, ((1,), (1,))).astype(BF)
    attended, dpre, dpre_sums = attention(pre_qkv, dattn, cos_table, sin_table, tok, first)
    grad_out = cube(dot(attended, dy, ((0,), (0,))).astype(BF))
    grad_qkv = cube(dot(normed, dpre, ((0,), (0,))).astype(BF))
    out_kept, out_sent = kept_and_sent(grad_out, 1)
    qkv_kept, qkv_sent = kept_and_sent(grad_qkv, 2)
    grad_fc2, grad_fc1, out_kept, out_sent, qkv_kept, qkv_sent, attended, dpre = stage(
        grad_fc2, grad_fc1, out_kept, out_sent, qkv_kept, qkv_sent, attended, dpre
    )

    rows = jnp.concatenate([added(out_kept, exchange(out_sent, 1)), grad_fc2], axis=3)
    columns = jnp.concatenate([added(qkv_kept, exchange(qkv_sent, 2)), grad_fc1], axis=4)
    inner_grad = jnp.concatenate([dpre, dhid], axis=1)
    normed_part = dot(inner_grad, mat_in, ((1,), (1,)))
    branch = dot(attended, mat_out, ((1,), (0,))) + dot(active, mat_fc2, ((1,), (0,)))

    def own_half(value):
        mine = value[:half_rows] + swap(value[half_rows:].astype(BF)).astype(F32)
        return mine.astype(BF).reshape(N_CTX, HALF_ROWS, D)

    normed_half = own_half(normed_part)
    branch_half = own_half(branch)
    norm_terms = jnp.stack(
        [
            jnp.sum(normed_part * normal(x_wide[:, :D])[0], axis=0),
            jnp.sum(normed_part, axis=0),
        ]
    )
    dy_sum = jnp.sum(dy.astype(F32), axis=0)
    dy_sum = lax.dynamic_slice_in_dim(dy_sum, team_rank * FEAT, FEAT)
    terms = jnp.concatenate(
        [dpre_sums[0], dy_sum, jnp.sum(dhid.astype(F32), axis=0), norm_terms.reshape(2 * D)]
    ).reshape(1, 40, 128)
    rows_kept, rows_sent = kept_and_sent(rows, 2)
    columns_kept, columns_sent = kept_and_sent(columns, 1)
    rows_kept, rows_sent, columns_kept, columns_sent, normed_half, branch_half, terms = stage(
        rows_kept, rows_sent, columns_kept, columns_sent, normed_half, branch_half, terms
    )

    def to_neighbour(value, masks, flip, later):
        keep = [0]
        for other in later:
            keep = keep + [m ^ other for m in keep]
        kept = jnp.concatenate([value[j : j + 1] for j in map(masks.index, keep)], axis=0)
        sent = [masks.index(m ^ flip) for m in keep]
        sent = jnp.concatenate([value[j : j + 1] for j in sent], axis=0)
        return added(kept, exchange_ctx(sent, flip)), tuple(keep)

    rows = added(rows_kept, exchange(rows_sent, 2))
    columns = added(columns_kept, exchange(columns_sent, 1))
    normed_half, normed_masks = to_neighbour(normed_half, BLOCKS, CTX_B, (CTX_A, CTX_Y))
    branch_half, branch_masks = to_neighbour(branch_half, BLOCKS, CTX_A, (CTX_B, CTX_Y))
    rows, columns, normed_half, branch_half = stage(rows, columns, normed_half, branch_half)
    terms = lax.all_to_all(
        jnp.broadcast_to(terms, (N_DP,) + terms.shape[1:]), "dp", 0, 0, tiled=True
    )
    terms = jnp.sum(terms, axis=0)
    rows = halved(rows, 0)
    columns = halved(columns, 0)
    normed_half, normed_masks = to_neighbour(normed_half, normed_masks, CTX_A, (CTX_Y,))
    branch_half, branch_masks = to_neighbour(branch_half, branch_masks, CTX_B, (CTX_Y,))
    rows, columns, normed_half, branch_half, terms = stage(
        rows, columns, normed_half, branch_half, terms
    )
    normed_half, _ = to_neighbour(normed_half, normed_masks, CTX_Y, ())
    branch_half, _ = to_neighbour(branch_half, branch_masks, CTX_Y, ())
    normed_grad = normed_half[0].astype(F32)
    branch = branch_half[0].astype(F32)

    def both_halves(value):
        other = swap(value)
        first_core = tp_rank == 0
        return jnp.concatenate(
            [jnp.where(first_core, value, other), jnp.where(first_core, other, value)], axis=0
        )

    block_output = half(block_input).astype(F32) + branch + vectors[7] + vectors[8]
    block_output = both_halves(block_output.astype(BF))
    own_normal, inv_std = normal(x_own)
    scaled_grad = normed_grad * norm_gain
    input_grad = inv_std * (
        scaled_grad
        - jnp.mean(scaled_grad, axis=-1, keepdims=True)
        - own_normal * jnp.mean(scaled_grad * own_normal, axis=-1, keepdims=True)
    )
    input_grad = both_halves(dy_own.astype(F32) + placed(input_grad, 1))

    term_rows = -(-terms.size // lanes)
    terms = jnp.pad(terms.reshape(-1), (0, term_rows * lanes - terms.size))
    back = jnp.concatenate(
        [
            columns.astype(F32).reshape(N_CTX, own_d, lanes),
            jnp.broadcast_to(terms.reshape(1, term_rows, lanes), (N_CTX, term_rows, lanes)),
        ],
        axis=1,
    )
    back = lax.all_to_all(back, "ctx", 0, 0, tiled=True)
    columns = back[:, :own_d].transpose(1, 0, 2)
    sum_qkv = jnp.stack(
        [
            columns[:, :, part * FEAT : (part + 1) * FEAT].reshape(own_d, N_CTX * FEAT)
            for part in range(3)
        ],
        axis=1,
    )
    sum_fc1 = columns[:, :, QKV:].reshape(own_d, N_CTX, N_DP, UNITS).transpose(0, 2, 1, 3)
    sum_fc1 = placed(sum_fc1.reshape(own_d, N_CTX * HIDDEN), 1)
    rows = rows[0, 0, 0]
    sum_out = rows_to_owner(rows[: FEAT // N_DP]).astype(F32)[None]
    sum_fc2 = rows[FEAT // N_DP :].astype(F32)[None]
    terms = back[:, own_d:].reshape(N_CTX, term_rows * lanes)
    team = terms[:, : 4 * FEAT].reshape(N_CTX, 4, FEAT).transpose(1, 0, 2).reshape(4, D // N_TP)
    team = jnp.concatenate(
        [
            team.reshape(4 * D // N_TP),
            placed(
                terms[:, 4 * FEAT : 4 * FEAT + HIDDEN]
                .reshape(N_CTX, N_DP, UNITS)
                .transpose(1, 0, 2)
                .reshape(FF // N_TP),
                0,
            ),
            jnp.sum(terms[:, 4 * FEAT + HIDDEN : 4 * FEAT + HIDDEN + 2 * D], axis=0),
        ]
    ).reshape(12, D // N_TP)
    other = swap(team)
    first_core = tp_rank == 0
    low = jnp.where(first_core, team, other)
    high = jnp.where(first_core, other, team)
    features = jnp.concatenate([low[:4], high[:4]], axis=1)
    hidden_sums = jnp.concatenate([low[4:8], high[4:8]], axis=0).reshape(FF // D, D)
    norm_sums = placed((low[8:] + high[8:]).reshape(2, D), 1)
    vector_grad = jnp.concatenate(
        [features[:3], hidden_sums, features[3:], features[3:], norm_sums], axis=0
    )

    new_qkv = adam_update(w_qkv, sum_qkv, mom1_qkv, mom2_qkv, 2.0 / math.sqrt(D))
    new_out = adam_update(w_out, sum_out, mom1_out, mom2_out, 16.0 / math.sqrt(D))
    new_fc1 = adam_update(w_fc1, sum_fc1, mom1_fc1, mom2_fc1, 2.0 / math.sqrt(D))
    new_fc2 = adam_update(w_fc2, sum_fc2, mom1_fc2, mom2_fc2, 2.0 / math.sqrt(FF))
    new_vec = adam_update(vectors, vector_grad, mom1_vec, mom2_vec, 0.2)
    return (
        block_output,
        input_grad,
        new_qkv[0],
        new_out[0],
        new_fc1[0],
        new_fc2[0],
        new_vec[0],
        new_qkv[1],
        new_out[1],
        new_fc1[1],
        new_fc2[1],
        new_vec[1],
        new_qkv[2],
        new_out[2],
        new_fc1[2],
        new_fc2[2],
        new_vec[2],
    )


def solution(mesh):
    in_specs = (
        P(("dp", "ctx"), None),
        P(("dp", "ctx"), None),
        P("dp", "ctx"),
        P("dp", None),
        P(("dp", "ctx"), None, "tp"),
        P("tp", ("dp", "ctx"), None),
        P(("dp", "ctx"), "tp"),
        P("tp", ("dp", "ctx"), None),
        P(),
        P(("dp", "ctx"), None, "tp"),
        P("tp", ("dp", "ctx"), None),
        P(("dp", "ctx"), "tp"),
        P("tp", ("dp", "ctx"), None),
        P(),
        P(("dp", "ctx"), None, "tp"),
        P("tp", ("dp", "ctx"), None),
        P(("dp", "ctx"), "tp"),
        P("tp", ("dp", "ctx"), None),
        P(),
    )
    out_specs = (
        P(("dp", "ctx"), None),
        P(("dp", "ctx"), None),
        P(("dp", "ctx"), None, "tp"),
        P("tp", ("dp", "ctx"), None),
        P(("dp", "ctx"), "tp"),
        P("tp", ("dp", "ctx"), None),
        P(),
        P(("dp", "ctx"), None, "tp"),
        P("tp", ("dp", "ctx"), None),
        P(("dp", "ctx"), "tp"),
        P("tp", ("dp", "ctx"), None),
        P(),
        P(("dp", "ctx"), None, "tp"),
        P("tp", ("dp", "ctx"), None),
        P(("dp", "ctx"), "tp"),
        P("tp", ("dp", "ctx"), None),
        P(),
    )
    return jax.shard_map(shards, mesh=mesh, in_specs=in_specs, out_specs=out_specs, check_vma=False)
```

```python
import math

import jax
import jax.numpy as jnp
from jax import lax
from jax.experimental import pallas as pl
from jax.experimental.pallas import tpu as pltpu
from jax.sharding import PartitionSpec as P

D = 2048
FF = 8192
HD = 64
ROT = 32
STEP = 10

NORM_EPS = 1e-05
SCORE_SCALE = 0.125
MASKED = -1e30
ROPE_BASE = 10000.0
BETA_ONE = 0.9
BETA_TWO = 0.95
ADAM_EPS = 1e-08
WEIGHT_DECAY = 0.1

N_DP = 8
N_CTX = 8
N_TP = 2
TEAM = N_CTX * N_TP
GROUP = 1024
HALF_ROWS = 64
FEAT = D // TEAM
HIDDEN = FF // TEAM
QKV = 3 * FEAT
Q_BLOCK = 256
UNITS = HIDDEN // N_DP

BF = jnp.bfloat16
F32 = jnp.float32


def adam_update(weight, gradient, moment_one, moment_two, step_rate):
    moment_one = BETA_ONE * moment_one + (1.0 - BETA_ONE) * gradient
    moment_two = BETA_TWO * moment_two + (1.0 - BETA_TWO) * gradient * gradient
    first_hat = moment_one / (1.0 - BETA_ONE**STEP)
    second_hat = moment_two / (1.0 - BETA_TWO**STEP)
    weight = weight - step_rate * (
        first_hat / (jnp.sqrt(second_hat) + ADAM_EPS) + WEIGHT_DECAY * weight
    )
    return (weight, moment_one, moment_two)


def gelu_and_slope(hidden):
    root = math.sqrt(2.0 / math.pi)
    square = hidden * hidden
    bent = jnp.tanh(root * (hidden + 0.044715 * hidden * square))
    value = 0.5 * hidden * (1.0 + bent)
    slope = 0.5 * (1.0 + bent) + 0.5 * hidden * (1.0 - bent * bent) * root * (
        1.0 + 3.0 * 0.044715 * square
    )
    return (value, slope)


def dot(left, right, dims):
    return lax.dot_general(left, right, (dims, ((), ())), preferred_element_type=F32)


WHOLE = pl.BlockSpec(memory_space=pltpu.VMEM)
SCALAR = pl.BlockSpec(memory_space=pltpu.SMEM)
ROOM = pltpu.CompilerParams(vmem_limit_bytes=60 * 2**20)


def loaded(kernel, out_shape, operands, scalars=(), scratch=(), flops=0, late=False):
    lists = [list(v) if isinstance(v, (list, tuple)) else [v] for v in operands]
    arrays = [v for values in lists for v in values]
    held_shapes = [(sum(v.shape[0] for v in vs),) + vs[0].shape[1:] for vs in lists]
    cuts = []
    for i, values in enumerate(lists):
        at = 0
        for part, value in enumerate(values):
            rows, pieces = value.shape[0], 1
            while value.nbytes // pieces > 2**19 and rows % (pieces * 32) == 0:
                pieces = pieces * 2
            size = rows // pieces
            cuts = cuts + [(i, part, k * size, at + k * size, size) for k in range(pieces)]
            at = at + rows
    first = [sum(len(v) for v in lists[:i]) for i in range(len(lists))]
    counts = (len(scalars), len(arrays), len(out_shape), len(lists), len(out_shape))

    def body(*refs):
        parts, at = [], 0
        for count in counts:
            parts.append(refs[at : at + count])
            at = at + count
        given, ins, outs, held, written = parts
        rest, in_sems, out_sems = refs[at:-2], refs[-2], refs[-1]
        copies, waited, sent = [], set(), {}
        for k, (i, part, source, to, size) in enumerate(cuts):
            copies.append(
                pltpu.make_async_copy(
                    ins[first[i] + part].at[pl.ds(source, size)],
                    held[i].at[pl.ds(to, size)],
                    in_sems.at[k],
                )
            )
            copies[-1].start()

        def ready(operand, array=None):
            for k, (i, part, _, _, _) in enumerate(cuts):
                if i == operand and array in (None, part) and k not in waited:
                    copies[k].wait()
                    waited.add(k)

        def done(k):
            sent[k] = pltpu.make_async_copy(written[k], outs[k], out_sems.at[k])
            sent[k].start()

        if late:
            kernel(ready, done, *given, *held, *written, *rest)
        else:
            for i in range(len(lists)):
                ready(i)
            kernel(*given, *held, *written, *rest)
        for i in range(len(lists)):
            ready(i)
        for k in range(len(out_shape)):
            if k not in sent:
                done(k)
        for copy in sent.values():
            copy.wait()

    moved = sum(v.nbytes for v in arrays) + sum(
        math.prod(v.shape) * jnp.dtype(v.dtype).itemsize for v in out_shape
    )
    anywhere = pl.BlockSpec(memory_space=pl.ANY)
    return pl.pallas_call(
        body,
        out_shape=tuple(out_shape),
        in_specs=[SCALAR] * len(scalars) + [anywhere] * len(arrays),
        out_specs=(anywhere,) * len(out_shape),
        scratch_shapes=[pltpu.VMEM(h, vs[0].dtype) for h, vs in zip(held_shapes, lists)]
        + [pltpu.VMEM(v.shape, v.dtype) for v in out_shape]
        + list(scratch)
        + [pltpu.SemaphoreType.DMA((len(cuts),)), pltpu.SemaphoreType.DMA((len(out_shape),))],
        compiler_params=ROOM,
        cost_estimate=pl.CostEstimate(flops=flops, bytes_accessed=moved, transcendentals=0),
    )(*scalars, *arrays)


TILES = D // 128
COLS = (QKV + HIDDEN) // 128
OUT_ROWS = FEAT // N_DP
COL_ROWS = N_CTX * COLS * (D // N_DP // N_CTX)
PIECE = COL_ROWS + TILES * (OUT_ROWS + UNITS)
THIRD = PIECE // 3


def pack_kernel(qkv_ref, fc1_ref, tok_ref, out_ref, fc2_ref, columns_ref, outs_ref, fc2s_ref):
    for c in range(N_CTX):
        for part in range(3):
            columns_ref[c, part] = qkv_ref[part, :, c * FEAT : (c + 1) * FEAT].astype(BF)
        for pair in range(HIDDEN // 128):
            at = [(2 * pair + e) * N_CTX * UNITS + c * UNITS for e in range(2)]
            columns_ref[c, 3 + pair] = jnp.concatenate(
                [fc1_ref[:, i : i + UNITS] for i in at], axis=1
            ).astype(BF)
        columns_ref[c, COLS] = tok_ref[...].astype(BF)
    for tile in range(TILES):
        outs_ref[tile] = out_ref[:, tile * 128 : (tile + 1) * 128].astype(BF)
        fc2s_ref[tile] = fc2_ref[:, tile * 128 : (tile + 1) * 128].astype(BF)


MASKS = (0, 4, 1, 3, 4 ^ 1, 4 ^ 3, 1 ^ 3, 4 ^ 1 ^ 3)


NT = ((1,), (1,))
NN = ((1,), (0,))
TN = ((0,), (0,))


def place(block, piece, qkv, fc1, out, fc2):
    own_d = D // N_DP // N_CTX
    for src in range(N_CTX):
        at = pl.ds(pl.multiple_of(block * (D // N_DP) + src * own_d, own_d), own_d)
        for j in range(COLS):
            start = (src * COLS + j) * own_d
            rows = piece[start : start + own_d, :]
            if j < 3:
                qkv[at, j * 128 : (j + 1) * 128] = rows
            else:
                fc1[at, (j - 3) * 128 : (j - 2) * 128] = rows
    for to, start, count in (
        (out, COL_ROWS, OUT_ROWS),
        (fc2, COL_ROWS + TILES * OUT_ROWS, UNITS),
    ):
        at = pl.ds(pl.multiple_of(block * count, count), count)
        for tile in range(TILES):
            to[at, tile * 128 : (tile + 1) * 128] = piece[
                start + tile * count : start + (tile + 1) * count, :
            ]


def fold(block, cols_ref, rows_ref, piece):
    own_d = D // N_DP // N_CTX
    n_cols = cols_ref.shape[1] // 128
    n_rows = rows_ref.shape[0] // N_DP
    for src in range(N_CTX):
        at = pl.ds(pl.multiple_of(block * (D // N_DP) + src * own_d, own_d), own_d)
        for j in range(n_cols):
            to = (src * n_cols + j) * own_d
            piece[to : to + own_d, :] = cols_ref[at, j * 128 : (j + 1) * 128]
    at = pl.ds(pl.multiple_of(block * n_rows, n_rows), n_rows)
    for tile in range(TILES):
        to = N_CTX * n_cols * own_d + tile * n_rows
        piece[to : to + n_rows, :] = rows_ref[at, tile * 128 : (tile + 1) * 128]


def normal(value):
    value = value.astype(F32)
    centered = value - jnp.mean(value, axis=-1, keepdims=True)
    inv_std = lax.rsqrt(jnp.mean(centered * centered, axis=-1, keepdims=True) + NORM_EPS)
    return (centered * inv_std, inv_std)


def norm_kernel(ready, done, x, dy, gain, shift, normed, dy_out):
    ready(2)
    ready(3)
    for part in range(4):
        at = slice(part * 2 * HALF_ROWS, (part + 1) * 2 * HALF_ROWS)
        ready(0, part)
        normed[at, :] = (normal(x[at, :])[0] * gain[...] + shift[...]).astype(BF)
    done(0)
    ready(1)
    dy_out[...] = dy[...]


def half_branch(normed, dy, mats, biases, outs):
    qkv, fc1, out, fc2 = mats
    bias_fc1, bias_qkv = biases
    active, dhid, sums, pre, dattn = outs
    value, slope = gelu_and_slope(dot(normed[...], fc1[...], NN) + bias_fc1[...])
    active[...] = value.astype(BF)
    grad = (dot(dy[...], fc2[...], NT) * slope).astype(BF)
    dhid[...] = grad
    sums[...] = jnp.sum(grad.astype(F32), axis=0, keepdims=True)
    pre[...] = dot(normed[...], qkv[...], NN) + bias_qkv[...]
    dattn[...] = dot(dy[...], out[...], NT).astype(BF)


def place_kernel(ready, done, rank_ref, *refs):
    pieces, (normed, dy, *biases), outs = refs[:N_DP], refs[N_DP : N_DP + 4], refs[N_DP + 4 :]
    mats = outs[:4]
    for k, flip in enumerate(MASKS):
        ready(k)
        place(rank_ref[0] ^ flip, pieces[k], *mats)
    for k in range(4):
        done(k)
        ready(N_DP + k)
    half_branch(normed, dy, mats, biases, outs[4:])


def feed_forward_kernel(ready, done, rank_ref, *refs):
    normed_mine, dy_mine, active_mine, dhid_mine, normed, dy, *mats = refs[:10]
    biases, outs, grads = refs[10:12], refs[12:17], refs[17 : 17 + N_DP]
    grad_fc1, grad_fc2 = refs[17 + N_DP :]
    for i in range(4, 12):
        ready(i)
    half_branch(normed, dy, mats, biases, outs)
    active, dhid = outs[:2]
    for k in range(5):
        done(k)
    for i in range(4):
        ready(i)
    for k in range(D // HIDDEN):
        at = slice(k * HIDDEN, (k + 1) * HIDDEN)
        grad_fc2[:, at] = (
            dot(active_mine[...], dy_mine[:, at], TN) + dot(active[...], dy[:, at], TN)
        ).astype(BF)
        grad_fc1[at, :] = (
            dot(normed_mine[:, at], dhid_mine[...], TN) + dot(normed[:, at], dhid[...], TN)
        ).astype(BF)
    for k in reversed(range(N_DP)):
        fold(rank_ref[0] ^ MASKS[k], grad_fc1, grad_fc2, grads[k])
        done(5 + k)


def attention_kernel(
    pre,
    dattn_all,
    cos,
    sin,
    tok,
    start,
    key_tok,
    attended,
    dpre,
    sums,
    query_scr,
    key_scr,
    value_scr,
    dkey_scr,
    dvalue_scr,
):
    lane = lax.broadcasted_iota(jnp.int32, (1, FEAT), 1)
    early = (lane % HD) < (ROT // 2)
    first_head = lane < HD

    def partner(value):
        return jnp.where(
            early,
            pltpu.roll(value, FEAT - ROT // 2, axis=1),
            pltpu.roll(value, ROT // 2, axis=1),
        )

    query = pre[:, :FEAT]
    query = (query * cos[...] + partner(query) * sin[...]).astype(BF)
    query_scr[...] = query * jnp.asarray(SCORE_SCALE, BF)
    key = pre[:, FEAT : 2 * FEAT]
    key_scr[...] = (key * cos[...] + partner(key) * sin[...]).astype(BF)
    value_scr[...] = pre[:, 2 * FEAT :].astype(BF)
    dkey_scr[...] = jnp.zeros_like(dkey_scr)
    dvalue_scr[...] = jnp.zeros_like(dvalue_scr)

    @pl.loop(0, GROUP // Q_BLOCK)
    def _(step):
        rows = pl.ds(pl.multiple_of(step * Q_BLOCK, Q_BLOCK), Q_BLOCK)
        query = query_scr[rows, :]
        dattn = dattn_all[rows, :]
        key = key_scr[...]
        value = value_scr[...]
        token = key_tok[...]
        mask = (token <= tok[rows, :]) & (token >= start[rows, :])
        zero = jnp.zeros((), BF)
        out_parts = []
        dquery_parts = []
        for head in range(2):
            inside = first_head if head == 0 else jnp.logical_not(first_head)
            query_h = jnp.where(inside, query, zero)
            dattn_h = jnp.where(inside, dattn, zero)
            scores = dot(query_h, key, NT)
            scores = jnp.where(mask, scores, MASKED)
            top = jnp.max(scores, axis=1, keepdims=True)
            probs = jnp.exp(scores - top)
            probs = probs * (1.0 / jnp.sum(probs, axis=1, keepdims=True))
            probs_b = probs.astype(BF)
            mixed = dot(probs_b, value, NN)
            delta = jnp.sum(
                jnp.where(inside, mixed, 0.0) * dattn_h.astype(F32), axis=1, keepdims=True
            )
            dprobs = dot(dattn_h, value, NT)
            dscore = (probs * (dprobs - delta)).astype(BF)
            dquery_parts.append(dot(dscore, key, NN))
            dkey_scr[...] += dot(dscore, query_h, TN)
            dvalue_scr[...] += dot(probs_b, dattn_h, TN)
            out_parts.append(mixed)
        attended[rows, :] = jnp.where(first_head, out_parts[0], out_parts[1]).astype(BF)
        dquery = jnp.where(first_head, dquery_parts[0], dquery_parts[1]) * SCORE_SCALE
        dpre[rows, :FEAT] = (dquery * cos[rows, :] - partner(dquery) * sin[rows, :]).astype(BF)

    dkey = dkey_scr[...]
    dpre[:, FEAT : 2 * FEAT] = (dkey * cos[...] - partner(dkey) * sin[...]).astype(BF)
    dpre[:, 2 * FEAT :] = dvalue_scr[...].astype(BF)
    sums[...] = jnp.sum(dpre[...].astype(F32), axis=0, keepdims=True)


def heads_kernel(ready, done, rank_ref, *refs):
    attended, dpre, active, dhid, qkv, fc1, out, fc2, normed, dy = refs[:10]
    normed_out, branch_out, normed_part, branch_part = refs[10:14]
    grads, (grad_qkv, grad_out) = refs[14 : 14 + N_DP], refs[14 + N_DP :]
    for i in range(8):
        ready(i)
    half = GROUP // 2
    for k in range(D // HIDDEN):
        at = slice(k * HIDDEN, (k + 1) * HIDDEN)
        for rows, to in ((slice(half, GROUP), normed_out), (slice(0, half), normed_part)):
            to[:, at] = (
                dot(dpre[rows, :], qkv[at, :], NT) + dot(dhid[rows, :], fc1[at, :], NT)
            ).astype(BF)
        for rows, to in ((slice(half, GROUP), branch_out), (slice(0, half), branch_part)):
            to[:, at] = (
                dot(attended[rows, :], out[:, at], NN) + dot(active[rows, :], fc2[:, at], NN)
            ).astype(BF)
    for k in range(4):
        done(k)
    ready(8)
    ready(9)
    for k in range(D // HIDDEN):
        at = slice(k * HIDDEN, (k + 1) * HIDDEN)
        grad_qkv[at, :] = dot(normed[:, at], dpre[...], TN).astype(BF)
        grad_out[:, at] = dot(attended[...], dy[:, at], TN).astype(BF)
    for k in reversed(range(N_DP)):
        fold(rank_ref[0] ^ MASKS[k], grad_qkv, grad_out, grads[k])
        done(4 + k)


def rows_kernel(ready, done, normed_ref, normed_in, branch_ref, branch_in, x, *outs):
    normed_keep, normed_send, branch_keep, branch_send, gain_ref, shift_ref = outs
    block = 2 * HALF_ROWS
    ready(2)
    ready(3)
    for i in range(4):
        rows, to = slice(i * block, (i + 1) * block), branch_keep if i % 2 == 0 else branch_send
        total = branch_ref[rows, :].astype(F32) + branch_in[rows, :].astype(F32)
        to[(i // 2) * block : (i // 2 + 1) * block, :] = total.astype(BF)
    done(2)
    done(3)
    ready(0)
    ready(1)
    ready(4)
    gain = jnp.zeros((1, D), F32)
    shift = jnp.zeros((1, D), F32)
    for i in range(4):
        rows, to = slice(i * block, (i + 1) * block), normed_keep if i < 2 else normed_send
        total = normed_ref[rows, :].astype(F32) + normed_in[rows, :].astype(F32)
        gain = gain + jnp.sum(total * normal(x[rows, :])[0], axis=0, keepdims=True)
        shift = shift + jnp.sum(total, axis=0, keepdims=True)
        to[(i % 2) * block : (i % 2 + 1) * block, :] = total.astype(BF)
    gain_ref[...] = gain
    shift_ref[...] = shift


def combine(*jobs):
    operands = [value for values, _ in jobs for value in values]
    outs = [
        jax.ShapeDtypeStruct((stop - start, values[0].shape[1]), BF)
        for values, ranges in jobs
        for start, stop in ranges
    ]

    def kernel(*refs):
        ins, to = list(refs[: len(operands)]), list(refs[len(operands) :])
        for values, ranges in jobs:
            mine, ins = ins[: len(values)], ins[len(values) :]
            for start, stop in ranges:
                total = mine[0][start:stop, :].astype(F32)
                for ref in mine[1:]:
                    total = total + ref[start:stop, :].astype(F32)
                to.pop(0)[...] = total.astype(BF)

    return loaded(kernel, outs, operands)


def patched(pieces, others, starts):
    count = len(pieces)

    def kernel(*refs):
        for i in range(count):
            piece, other, to = refs[i], refs[count + i], refs[2 * count + i]
            start, stop = starts[i], starts[i] + other.shape[0]
            if start > 0:
                to[:start, :] = piece[:start, :]
            to[start:stop, :] = (piece[start:stop, :].astype(F32) + other[...].astype(F32)).astype(BF)
            if stop < piece.shape[0]:
                to[stop:, :] = piece[stop:, :]

    outs = [jax.ShapeDtypeStruct(v.shape, BF) for v in pieces]
    return loaded(kernel, outs, list(pieces) + list(others))


def finish_kernel(core_ref, gain_ref, bias_ref, x_ref, dy_ref, *refs):
    (normed_own, branch_own, normed_other, branch_other), (output_ref, grad_ref) = refs[:4], refs[4:]
    core = core_ref[0]
    for side, normed_in, branch_in in (
        (core, normed_own, branch_own),
        (1 - core, normed_other, branch_other),
    ):
        rows = pl.ds(pl.multiple_of(side * HALF_ROWS, HALF_ROWS), HALF_ROWS)
        value = x_ref[rows, :]
        normal_x, inv_std = normal(value)
        value = value.astype(F32)
        output_ref[rows, :] = (value + branch_in[...].astype(F32) + bias_ref[...]).astype(BF)
        scaled = normed_in[...].astype(F32) * gain_ref[...]
        grad_ref[rows, :] = dy_ref[rows, :].astype(F32) + inv_std * (
            scaled
            - jnp.mean(scaled, axis=-1, keepdims=True)
            - normal_x * jnp.mean(scaled * normal_x, axis=-1, keepdims=True)
        )


def vector_kernel(core_ref, own_ref, other_ref, *refs):
    (vectors_ref, first_ref, second_ref), outs, grad = refs[:3], refs[3:6], refs[6]
    first_core = core_ref[0] == 0
    units = FF // N_TP // D
    gain = jnp.zeros((TILES, 128), F32)
    shift = jnp.zeros((TILES, 128), F32)
    for side in range(N_TP):
        terms = jnp.where(first_core == (side == 0), own_ref[...], other_ref[...])
        for c in range(N_CTX):
            at = slice(side * (D // N_TP) + c * FEAT, side * (D // N_TP) + (c + 1) * FEAT)
            grad[0:3, at] = terms[c, 0:3, :]
            grad[7:8, at] = terms[c, 3:4, :]
            grad[8:9, at] = terms[c, 3:4, :]
            gain = gain + terms[c, 8 : 8 + TILES, :]
            shift = shift + terms[c, 8 + TILES : 8 + 2 * TILES, :]
        for e in range(N_DP):
            row = slice(3 + side * units + e // (N_DP // units), 4 + side * units + e // (N_DP // units))
            for c in range(0, N_CTX, 2):
                lanes = (e % (N_DP // units)) * N_CTX * UNITS + c * UNITS
                pair = [
                    terms[c + k, 4 + e // 2 : 5 + e // 2, (e % 2) * UNITS : (e % 2 + 1) * UNITS]
                    for k in range(2)
                ]
                grad[row, lanes : lanes + 2 * UNITS] = jnp.concatenate(pair, axis=1)
    for tile in range(TILES):
        grad[9:10, tile * 128 : (tile + 1) * 128] = gain[tile : tile + 1, :]
        grad[10:11, tile * 128 : (tile + 1) * 128] = shift[tile : tile + 1, :]
    new = adam_update(vectors_ref[...], grad[0:11, :], first_ref[...], second_ref[...], 0.2)
    for ref, value in zip(outs, new):
        ref[...] = value


def adam_kernel(back_ref, *refs):
    ins, outs = refs[:6], refs[6:]

    def update(group, at, gradient, rate):
        new = adam_update(*[gradient if i == 1 else ins[group * 3 + i - (i > 1)][at] for i in range(4)], rate)
        for i in range(3):
            outs[group * 3 + i][at] = new[i]

    for c in range(N_CTX):
        for part in range(3):
            at = (part, slice(None), slice(c * FEAT, (c + 1) * FEAT))
            update(0, at, back_ref[c, part].astype(F32), 2.0 / math.sqrt(D))
    own_d = back_ref.shape[2]
    for e in range(N_DP):
        pair, side = divmod(e, 2)
        for c in range(0, N_CTX, 2):
            gradient = jnp.concatenate(
                [
                    back_ref[c + k, 3 + pair].astype(F32)[:, side * UNITS : (side + 1) * UNITS]
                    for k in range(2)
                ],
                axis=1,
            )
            to = e * N_CTX * UNITS + c * UNITS
            at = (slice(None), slice(to, to + 2 * UNITS))
            update(1, at, gradient, 2.0 / math.sqrt(D))


def swap(value):
    return lax.ppermute(value, "tp", [(0, 1), (1, 0)])


DP_Y, DP_A, DP_B = 4, 1, 3
CTX_Y, CTX_A, CTX_B = 1, 2, 6
BLOCKS = (0, 1, 2, 3, 6, 7, 4, 5)


def exchange(value, flip):
    return lax.ppermute(value, "dp", [(d, d ^ flip) for d in range(N_DP)])


def exchange_ctx(value, flip):
    return lax.ppermute(value, "ctx", [(c, c ^ flip) for c in range(N_CTX)])


def stage(*values):
    return lax.optimization_barrier(values)


def added(left, right):
    return (left.astype(F32) + right.astype(F32)).astype(BF)


def rows_to_team(value):
    pairs = [
        (d * N_CTX + c, c * N_CTX + d) for d in range(N_DP) for c in range(N_CTX)
    ]
    return lax.ppermute(value, ("dp", "ctx"), pairs)


def rows_to_owner(value):
    pairs = [
        (c * N_CTX + d, d * N_CTX + c) for d in range(N_DP) for c in range(N_CTX)
    ]
    return lax.ppermute(value, ("dp", "ctx"), pairs)


def shards(
    block_input,
    out_cotangent,
    token_order,
    seq_lengths,
    w_qkv,
    w_out,
    w_fc1,
    w_fc2,
    vectors,
    mom1_qkv,
    mom1_out,
    mom1_fc1,
    mom1_fc2,
    mom1_vec,
    mom2_qkv,
    mom2_out,
    mom2_fc1,
    mom2_fc2,
    mom2_vec,
):
    ctx_rank = lax.axis_index("ctx")
    tp_rank = lax.axis_index("tp")
    team_rank = tp_rank * N_CTX + ctx_rank
    own_d = D // (N_DP * N_CTX)
    half_rows = N_CTX * HALF_ROWS
    two = 2 * HALF_ROWS
    lanes = QKV + HIDDEN

    def half(value):
        return lax.dynamic_slice_in_dim(value, tp_rank * HALF_ROWS, HALF_ROWS, 0)

    tok_pair = jnp.concatenate([token_order // 32, token_order % 32], axis=0)
    columns, out, fc2 = pl.pallas_call(
        pack_kernel,
        out_shape=(
            jax.ShapeDtypeStruct((N_CTX, COLS + 1, own_d, 128), BF),
            jax.ShapeDtypeStruct((TILES, OUT_ROWS, 128), BF),
            jax.ShapeDtypeStruct((TILES, UNITS, 128), BF),
        ),
        in_specs=[WHOLE] * 5,
        out_specs=(WHOLE,) * 3,
        compiler_params=ROOM,
    )(
        w_qkv.transpose(1, 0, 2),
        w_fc1,
        jnp.pad(tok_pair.astype(F32), ((0, own_d - 2), (0, 0))),
        w_out[0],
        w_fc2[0],
    )
    x_own = half(block_input)
    dy_own = half(out_cotangent)
    x_other, dy_other, columns, out, fc2 = stage(
        exchange_ctx(x_own, CTX_Y), exchange_ctx(dy_own, CTX_Y), columns, out, fc2
    )

    columns = lax.all_to_all(columns, "ctx", 0, 0, tiled=True)
    columns, out, x_other, dy_other = stage(columns, rows_to_team(out), x_other, dy_other)
    piece = jnp.concatenate(
        [
            columns[:, :COLS].reshape(COL_ROWS, 128),
            out.reshape(TILES * OUT_ROWS, 128),
            fc2.reshape(TILES * UNITS, 128),
        ],
        axis=0,
    )
    x_two = jnp.concatenate([x_own, x_other], axis=0)
    dy_two = jnp.concatenate([dy_own, dy_other], axis=0)
    piece, x_two, dy_two, columns = stage(piece, x_two, dy_two, columns)

    by_y, by_a, by_b, x_a, dy_b = stage(
        exchange(piece, DP_Y),
        exchange(piece, DP_A),
        exchange(piece, DP_B),
        exchange_ctx(x_two, CTX_A),
        exchange_ctx(dy_two, CTX_B),
    )
    tok = columns[:, COLS, :2].astype(jnp.int32)
    tok = (tok[:, 0] * 32 + tok[:, 1]).reshape(N_CTX * N_TP, HALF_ROWS)
    blocks = jnp.bitwise_xor(ctx_rank, jnp.asarray(BLOCKS, jnp.int32)) * N_TP + tp_rank
    tok = tok[jnp.concatenate([blocks, jnp.bitwise_xor(blocks, 1)])].reshape(GROUP)
    first = jnp.zeros_like(tok)
    end = jnp.zeros((), jnp.int32)
    for i in range(seq_lengths.shape[1]):
        first = jnp.where(tok >= end, end, first)
        end = end + seq_lengths[0, i]
    position = (tok - first).astype(F32)
    lane = jnp.arange(FEAT) % HD
    inverse = ROPE_BASE ** (-(2.0 * (lane % (ROT // 2)).astype(F32)) / ROT)
    inverse = jnp.where(lane < ROT, inverse, 0.0)
    rotation = position[:, None] * inverse[None, :]
    cos_table = jnp.cos(rotation)
    sin_table = jnp.sin(rotation) * jnp.where(lane < ROT // 2, -1.0, 1.0)
    norm_gain = vectors[9]
    norm_shift = vectors[10]
    bias_qkv = lax.dynamic_slice(vectors, (0, team_rank * FEAT), (3, FEAT))
    bias_fc1 = vectors[3:7].reshape(N_TP, N_DP, N_CTX, UNITS)
    bias_fc1 = lax.dynamic_slice(bias_fc1, (tp_rank, 0, ctx_rank, 0), (1, N_DP, 1, UNITS))
    bias_fc1 = bias_fc1.reshape(HIDDEN)

    by_ya, by_yb, by_ab, x_b, dy_a, tok, first, cos_table, sin_table, bias_qkv, bias_fc1 = stage(
        exchange(by_y, DP_A),
        exchange(by_b, DP_Y),
        exchange(by_a, DP_B),
        exchange_ctx(x_two, CTX_B),
        exchange_ctx(dy_two, CTX_A),
        tok,
        first,
        cos_table,
        sin_table,
        bias_qkv,
        bias_fc1,
    )

    far1, far2, far3, x_ba, dy_ba = stage(
        exchange(by_ya[:THIRD], DP_B),
        exchange(by_yb[THIRD : 2 * THIRD], DP_A),
        exchange(by_ab[2 * THIRD :], DP_Y),
        exchange_ctx(x_a, CTX_B),
        exchange_ctx(dy_b, CTX_A),
    )

    def shaped(rows, columns, kind=BF):
        return jax.ShapeDtypeStruct((rows, columns), kind)

    dp_rank = lax.axis_index("dp").astype(jnp.int32).reshape(1)
    x_mine = [x_two, x_a, x_b, x_ba]
    normed_mine, dy_mine = loaded(
        norm_kernel,
        [shaped(half_rows, D)] * 2,
        [x_mine, [dy_two, dy_a, dy_b, dy_ba], norm_gain[None], norm_shift[None]],
        late=True,
    )
    normed_mine, dy_mine, far1, far2, far3 = stage(normed_mine, dy_mine, far1, far2, far3)
    half_shapes = [
        shaped(half_rows, HIDDEN),
        shaped(half_rows, HIDDEN),
        shaped(1, HIDDEN, F32),
        shaped(half_rows, QKV, F32),
        shaped(half_rows, FEAT),
    ]
    biases = [bias_fc1[None], bias_qkv.reshape(1, QKV)]
    mat_qkv, mat_fc1, mat_out, mat_fc2, active_mine, dhid_mine, sums_mine, pre_mine, dattn_mine = (
        loaded(
            place_kernel,
            [shaped(D, QKV), shaped(D, HIDDEN), shaped(FEAT, D), shaped(HIDDEN, D)] + half_shapes,
            [piece, by_y, by_a, by_b, by_ya, by_yb, by_ab, [far1, far2, far3], normed_mine, dy_mine]
            + biases,
            [dp_rank],
            flops=2 * half_rows * D * (2 * HIDDEN + QKV + FEAT),
            late=True,
        )
    )
    mats = [mat_qkv, mat_fc1, mat_out, mat_fc2]
    normed_theirs, dy_theirs, mats, active_mine, dhid_mine, pre_mine, dattn_mine = stage(
        swap(normed_mine), swap(dy_mine), mats, active_mine, dhid_mine, pre_mine, dattn_mine
    )
    active_theirs, dhid_theirs, sums_theirs, pre_theirs, dattn_theirs, *ff = loaded(
        feed_forward_kernel,
        half_shapes + [shaped(2 * D * HIDDEN // N_DP // 128, 128)] * N_DP,
        [normed_mine, dy_mine, active_mine, dhid_mine, normed_theirs, dy_theirs, *mats] + biases,
        [dp_rank],
        [pltpu.VMEM((D, HIDDEN), BF), pltpu.VMEM((HIDDEN, D), BF)],
        flops=12 * half_rows * D * HIDDEN,
        late=True,
    )
    ff = tuple(ff)

    def far_sent(pieces):
        cut = pieces[7].shape[0] // 3 // 16 * 16
        far = pieces[7]
        return (
            exchange(far[:cut], DP_B),
            exchange(far[cut : 2 * cut], DP_A),
            exchange(far[2 * cut :], DP_Y),
        )

    def far_added(pieces, others):
        cut = pieces[7].shape[0] // 3 // 16 * 16
        return pieces[:4] + tuple(patched(pieces[4:7], others, (0, cut, 2 * cut)))

    def middle_sent(pieces):
        return exchange(pieces[4], DP_A), exchange(pieces[5], DP_Y), exchange(pieces[6], DP_B)

    def middle_jobs(pieces, others):
        whole = [(0, pieces[0].shape[0])]
        return (
            ((pieces[1], others[0]), whole),
            ((pieces[2], others[2]), whole),
            ((pieces[3], others[1]), whole),
        )

    def near_sent(pieces):
        return exchange(pieces[1], DP_Y), exchange(pieces[2], DP_A), exchange(pieces[3], DP_B)

    ff, pre_theirs, dattn_theirs = stage(ff, pre_theirs, dattn_theirs)
    attended, dpre, dpre_sums = loaded(
        attention_kernel,
        [shaped(GROUP, FEAT), shaped(GROUP, QKV), shaped(1, QKV, F32)],
        [
            [pre_mine, pre_theirs],
            [dattn_mine, dattn_theirs],
            cos_table,
            sin_table,
            tok[:, None],
            first[:, None],
            tok[None, :],
        ],
        scratch=[
            pltpu.VMEM((GROUP, FEAT), BF),
            pltpu.VMEM((GROUP, FEAT), BF),
            pltpu.VMEM((GROUP, FEAT), BF),
            pltpu.VMEM((GROUP, FEAT), F32),
            pltpu.VMEM((GROUP, FEAT), F32),
        ],
        flops=28 * GROUP * GROUP * HD,
    )
    others, attended, dpre, dpre_sums = stage(far_sent(ff), attended, dpre, dpre_sums)
    ff = far_added(ff, others)
    ff, attended, dpre = stage(ff, attended, dpre)

    normed_out, branch_out, normed_part, branch_part, *heads = loaded(
        heads_kernel,
        [shaped(half_rows, D)] * 4 + [shaped(D * (QKV + FEAT) // N_DP // 128, 128)] * N_DP,
        [
            attended,
            dpre,
            [active_mine, active_theirs],
            [dhid_mine, dhid_theirs],
            *mats,
            [normed_mine, normed_theirs],
            [dy_mine, dy_theirs],
        ],
        [dp_rank],
        [pltpu.VMEM((D, QKV), BF), pltpu.VMEM((FEAT, D), BF)],
        flops=4 * GROUP * D * (QKV + FEAT + HIDDEN),
        late=True,
    )
    others, normed_out, branch_out, heads = stage(
        middle_sent(ff), normed_out, branch_out, tuple(heads)
    )
    ff = ff[:1] + tuple(combine(*middle_jobs(ff, others)))
    ff, normed_out, branch_out, heads = stage(ff, normed_out, branch_out, heads)
    dy_sum = sum(
        jnp.sum(lax.dynamic_slice_in_dim(value, team_rank * FEAT, FEAT, 1).astype(F32), axis=0)
        for value in (dy_mine, dy_theirs)
    )
    near_ff, normed_in, branch_in, dy_sum = stage(
        near_sent(ff), swap(normed_out), swap(branch_out), dy_sum
    )
    part_shape = jax.ShapeDtypeStruct((half_rows // 2, D), BF)
    term_shape = jax.ShapeDtypeStruct((1, D), F32)
    normed_keep, normed_send, branch_keep, branch_send, gain_term, shift_term = loaded(
        rows_kernel,
        [part_shape] * 4 + [term_shape] * 2,
        [normed_part, normed_in, branch_part, branch_in, x_mine],
        late=True,
    )
    terms = jnp.concatenate(
        [dpre_sums[0], dy_sum, (sums_mine + sums_theirs)[0], gain_term[0], shift_term[0]]
    ).reshape(1, 40, 128)
    others, normed_send, branch_send, terms = stage(
        far_sent(heads), normed_send, branch_send, terms
    )
    heads = far_added(heads, others)
    heads, normed_send, branch_send, terms = stage(heads, normed_send, branch_send, terms)

    quarter = half_rows // 4
    halves = [(0, quarter), (quarter, 2 * quarter)]
    terms = lax.all_to_all(
        jnp.broadcast_to(terms, (N_DP,) + terms.shape[1:]), "dp", 0, 0, tiled=True
    )
    others, normed_other, branch_other, terms = stage(
        middle_sent(heads),
        exchange_ctx(normed_send, CTX_B),
        exchange_ctx(branch_send, CTX_A),
        terms,
    )
    head_own = heads[0]
    normed_keep, normed_send, branch_keep, branch_send, *heads = combine(
        ((normed_keep, normed_other), halves),
        ((branch_keep, branch_other), halves),
        *middle_jobs(heads, others),
    )
    terms = jnp.sum(terms, axis=0, keepdims=True)
    heads, normed_keep, normed_send, branch_keep, branch_send, terms = stage(
        (head_own,) + tuple(heads), normed_keep, normed_send, branch_keep, branch_send, terms
    )
    terms = lax.all_to_all(
        jnp.broadcast_to(terms, (N_CTX,) + terms.shape[1:]), "ctx", 0, 0, tiled=True
    )
    ff_cut = N_CTX * 4 * own_d
    ff_columns, ff_rows = combine(
        ((ff[0],) + near_ff, [(0, ff_cut), (ff_cut, ff[0].shape[0])])
    )

    def rows_of(value):
        return value.reshape(TILES, -1, 128).transpose(1, 0, 2).reshape(1, -1, D).astype(F32)

    new_fc2 = adam_update(w_fc2, rows_of(ff_rows), mom1_fc2, mom2_fc2, 2.0 / math.sqrt(FF))
    others, normed_other, branch_other, terms, ff_columns, new_fc2 = stage(
        near_sent(heads),
        exchange_ctx(normed_send, CTX_A),
        exchange_ctx(branch_send, CTX_B),
        terms,
        ff_columns,
        new_fc2,
    )
    eighth = [(0, HALF_ROWS), (HALF_ROWS, 2 * HALF_ROWS)]
    cut = N_CTX * 3 * own_d
    normed_keep, normed_send, branch_keep, branch_send, head_columns, head_rows = combine(
        ((normed_keep, normed_other), eighth),
        ((branch_keep, branch_other), eighth),
        ((heads[0],) + others, [(0, cut), (cut, heads[0].shape[0])]),
    )
    back = jnp.concatenate(
        [
            head_columns.reshape(N_CTX, 3, own_d, 128),
            ff_columns.reshape(N_CTX, 4, own_d, 128),
        ],
        axis=1,
    )
    back, normed_keep, normed_send, branch_keep, branch_send, head_rows, terms = stage(
        back, normed_keep, normed_send, branch_keep, branch_send, head_rows, terms
    )
    back, head_rows, normed_other, branch_other = stage(
        lax.all_to_all(back, "ctx", 0, 0, tiled=True),
        rows_to_owner(head_rows),
        exchange_ctx(normed_send, CTX_Y),
        exchange_ctx(branch_send, CTX_Y),
    )
    normed_rows, branch_rows = combine(
        ((normed_keep, normed_other), [(0, HALF_ROWS)]),
        ((branch_keep, branch_other), [(0, HALF_ROWS)]),
    )
    terms_other = swap(terms)
    new_vec = pl.pallas_call(
        vector_kernel,
        out_shape=(jax.ShapeDtypeStruct(vectors.shape, F32),) * 3,
        in_specs=[SCALAR] + [WHOLE] * 5,
        out_specs=(WHOLE,) * 3,
        scratch_shapes=[pltpu.VMEM((16, D), F32)],
        compiler_params=ROOM,
    )(
        tp_rank.astype(jnp.int32).reshape(1),
        terms,
        terms_other,
        vectors,
        mom1_vec,
        mom2_vec,
    )
    new_out = adam_update(w_out, rows_of(head_rows), mom1_out, mom2_out, 16.0 / math.sqrt(D))
    block_output, input_grad = pl.pallas_call(
        finish_kernel,
        out_shape=(
            jax.ShapeDtypeStruct(block_input.shape, BF),
            jax.ShapeDtypeStruct(block_input.shape, F32),
        ),
        in_specs=[SCALAR] + [WHOLE] * 8,
        out_specs=(WHOLE,) * 2,
        compiler_params=ROOM,
    )(
        tp_rank.astype(jnp.int32).reshape(1),
        norm_gain[None],
        (vectors[7] + vectors[8])[None],
        block_input,
        out_cotangent,
        normed_rows,
        branch_rows,
        swap(normed_rows),
        swap(branch_rows),
    )
    columns_state = (
        w_qkv.transpose(1, 0, 2),
        mom1_qkv.transpose(1, 0, 2),
        mom2_qkv.transpose(1, 0, 2),
        w_fc1,
        mom1_fc1,
        mom2_fc1,
    )
    new_columns = pl.pallas_call(
        adam_kernel,
        out_shape=tuple(jax.ShapeDtypeStruct(v.shape, F32) for v in columns_state),
        in_specs=[WHOLE] * 7,
        out_specs=(WHOLE,) * 6,
        compiler_params=ROOM,
    )(back, *columns_state)
    new_qkv = [value.transpose(1, 0, 2) for value in new_columns[:3]]
    new_fc1 = new_columns[3:]
    return (
        block_output,
        input_grad,
        new_qkv[0],
        new_out[0],
        new_fc1[0],
        new_fc2[0],
        new_vec[0],
        new_qkv[1],
        new_out[1],
        new_fc1[1],
        new_fc2[1],
        new_vec[1],
        new_qkv[2],
        new_out[2],
        new_fc1[2],
        new_fc2[2],
        new_vec[2],
    )


def solution(mesh):
    in_specs = (
        P(("dp", "ctx"), None),
        P(("dp", "ctx"), None),
        P("dp", "ctx"),
        P("dp", None),
        P(("dp", "ctx"), None, "tp"),
        P("tp", ("dp", "ctx"), None),
        P(("dp", "ctx"), "tp"),
        P("tp", ("dp", "ctx"), None),
        P(),
        P(("dp", "ctx"), None, "tp"),
        P("tp", ("dp", "ctx"), None),
        P(("dp", "ctx"), "tp"),
        P("tp", ("dp", "ctx"), None),
        P(),
        P(("dp", "ctx"), None, "tp"),
        P("tp", ("dp", "ctx"), None),
        P(("dp", "ctx"), "tp"),
        P("tp", ("dp", "ctx"), None),
        P(),
    )
    out_specs = (
        P(("dp", "ctx"), None),
        P(("dp", "ctx"), None),
        P(("dp", "ctx"), None, "tp"),
        P("tp", ("dp", "ctx"), None),
        P(("dp", "ctx"), "tp"),
        P("tp", ("dp", "ctx"), None),
        P(),
        P(("dp", "ctx"), None, "tp"),
        P("tp", ("dp", "ctx"), None),
        P(("dp", "ctx"), "tp"),
        P("tp", ("dp", "ctx"), None),
        P(),
        P(("dp", "ctx"), None, "tp"),
        P("tp", ("dp", "ctx"), None),
        P(("dp", "ctx"), "tp"),
        P("tp", ("dp", "ctx"), None),
        P(),
    )
    return jax.shard_map(shards, mesh=mesh, in_specs=in_specs, out_specs=out_specs, check_vma=False)
```

```python
import math

import jax
import jax.numpy as jnp
from jax import lax
from jax.experimental import pallas as pl
from jax.experimental.pallas import tpu as pltpu
from jax.sharding import PartitionSpec as P

D = 2048
FF = 8192
HD = 64
ROT = 32
STEP = 10

NORM_EPS = 1e-05
SCORE_SCALE = 0.125
MASKED = -1e30
ROPE_BASE = 10000.0
BETA_ONE = 0.9
BETA_TWO = 0.95
ADAM_EPS = 1e-08
WEIGHT_DECAY = 0.1

N_DP = 8
N_CTX = 8
N_TP = 2
TEAM = N_CTX * N_TP
GROUP = 1024
HALF_ROWS = 64
FEAT = D // TEAM
HIDDEN = FF // TEAM
QKV = 3 * FEAT
Q_BLOCK = 256
UNITS = HIDDEN // N_DP

BF = jnp.bfloat16
F32 = jnp.float32


def adam_update(weight, gradient, moment_one, moment_two, step_rate):
    moment_one = BETA_ONE * moment_one + (1.0 - BETA_ONE) * gradient
    moment_two = BETA_TWO * moment_two + (1.0 - BETA_TWO) * gradient * gradient
    first_hat = moment_one / (1.0 - BETA_ONE**STEP)
    second_hat = moment_two / (1.0 - BETA_TWO**STEP)
    weight = weight - step_rate * (
        first_hat / (jnp.sqrt(second_hat) + ADAM_EPS) + WEIGHT_DECAY * weight
    )
    return (weight, moment_one, moment_two)


def gelu_and_slope(hidden):
    root = math.sqrt(2.0 / math.pi)
    square = hidden * hidden
    bent = jnp.tanh(root * (hidden + 0.044715 * hidden * square))
    value = 0.5 * hidden * (1.0 + bent)
    slope = 0.5 * (1.0 + bent) + 0.5 * hidden * (1.0 - bent * bent) * root * (
        1.0 + 3.0 * 0.044715 * square
    )
    return (value, slope)


def dot(left, right, dims):
    return lax.dot_general(left, right, (dims, ((), ())), preferred_element_type=F32)


WHOLE = pl.BlockSpec(memory_space=pltpu.VMEM)
SCALAR = pl.BlockSpec(memory_space=pltpu.SMEM)
ROOM = pltpu.CompilerParams(vmem_limit_bytes=24 * 2**20)


class Near:
    def __init__(self, value):
        self.value = value


def loaded(kernel, out_shape, operands, scalars=(), scratch=(), flops=0, late=False, limit=36):
    near_ins = [isinstance(v, Near) for v in operands]
    lists = [
        [v.value] if isinstance(v, Near) else v if isinstance(v, list) else [v] for v in operands
    ]
    parts_at = [[(v[1], v[2]) if isinstance(v, tuple) else (0, v.shape[0]) for v in vs] for vs in lists]
    lists = [[v[0] if isinstance(v, tuple) else v for v in vs] for vs in lists]
    near_outs = [isinstance(v, Near) for v in out_shape]
    shapes = [v.value if isinstance(v, Near) else v for v in out_shape]
    arrays = [v for values in lists for v in values]
    far_ins = [i for i, near in enumerate(near_ins) if not near]
    far_outs = [k for k, near in enumerate(near_outs) if not near]
    cuts = []
    for i in far_ins:
        at = 0
        for part, value in enumerate(lists[i]):
            (start, rows), pieces = parts_at[i][part], 1
            nbytes = value.nbytes // value.shape[0] * rows
            while nbytes // pieces > 2**19 and rows % (pieces * 32) == 0:
                pieces = pieces * 2
            size = rows // pieces
            cuts = cuts + [(i, part, start + k * size, at + k * size, size) for k in range(pieces)]
            at = at + rows
    first = [sum(len(v) for v in lists[:i]) for i in range(len(lists))]
    counts = (len(scalars), len(arrays), len(shapes), len(far_ins), len(far_outs))

    def body(*refs):
        parts, at = [], 0
        for count in counts:
            parts.append(refs[at : at + count])
            at = at + count
        given, ins, outs, held, written = parts
        rest, in_sems, out_sems = refs[at:-2], refs[-2], refs[-1]
        ins_at = [ins[first[i]] for i in range(len(lists))]
        for i, ref in zip(far_ins, held):
            ins_at[i] = ref
        outs_at = list(outs)
        for k, ref in zip(far_outs, written):
            outs_at[k] = ref
        copies, waited, sent = [], set(), {}
        for n, (i, part, source, to, size) in enumerate(cuts):
            copies.append(
                pltpu.make_async_copy(
                    ins[first[i] + part].at[pl.ds(source, size)],
                    ins_at[i].at[pl.ds(to, size)],
                    in_sems.at[n],
                )
            )
            copies[-1].start()

        def ready(operand, array=None):
            for n, (i, part, _, _, _) in enumerate(cuts):
                if i == operand and array in (None, part) and n not in waited:
                    copies[n].wait()
                    waited.add(n)

        def done(k):
            if not near_outs[k]:
                sent[k] = pltpu.make_async_copy(outs_at[k], outs[k], out_sems.at[k])
                sent[k].start()

        if late:
            kernel(ready, done, *given, *ins_at, *outs_at, *rest)
        else:
            for i in range(len(lists)):
                ready(i)
            kernel(*given, *ins_at, *outs_at, *rest)
        for i in range(len(lists)):
            ready(i)
        for k in range(len(shapes)):
            if k not in sent:
                done(k)
        for copy in sent.values():
            copy.wait()

    moved = sum(v.nbytes for v in arrays) + sum(
        math.prod(v.shape) * jnp.dtype(v.dtype).itemsize for v in shapes
    )
    anywhere = pl.BlockSpec(memory_space=pl.ANY)
    in_specs, placed = [SCALAR] * len(scalars), []
    for near, values in zip(near_ins, lists):
        in_specs = in_specs + [WHOLE if near else anywhere] * len(values)
        space = pltpu.VMEM if near else pltpu.HBM
        placed = placed + [pltpu.with_memory_space_constraint(v, space) for v in values]
    return pl.pallas_call(
        body,
        out_shape=tuple(
            (pltpu.VMEM if near else pltpu.HBM)(v.shape, v.dtype)
            for near, v in zip(near_outs, shapes)
        ),
        in_specs=in_specs,
        out_specs=tuple(WHOLE if near else anywhere for near in near_outs),
        scratch_shapes=[
            pltpu.VMEM((sum(n for _, n in parts_at[i]),) + lists[i][0].shape[1:], lists[i][0].dtype)
            for i in far_ins
        ]
        + [pltpu.VMEM(shapes[k].shape, shapes[k].dtype) for k in far_outs]
        + list(scratch)
        + [
            pltpu.SemaphoreType.DMA((max(1, len(cuts)),)),
            pltpu.SemaphoreType.DMA((len(shapes),)),
        ],
        compiler_params=pltpu.CompilerParams(vmem_limit_bytes=limit * 2**20),
        cost_estimate=pl.CostEstimate(flops=flops, bytes_accessed=moved, transcendentals=0),
    )(*scalars, *placed)


TILES = D // 128
COLS = (QKV + HIDDEN) // 128
OUT_ROWS = FEAT // N_DP
COL_ROWS = N_CTX * COLS * (D // N_DP // N_CTX)
PIECE = COL_ROWS + TILES * (OUT_ROWS + UNITS)
THIRD = PIECE // 3


def pack_kernel(qkv_ref, fc1_ref, tok_ref, fc2_ref, columns_ref, fc2s_ref):
    for c in range(N_CTX):
        for part in range(3):
            columns_ref[c, part] = qkv_ref[part, :, c * FEAT : (c + 1) * FEAT].astype(BF)
        for pair in range(HIDDEN // 128):
            at = [(2 * pair + e) * N_CTX * UNITS + c * UNITS for e in range(2)]
            columns_ref[c, 3 + pair] = jnp.concatenate(
                [fc1_ref[:, i : i + UNITS] for i in at], axis=1
            ).astype(BF)
        columns_ref[c, COLS] = tok_ref[...].astype(BF)
    for tile in range(TILES):
        fc2s_ref[tile] = fc2_ref[:, tile * 128 : (tile + 1) * 128].astype(BF)


MASKS = (0, 4, 1, 3, 4 ^ 1, 4 ^ 3, 1 ^ 3, 4 ^ 1 ^ 3)


NT = ((1,), (1,))
NN = ((1,), (0,))
TN = ((0,), (0,))


def place(block, piece, qkv, fc1, out, fc2):
    own_d = D // N_DP // N_CTX
    for src in range(N_CTX):
        at = pl.ds(pl.multiple_of(block * (D // N_DP) + src * own_d, own_d), own_d)
        for j in range(COLS):
            start = (src * COLS + j) * own_d
            rows = piece[start : start + own_d, :]
            if j < 3:
                qkv[at, j * 128 : (j + 1) * 128] = rows
            else:
                fc1[at, (j - 3) * 128 : (j - 2) * 128] = rows
    for to, start, count in (
        (out, COL_ROWS, OUT_ROWS),
        (fc2, COL_ROWS + TILES * OUT_ROWS, UNITS),
    ):
        at = pl.ds(pl.multiple_of(block * count, count), count)
        for tile in range(TILES):
            to[at, tile * 128 : (tile + 1) * 128] = piece[
                start + tile * count : start + (tile + 1) * count, :
            ]


def fold(block, cols_ref, rows_ref, piece):
    own_d = D // N_DP // N_CTX
    n_cols = cols_ref.shape[1] // 128
    n_rows = rows_ref.shape[0] // N_DP
    for src in range(N_CTX):
        at = pl.ds(pl.multiple_of(block * (D // N_DP) + src * own_d, own_d), own_d)
        for j in range(n_cols):
            to = (src * n_cols + j) * own_d
            piece[to : to + own_d, :] = cols_ref[at, j * 128 : (j + 1) * 128]
    at = pl.ds(pl.multiple_of(block * n_rows, n_rows), n_rows)
    for tile in range(TILES):
        to = N_CTX * n_cols * own_d + tile * n_rows
        piece[to : to + n_rows, :] = rows_ref[at, tile * 128 : (tile + 1) * 128]


def normal(value):
    value = value.astype(F32)
    centered = value - jnp.mean(value, axis=-1, keepdims=True)
    inv_std = lax.rsqrt(jnp.mean(centered * centered, axis=-1, keepdims=True) + NORM_EPS)
    return (centered * inv_std, inv_std)


def norm_kernel(ready, done, x, dy, gain, shift, normed, dy_out):
    ready(2)
    ready(3)
    for part in range(4):
        at = slice(part * 2 * HALF_ROWS, (part + 1) * 2 * HALF_ROWS)
        ready(0, part)
        normed[at, :] = (normal(x[at, :])[0] * gain[...] + shift[...]).astype(BF)
    done(0)
    ready(1)
    dy_out[...] = dy[...]


def half_branch(normed, dy, mats, biases, outs):
    qkv, fc1, out, fc2 = mats
    bias_fc1, bias_qkv = biases
    active, dhid, sums, pre, dattn = outs
    value, slope = gelu_and_slope(dot(normed[...], fc1[...], NN) + bias_fc1[...])
    active[...] = value.astype(BF)
    grad = (dot(dy[...], fc2[...], NT) * slope).astype(BF)
    dhid[...] = grad
    sums[...] = jnp.sum(grad.astype(F32), axis=0, keepdims=True)
    pre[...] = dot(normed[...], qkv[...], NN) + bias_qkv[...]
    dattn[...] = dot(dy[...], out[...], NT).astype(BF)


def place_kernel(ready, done, rank_ref, *refs):
    pieces, (normed, dy, *biases), outs = refs[:N_DP], refs[N_DP : N_DP + 4], refs[N_DP + 4 :]
    mats = outs[:4]
    for k, flip in enumerate(MASKS):
        ready(k)
        place(rank_ref[0] ^ flip, pieces[k], *mats)
    for k in range(4):
        done(k)
        ready(N_DP + k)
    half_branch(normed, dy, mats, biases, outs[4:])


def feed_forward_kernel(ready, done, rank_ref, *refs):
    normed_mine, dy_mine, active_mine, dhid_mine, normed, dy, *mats = refs[:10]
    biases, outs, grads = refs[10:12], refs[12:17], refs[17 : 17 + N_DP]
    grad_fc1, grad_fc2 = refs[17 + N_DP :]
    for i in range(4, 12):
        ready(i)
    half_branch(normed, dy, mats, biases, outs)
    active, dhid = outs[:2]
    for k in range(5):
        done(k)
    for i in range(4):
        ready(i)
    for k in range(D // HIDDEN):
        at = slice(k * HIDDEN, (k + 1) * HIDDEN)
        grad_fc2[:, at] = (
            dot(active_mine[...], dy_mine[:, at], TN) + dot(active[...], dy[:, at], TN)
        ).astype(BF)
        grad_fc1[at, :] = (
            dot(normed_mine[:, at], dhid_mine[...], TN) + dot(normed[:, at], dhid[...], TN)
        ).astype(BF)
    for k in reversed(range(N_DP)):
        fold(rank_ref[0] ^ MASKS[k], grad_fc1, grad_fc2, grads[k])
        done(5 + k)


def attention_kernel(
    pre_mine,
    pre_theirs,
    dattn_mine,
    dattn_theirs,
    cos,
    sin,
    marks,
    key_tok,
    attended,
    dpre,
    sums,
    query_scr,
    key_scr,
    value_scr,
    dkey_scr,
    dvalue_scr,
    dattn_all,
):
    lane = lax.broadcasted_iota(jnp.int32, (1, FEAT), 1)
    early = (lane % HD) < (ROT // 2)
    first_head = lane < HD

    def partner(value):
        return jnp.where(
            early,
            pltpu.roll(value, FEAT - ROT // 2, axis=1),
            pltpu.roll(value, ROT // 2, axis=1),
        )

    half = GROUP // 2
    for i, (pre, dattn) in enumerate(((pre_mine, dattn_mine), (pre_theirs, dattn_theirs))):
        at = slice(i * half, (i + 1) * half)
        query = pre[:, :FEAT]
        query = (query * cos[at, :] + partner(query) * sin[at, :]).astype(BF)
        query_scr[at, :] = query * jnp.asarray(SCORE_SCALE, BF)
        key = pre[:, FEAT : 2 * FEAT]
        key_scr[at, :] = (key * cos[at, :] + partner(key) * sin[at, :]).astype(BF)
        value_scr[at, :] = pre[:, 2 * FEAT :].astype(BF)
        dattn_all[at, :] = dattn[...]
    dkey_scr[...] = jnp.zeros_like(dkey_scr)
    dvalue_scr[...] = jnp.zeros_like(dvalue_scr)

    @pl.loop(0, GROUP // Q_BLOCK)
    def _(step):
        rows = pl.ds(pl.multiple_of(step * Q_BLOCK, Q_BLOCK), Q_BLOCK)
        query = query_scr[rows, :]
        dattn = dattn_all[rows, :]
        key = key_scr[...]
        value = value_scr[...]
        token = key_tok[...]
        mask = (token <= marks[rows, 0:1]) & (token >= marks[rows, 1:2])
        zero = jnp.zeros((), BF)
        out_parts = []
        dquery_parts = []
        for head in range(2):
            inside = first_head if head == 0 else jnp.logical_not(first_head)
            query_h = jnp.where(inside, query, zero)
            dattn_h = jnp.where(inside, dattn, zero)
            scores = dot(query_h, key, NT)
            scores = jnp.where(mask, scores, MASKED)
            top = jnp.max(scores, axis=1, keepdims=True)
            probs = jnp.exp(scores - top)
            probs = probs * (1.0 / jnp.sum(probs, axis=1, keepdims=True))
            probs_b = probs.astype(BF)
            mixed = dot(probs_b, value, NN)
            delta = jnp.sum(
                jnp.where(inside, mixed, 0.0) * dattn_h.astype(F32), axis=1, keepdims=True
            )
            dprobs = dot(dattn_h, value, NT)
            dscore = (probs * (dprobs - delta)).astype(BF)
            dquery_parts.append(dot(dscore, key, NN))
            dkey_scr[...] += dot(dscore, query_h, TN)
            dvalue_scr[...] += dot(probs_b, dattn_h, TN)
            out_parts.append(mixed)
        attended[rows, :] = jnp.where(first_head, out_parts[0], out_parts[1]).astype(BF)
        dquery = jnp.where(first_head, dquery_parts[0], dquery_parts[1]) * SCORE_SCALE
        dpre[rows, :FEAT] = (dquery * cos[rows, :] - partner(dquery) * sin[rows, :]).astype(BF)

    dkey = dkey_scr[...]
    dpre[:, FEAT : 2 * FEAT] = (dkey * cos[...] - partner(dkey) * sin[...]).astype(BF)
    dpre[:, 2 * FEAT :] = dvalue_scr[...].astype(BF)
    sums[...] = jnp.sum(dpre[...].astype(F32), axis=0, keepdims=True)


def heads_kernel(ready, done, rank_ref, *refs):
    attended, dpre, qkv, fc1, out, fc2 = refs[:6]
    active, dhid, normed, dy = refs[6:8], refs[8:10], refs[10:12], refs[12:14]
    sums = refs[14:18]
    grads, (grad_qkv, grad_out) = refs[18 : 18 + N_DP], refs[18 + N_DP :]
    halves = [slice(i * GROUP // 2, (i + 1) * GROUP // 2) for i in range(2)]
    for i in (1, 0):
        rows = halves[i]
        for k in range(D // HIDDEN):
            at = slice(k * HIDDEN, (k + 1) * HIDDEN)
            sums[2 * i][:, at] = (
                dot(dpre[rows, :], qkv[at, :], NT) + dot(dhid[i][...], fc1[at, :], NT)
            ).astype(BF)
            sums[2 * i + 1][:, at] = (
                dot(attended[rows, :], out[:, at], NN) + dot(active[i][...], fc2[:, at], NN)
            ).astype(BF)
        done(2 * i)
        done(2 * i + 1)
    for i in range(10, 14):
        ready(i)
    for k in range(D // HIDDEN):
        at = slice(k * HIDDEN, (k + 1) * HIDDEN)
        grad_qkv[at, :] = sum(
            dot(normed[i][:, at], dpre[halves[i], :], TN) for i in range(2)
        ).astype(BF)
        grad_out[:, at] = sum(
            dot(attended[halves[i], :], dy[i][:, at], TN) for i in range(2)
        ).astype(BF)
    for k in reversed(range(N_DP)):
        fold(rank_ref[0] ^ MASKS[k], grad_qkv, grad_out, grads[k])
        done(4 + k)


def rows_kernel(ready, done, normed_ref, normed_in, branch_ref, branch_in, x, *outs):
    normed_keep, normed_send, branch_keep, branch_send, gain_ref, shift_ref = outs
    block = 2 * HALF_ROWS
    ready(2)
    ready(3)
    for i in range(4):
        rows, to = slice(i * block, (i + 1) * block), branch_keep if i % 2 == 0 else branch_send
        total = branch_ref[rows, :].astype(F32) + branch_in[rows, :].astype(F32)
        to[(i // 2) * block : (i // 2 + 1) * block, :] = total.astype(BF)
    done(2)
    done(3)
    ready(0)
    ready(1)
    ready(4)
    gain = jnp.zeros((1, D), F32)
    shift = jnp.zeros((1, D), F32)
    for i in range(4):
        rows, to = slice(i * block, (i + 1) * block), normed_keep if i < 2 else normed_send
        total = normed_ref[rows, :].astype(F32) + normed_in[rows, :].astype(F32)
        gain = gain + jnp.sum(total * normal(x[rows, :])[0], axis=0, keepdims=True)
        shift = shift + jnp.sum(total, axis=0, keepdims=True)
        to[(i % 2) * block : (i % 2 + 1) * block, :] = total.astype(BF)
    gain_ref[...] = gain
    shift_ref[...] = shift


def combine(*jobs):
    operands = [value for values, _ in jobs for value in values]
    outs = [
        jax.ShapeDtypeStruct((stop - start, values[0].shape[1]), BF)
        for values, ranges in jobs
        for start, stop in ranges
    ]

    def kernel(*refs):
        ins, to = list(refs[: len(operands)]), list(refs[len(operands) :])
        for values, ranges in jobs:
            mine, ins = ins[: len(values)], ins[len(values) :]
            for start, stop in ranges:
                total = mine[0][start:stop, :].astype(F32)
                for ref in mine[1:]:
                    total = total + ref[start:stop, :].astype(F32)
                to.pop(0)[...] = total.astype(BF)

    return loaded(kernel, outs, operands)


def patched(pieces, others, starts):
    count = len(pieces)

    def kernel(*refs):
        for i in range(count):
            piece, other, to = refs[i], refs[count + i], refs[2 * count + i]
            start, stop = starts[i], starts[i] + other.shape[0]
            if start > 0:
                to[:start, :] = piece[:start, :]
            to[start:stop, :] = (piece[start:stop, :].astype(F32) + other[...].astype(F32)).astype(BF)
            if stop < piece.shape[0]:
                to[stop:, :] = piece[stop:, :]

    outs = [jax.ShapeDtypeStruct(v.shape, BF) for v in pieces]
    return loaded(kernel, outs, list(pieces) + list(others))


def finish_kernel(core_ref, gain_ref, bias_ref, x_ref, dy_ref, *refs):
    (normed_own, branch_own, normed_other, branch_other), (output_ref, grad_ref) = refs[:4], refs[4:]
    core = core_ref[0]
    for side, normed_in, branch_in in (
        (core, normed_own, branch_own),
        (1 - core, normed_other, branch_other),
    ):
        rows = pl.ds(pl.multiple_of(side * HALF_ROWS, HALF_ROWS), HALF_ROWS)
        value = x_ref[rows, :]
        normal_x, inv_std = normal(value)
        value = value.astype(F32)
        output_ref[rows, :] = (value + branch_in[...].astype(F32) + bias_ref[...]).astype(BF)
        scaled = normed_in[...].astype(F32) * gain_ref[...]
        grad_ref[rows, :] = dy_ref[rows, :].astype(F32) + inv_std * (
            scaled
            - jnp.mean(scaled, axis=-1, keepdims=True)
            - normal_x * jnp.mean(scaled * normal_x, axis=-1, keepdims=True)
        )


def vector_kernel(core_ref, own_ref, other_ref, *refs):
    (vectors_ref, first_ref, second_ref), outs, grad = refs[:3], refs[3:6], refs[6]
    first_core = core_ref[0] == 0
    units = FF // N_TP // D
    gain = jnp.zeros((TILES, 128), F32)
    shift = jnp.zeros((TILES, 128), F32)
    for side in range(N_TP):
        terms = jnp.where(first_core == (side == 0), own_ref[...], other_ref[...])
        for c in range(N_CTX):
            at = slice(side * (D // N_TP) + c * FEAT, side * (D // N_TP) + (c + 1) * FEAT)
            grad[0:3, at] = terms[c, 0:3, :]
            grad[7:8, at] = terms[c, 3:4, :]
            grad[8:9, at] = terms[c, 3:4, :]
            gain = gain + terms[c, 8 : 8 + TILES, :]
            shift = shift + terms[c, 8 + TILES : 8 + 2 * TILES, :]
        for e in range(N_DP):
            row = slice(3 + side * units + e // (N_DP // units), 4 + side * units + e // (N_DP // units))
            for c in range(0, N_CTX, 2):
                lanes = (e % (N_DP // units)) * N_CTX * UNITS + c * UNITS
                pair = [
                    terms[c + k, 4 + e // 2 : 5 + e // 2, (e % 2) * UNITS : (e % 2 + 1) * UNITS]
                    for k in range(2)
                ]
                grad[row, lanes : lanes + 2 * UNITS] = jnp.concatenate(pair, axis=1)
    for tile in range(TILES):
        grad[9:10, tile * 128 : (tile + 1) * 128] = gain[tile : tile + 1, :]
        grad[10:11, tile * 128 : (tile + 1) * 128] = shift[tile : tile + 1, :]
    new = adam_update(vectors_ref[...], grad[0:11, :], first_ref[...], second_ref[...], 0.2)
    for ref, value in zip(outs, new):
        ref[...] = value


def adam_kernel(back_ref, *refs):
    ins, outs = refs[:6], refs[6:]

    def update(group, at, gradient, rate):
        new = adam_update(*[gradient if i == 1 else ins[group * 3 + i - (i > 1)][at] for i in range(4)], rate)
        for i in range(3):
            outs[group * 3 + i][at] = new[i]

    for c in range(N_CTX):
        for part in range(3):
            at = (part, slice(None), slice(c * FEAT, (c + 1) * FEAT))
            update(0, at, back_ref[c, part].astype(F32), 2.0 / math.sqrt(D))
    own_d = back_ref.shape[2]
    for e in range(N_DP):
        pair, side = divmod(e, 2)
        for c in range(0, N_CTX, 2):
            gradient = jnp.concatenate(
                [
                    back_ref[c + k, 3 + pair].astype(F32)[:, side * UNITS : (side + 1) * UNITS]
                    for k in range(2)
                ],
                axis=1,
            )
            to = e * N_CTX * UNITS + c * UNITS
            at = (slice(None), slice(to, to + 2 * UNITS))
            update(1, at, gradient, 2.0 / math.sqrt(D))


def swap(value):
    return lax.ppermute(value, "tp", [(0, 1), (1, 0)])


DP_Y, DP_A, DP_B = 4, 1, 3
CTX_Y, CTX_A, CTX_B = 1, 2, 6
BLOCKS = (0, 1, 2, 3, 6, 7, 4, 5)


def exchange(value, flip):
    return lax.ppermute(value, "dp", [(d, d ^ flip) for d in range(N_DP)])


def exchange_ctx(value, flip):
    return lax.ppermute(value, "ctx", [(c, c ^ flip) for c in range(N_CTX)])


def stage(*values):
    return lax.optimization_barrier(values)


def added(left, right):
    return (left.astype(F32) + right.astype(F32)).astype(BF)


def rows_to_team(value):
    pairs = [
        (d * N_CTX + c, c * N_CTX + d) for d in range(N_DP) for c in range(N_CTX)
    ]
    return lax.ppermute(value, ("dp", "ctx"), pairs)


def rows_to_owner(value):
    pairs = [
        (c * N_CTX + d, d * N_CTX + c) for d in range(N_DP) for c in range(N_CTX)
    ]
    return lax.ppermute(value, ("dp", "ctx"), pairs)


def shards(
    block_input,
    out_cotangent,
    token_order,
    seq_lengths,
    w_qkv,
    w_out,
    w_fc1,
    w_fc2,
    vectors,
    mom1_qkv,
    mom1_out,
    mom1_fc1,
    mom1_fc2,
    mom1_vec,
    mom2_qkv,
    mom2_out,
    mom2_fc1,
    mom2_fc2,
    mom2_vec,
):
    ctx_rank = lax.axis_index("ctx")
    tp_rank = lax.axis_index("tp")
    team_rank = tp_rank * N_CTX + ctx_rank
    own_d = D // (N_DP * N_CTX)
    half_rows = N_CTX * HALF_ROWS
    two = 2 * HALF_ROWS
    lanes = QKV + HIDDEN

    def half(value):
        return lax.dynamic_slice_in_dim(value, tp_rank * HALF_ROWS, HALF_ROWS, 0)

    tok_pair = jnp.concatenate([token_order // 32, token_order % 32], axis=0)
    columns, fc2 = pl.pallas_call(
        pack_kernel,
        out_shape=(
            jax.ShapeDtypeStruct((N_CTX, COLS + 1, own_d, 128), BF),
            jax.ShapeDtypeStruct((TILES, UNITS, 128), BF),
        ),
        in_specs=[WHOLE] * 4,
        out_specs=(WHOLE,) * 2,
        compiler_params=ROOM,
    )(
        w_qkv.transpose(1, 0, 2),
        w_fc1,
        jnp.pad(tok_pair.astype(F32), ((0, own_d - 2), (0, 0))),
        w_fc2[0],
    )
    x_own = half(block_input)
    dy_own = half(out_cotangent)
    out = w_out[0].astype(BF).reshape(OUT_ROWS, TILES, 128).transpose(1, 0, 2)
    x_other, dy_other, out, columns, fc2 = stage(
        exchange_ctx(x_own, CTX_Y), exchange_ctx(dy_own, CTX_Y), rows_to_team(out), columns, fc2
    )

    columns = lax.all_to_all(columns, "ctx", 0, 0, tiled=True)
    columns, out, x_other, dy_other = stage(columns, out, x_other, dy_other)
    piece = jnp.concatenate(
        [
            columns[:, :COLS].reshape(COL_ROWS, 128),
            out.reshape(TILES * OUT_ROWS, 128),
            fc2.reshape(TILES * UNITS, 128),
        ],
        axis=0,
    )
    x_two = jnp.concatenate([x_own, x_other], axis=0)
    dy_two = jnp.concatenate([dy_own, dy_other], axis=0)
    piece, x_two, dy_two, columns = stage(piece, x_two, dy_two, columns)

    by_y, by_a, by_b, x_a, dy_b = stage(
        exchange(piece, DP_Y),
        exchange(piece, DP_A),
        exchange(piece, DP_B),
        exchange_ctx(x_two, CTX_A),
        exchange_ctx(dy_two, CTX_B),
    )
    tok = columns[:, COLS, :2].astype(jnp.int32)
    tok = (tok[:, 0] * 32 + tok[:, 1]).reshape(N_CTX * N_TP, HALF_ROWS)
    blocks = jnp.bitwise_xor(ctx_rank, jnp.asarray(BLOCKS, jnp.int32)) * N_TP + tp_rank
    tok = tok[jnp.concatenate([blocks, jnp.bitwise_xor(blocks, 1)])].reshape(GROUP)
    first = jnp.zeros_like(tok)
    end = jnp.zeros((), jnp.int32)
    for i in range(seq_lengths.shape[1]):
        first = jnp.where(tok >= end, end, first)
        end = end + seq_lengths[0, i]
    position = (tok - first).astype(F32)
    lane = jnp.arange(FEAT) % HD
    inverse = ROPE_BASE ** (-(2.0 * (lane % (ROT // 2)).astype(F32)) / ROT)
    inverse = jnp.where(lane < ROT, inverse, 0.0)
    rotation = position[:, None] * inverse[None, :]
    cos_table = jnp.cos(rotation)
    sin_table = jnp.sin(rotation) * jnp.where(lane < ROT // 2, -1.0, 1.0)
    tok = tok.astype(F32)
    first = first.astype(F32)
    marks = jnp.where(jnp.arange(FEAT)[None, :] == 0, tok[:, None], first[:, None])
    norm_gain = vectors[9]
    norm_shift = vectors[10]
    bias_qkv = lax.dynamic_slice(vectors, (0, team_rank * FEAT), (3, FEAT))
    bias_fc1 = vectors[3:7].reshape(N_TP, N_DP, N_CTX, UNITS)
    bias_fc1 = lax.dynamic_slice(bias_fc1, (tp_rank, 0, ctx_rank, 0), (1, N_DP, 1, UNITS))
    bias_fc1 = bias_fc1.reshape(HIDDEN)

    x_four = jnp.concatenate([x_two, x_a], axis=0)
    dy_four = jnp.concatenate([dy_two, dy_b], axis=0)
    by_ya, by_yb, by_ab, x_b, dy_a, tok, marks, cos_table, sin_table, bias_qkv, bias_fc1 = stage(
        exchange(by_y, DP_A),
        exchange(by_b, DP_Y),
        exchange(by_a, DP_B),
        exchange_ctx(x_four, CTX_B),
        exchange_ctx(dy_four, CTX_A),
        tok,
        marks,
        cos_table,
        sin_table,
        bias_qkv,
        bias_fc1,
    )
    x_mine = [x_two, x_a, (x_b, 0, two), (x_b, two, two)]
    dy_parts = [dy_two, (dy_a, 0, two), dy_b, (dy_a, two, two)]

    def shaped(rows, columns, kind=BF):
        return jax.ShapeDtypeStruct((rows, columns), kind)

    dp_rank = lax.axis_index("dp").astype(jnp.int32).reshape(1)
    normed_mine, dy_mine = loaded(
        norm_kernel,
        [Near(shaped(half_rows, D))] * 2,
        [x_mine, dy_parts, norm_gain[None], norm_shift[None]],
        late=True,
    )
    normed_mine, dy_mine, far1, far2, far3 = stage(
        normed_mine,
        dy_mine,
        exchange(by_ya[:THIRD], DP_B),
        exchange(by_yb[THIRD : 2 * THIRD], DP_A),
        exchange(by_ab[2 * THIRD :], DP_Y),
    )
    half_shapes = [
        Near(shaped(half_rows, HIDDEN)),
        Near(shaped(half_rows, HIDDEN)),
        shaped(1, HIDDEN, F32),
        Near(shaped(half_rows, QKV, F32)),
        Near(shaped(half_rows, FEAT)),
    ]
    biases = [bias_fc1[None], bias_qkv.reshape(1, QKV)]
    mat_qkv, mat_fc1, mat_out, mat_fc2, active_mine, dhid_mine, sums_mine, pre_mine, dattn_mine = (
        loaded(
            place_kernel,
            [
                Near(shaped(D, QKV)),
                Near(shaped(D, HIDDEN)),
                Near(shaped(FEAT, D)),
                Near(shaped(HIDDEN, D)),
            ]
            + half_shapes,
            [piece, by_y, by_a, by_b, by_ya, by_yb, by_ab, [far1, far2, far3]]
            + [Near(normed_mine), Near(dy_mine)]
            + biases,
            [dp_rank],
            flops=2 * half_rows * D * (2 * HIDDEN + QKV + FEAT),
            late=True,
        )
    )
    mats = [mat_qkv, mat_fc1, mat_out, mat_fc2]
    normed_theirs, dy_theirs, mats, active_mine, dhid_mine, pre_mine, dattn_mine = stage(
        swap(normed_mine), swap(dy_mine), mats, active_mine, dhid_mine, pre_mine, dattn_mine
    )
    active_theirs, dhid_theirs, sums_theirs, pre_theirs, dattn_theirs, *ff = loaded(
        feed_forward_kernel,
        half_shapes + [shaped(2 * D * HIDDEN // N_DP // 128, 128)] * N_DP,
        [Near(v) for v in (normed_mine, dy_mine, active_mine, dhid_mine)]
        + [normed_theirs, dy_theirs]
        + [Near(v) for v in mats]
        + biases,
        [dp_rank],
        [pltpu.VMEM((D, HIDDEN), BF), pltpu.VMEM((HIDDEN, D), BF)],
        flops=12 * half_rows * D * HIDDEN,
        late=True,
    )
    ff = tuple(ff)

    def far_sent(pieces):
        cut = pieces[7].shape[0] // 3 // 16 * 16
        far = pieces[7]
        return (
            exchange(far[:cut], DP_B),
            exchange(far[cut : 2 * cut], DP_A),
            exchange(far[2 * cut :], DP_Y),
        )

    def far_added(pieces, others):
        cut = pieces[7].shape[0] // 3 // 16 * 16
        return pieces[:4] + tuple(patched(pieces[4:7], others, (0, cut, 2 * cut)))

    def middle_sent(pieces):
        return exchange(pieces[4], DP_A), exchange(pieces[5], DP_Y), exchange(pieces[6], DP_B)

    def middle_jobs(pieces, others):
        whole = [(0, pieces[0].shape[0])]
        return (
            ((pieces[1], others[0]), whole),
            ((pieces[2], others[2]), whole),
            ((pieces[3], others[1]), whole),
        )

    def near_sent(pieces):
        return exchange(pieces[1], DP_Y), exchange(pieces[2], DP_A), exchange(pieces[3], DP_B)

    ff, pre_theirs, dattn_theirs = stage(ff, pre_theirs, dattn_theirs)
    attended, dpre, dpre_sums = loaded(
        attention_kernel,
        [Near(shaped(GROUP, FEAT)), Near(shaped(GROUP, QKV)), shaped(1, QKV, F32)],
        [
            Near(pre_mine),
            Near(pre_theirs),
            Near(dattn_mine),
            Near(dattn_theirs),
            cos_table,
            sin_table,
            marks,
            tok[None, :],
        ],
        scratch=[
            pltpu.VMEM((GROUP, FEAT), BF),
            pltpu.VMEM((GROUP, FEAT), BF),
            pltpu.VMEM((GROUP, FEAT), BF),
            pltpu.VMEM((GROUP, FEAT), F32),
            pltpu.VMEM((GROUP, FEAT), F32),
            pltpu.VMEM((GROUP, FEAT), BF),
        ],
        flops=28 * GROUP * GROUP * HD,
        limit=26,
    )
    others, attended, dpre, dpre_sums = stage(far_sent(ff), attended, dpre, dpre_sums)
    ff = far_added(ff, others)
    ff, attended, dpre = stage(ff, attended, dpre)

    normed_part, branch_part, normed_out, branch_out, *heads = loaded(
        heads_kernel,
        [shaped(half_rows, D)] * 4
        + [shaped(D * (QKV + FEAT) // N_DP // 128, 128)] * N_DP,
        [Near(attended), Near(dpre)]
        + [Near(v) for v in mats]
        + [Near(v) for v in (active_mine, active_theirs, dhid_mine, dhid_theirs)]
        + [Near(normed_mine), normed_theirs, Near(dy_mine), dy_theirs],
        [dp_rank],
        [pltpu.VMEM((D, QKV), BF), pltpu.VMEM((FEAT, D), BF)],
        flops=4 * GROUP * D * (QKV + FEAT + HIDDEN),
        late=True,
    )
    others, normed_out, branch_out, heads = stage(
        middle_sent(ff), normed_out, branch_out, tuple(heads)
    )
    dy_sum = sum(
        jnp.sum(lax.dynamic_slice_in_dim(value, team_rank * FEAT, FEAT, 1).astype(F32), axis=0)
        for value in (dy_mine, dy_theirs)
    )
    ff = ff[:1] + tuple(combine(*middle_jobs(ff, others)))
    others, normed_in, branch_in, dy_sum, ff = stage(
        far_sent(heads), swap(normed_out), swap(branch_out), dy_sum, ff
    )
    heads = far_added(heads, others)
    heads, normed_in, branch_in = stage(heads, normed_in, branch_in)
    near_ff = near_sent(ff)
    part_shape = jax.ShapeDtypeStruct((half_rows // 2, D), BF)
    term_shape = jax.ShapeDtypeStruct((1, D), F32)
    normed_keep, normed_send, branch_keep, branch_send, gain_term, shift_term = loaded(
        rows_kernel,
        [part_shape] * 4 + [term_shape] * 2,
        [normed_part, normed_in, branch_part, branch_in, x_mine],
        late=True,
    )
    terms = jnp.concatenate(
        [dpre_sums[0], dy_sum, (sums_mine + sums_theirs)[0], gain_term[0], shift_term[0]]
    ).reshape(1, 40, 128)
    others, normed_send, branch_send, terms = stage(
        middle_sent(heads), normed_send, branch_send, terms
    )

    quarter = half_rows // 4
    halves = [(0, quarter), (quarter, 2 * quarter)]
    terms = lax.all_to_all(
        jnp.broadcast_to(terms, (N_DP,) + terms.shape[1:]), "dp", 0, 0, tiled=True
    )
    cut = N_CTX * 3 * own_d
    heads = heads[:1] + tuple(combine(*middle_jobs(heads, others)))
    others = near_sent(heads)
    head_columns, head_rows = combine(
        ((heads[0],) + others, [(0, cut), (cut, heads[0].shape[0])])
    )
    ff_cut = N_CTX * 4 * own_d
    ff_columns, ff_rows = combine(
        ((ff[0],) + near_ff, [(0, ff_cut), (ff_cut, ff[0].shape[0])])
    )
    back = jnp.concatenate(
        [
            head_columns.reshape(N_CTX, 3, own_d, 128),
            ff_columns.reshape(N_CTX, 4, own_d, 128),
        ],
        axis=1,
    )
    back, head_rows, normed_other, branch_other, terms = stage(
        back,
        head_rows,
        exchange_ctx(normed_send, CTX_B),
        exchange_ctx(branch_send, CTX_A),
        terms,
    )
    normed_keep, normed_send, branch_keep, branch_send = combine(
        ((normed_keep, normed_other), halves),
        ((branch_keep, branch_other), halves),
    )
    normed_keep, normed_send, branch_keep, branch_send, back, head_rows = stage(
        normed_keep, normed_send, branch_keep, branch_send, back, head_rows
    )
    back = lax.all_to_all(back, "ctx", 0, 0, tiled=True)
    head_rows = rows_to_owner(head_rows)
    terms = jnp.sum(terms, axis=0, keepdims=True)

    def rows_of(value):
        return value.reshape(TILES, -1, 128).transpose(1, 0, 2).reshape(1, -1, D).astype(F32)

    new_fc2 = adam_update(w_fc2, rows_of(ff_rows), mom1_fc2, mom2_fc2, 2.0 / math.sqrt(FF))
    normed_other, branch_other, terms, new_fc2 = stage(
        exchange_ctx(normed_send, CTX_A), exchange_ctx(branch_send, CTX_B), terms, new_fc2
    )
    eighth = [(0, HALF_ROWS), (HALF_ROWS, 2 * HALF_ROWS)]
    normed_keep, normed_send, branch_keep, branch_send = combine(
        ((normed_keep, normed_other), eighth),
        ((branch_keep, branch_other), eighth),
    )
    normed_keep, normed_send, branch_keep, branch_send, back = stage(
        normed_keep, normed_send, branch_keep, branch_send, back
    )
    terms = lax.all_to_all(
        jnp.broadcast_to(terms, (N_CTX,) + terms.shape[1:]), "ctx", 0, 0, tiled=True
    )
    normed_other, branch_other, head_rows, terms = stage(
        exchange_ctx(normed_send, CTX_Y), exchange_ctx(branch_send, CTX_Y), head_rows, terms
    )
    normed_rows, branch_rows = combine(
        ((normed_keep, normed_other), [(0, HALF_ROWS)]),
        ((branch_keep, branch_other), [(0, HALF_ROWS)]),
    )
    terms_other = swap(terms)
    new_vec = pl.pallas_call(
        vector_kernel,
        out_shape=(jax.ShapeDtypeStruct(vectors.shape, F32),) * 3,
        in_specs=[SCALAR] + [WHOLE] * 5,
        out_specs=(WHOLE,) * 3,
        scratch_shapes=[pltpu.VMEM((16, D), F32)],
        compiler_params=ROOM,
    )(
        tp_rank.astype(jnp.int32).reshape(1),
        terms,
        terms_other,
        vectors,
        mom1_vec,
        mom2_vec,
    )
    new_out = adam_update(w_out, rows_of(head_rows), mom1_out, mom2_out, 16.0 / math.sqrt(D))
    block_output, input_grad = pl.pallas_call(
        finish_kernel,
        out_shape=(
            jax.ShapeDtypeStruct(block_input.shape, BF),
            jax.ShapeDtypeStruct(block_input.shape, F32),
        ),
        in_specs=[SCALAR] + [WHOLE] * 8,
        out_specs=(WHOLE,) * 2,
        compiler_params=ROOM,
    )(
        tp_rank.astype(jnp.int32).reshape(1),
        norm_gain[None],
        (vectors[7] + vectors[8])[None],
        block_input,
        out_cotangent,
        normed_rows,
        branch_rows,
        swap(normed_rows),
        swap(branch_rows),
    )
    columns_state = (
        w_qkv.transpose(1, 0, 2),
        mom1_qkv.transpose(1, 0, 2),
        mom2_qkv.transpose(1, 0, 2),
        w_fc1,
        mom1_fc1,
        mom2_fc1,
    )
    new_columns = pl.pallas_call(
        adam_kernel,
        out_shape=tuple(jax.ShapeDtypeStruct(v.shape, F32) for v in columns_state),
        in_specs=[WHOLE] * 7,
        out_specs=(WHOLE,) * 6,
        compiler_params=ROOM,
    )(back, *columns_state)
    new_qkv = [value.transpose(1, 0, 2) for value in new_columns[:3]]
    new_fc1 = new_columns[3:]
    return (
        block_output,
        input_grad,
        new_qkv[0],
        new_out[0],
        new_fc1[0],
        new_fc2[0],
        new_vec[0],
        new_qkv[1],
        new_out[1],
        new_fc1[1],
        new_fc2[1],
        new_vec[1],
        new_qkv[2],
        new_out[2],
        new_fc1[2],
        new_fc2[2],
        new_vec[2],
    )


def solution(mesh):
    in_specs = (
        P(("dp", "ctx"), None),
        P(("dp", "ctx"), None),
        P("dp", "ctx"),
        P("dp", None),
        P(("dp", "ctx"), None, "tp"),
        P("tp", ("dp", "ctx"), None),
        P(("dp", "ctx"), "tp"),
        P("tp", ("dp", "ctx"), None),
        P(),
        P(("dp", "ctx"), None, "tp"),
        P("tp", ("dp", "ctx"), None),
        P(("dp", "ctx"), "tp"),
        P("tp", ("dp", "ctx"), None),
        P(),
        P(("dp", "ctx"), None, "tp"),
        P("tp", ("dp", "ctx"), None),
        P(("dp", "ctx"), "tp"),
        P("tp", ("dp", "ctx"), None),
        P(),
    )
    out_specs = (
        P(("dp", "ctx"), None),
        P(("dp", "ctx"), None),
        P(("dp", "ctx"), None, "tp"),
        P("tp", ("dp", "ctx"), None),
        P(("dp", "ctx"), "tp"),
        P("tp", ("dp", "ctx"), None),
        P(),
        P(("dp", "ctx"), None, "tp"),
        P("tp", ("dp", "ctx"), None),
        P(("dp", "ctx"), "tp"),
        P("tp", ("dp", "ctx"), None),
        P(),
        P(("dp", "ctx"), None, "tp"),
        P("tp", ("dp", "ctx"), None),
        P(("dp", "ctx"), "tp"),
        P("tp", ("dp", "ctx"), None),
        P(),
    )
    return jax.shard_map(shards, mesh=mesh, in_specs=in_specs, out_specs=out_specs, check_vma=False)
```

```python
import math

import jax
import jax.numpy as jnp
from jax import lax
from jax.experimental import pallas as pl
from jax.experimental.pallas import tpu as pltpu
from jax.sharding import PartitionSpec as P

D = 2048
FF = 8192
HD = 64
ROT = 32
STEP = 10

NORM_EPS = 1e-05
SCORE_SCALE = 0.125
MASKED = -1e30
ROPE_BASE = 10000.0
BETA_ONE = 0.9
BETA_TWO = 0.95
ADAM_EPS = 1e-08
WEIGHT_DECAY = 0.1

N_DP = 8
N_CTX = 8
N_TP = 2
TEAM = N_CTX * N_TP
GROUP = 1024
HALF_ROWS = 64
FEAT = D // TEAM
HIDDEN = FF // TEAM
QKV = 3 * FEAT
Q_BLOCK = 256
UNITS = HIDDEN // N_DP

BF = jnp.bfloat16
F32 = jnp.float32


def adam_update(weight, gradient, moment_one, moment_two, step_rate):
    moment_one = BETA_ONE * moment_one + (1.0 - BETA_ONE) * gradient
    moment_two = BETA_TWO * moment_two + (1.0 - BETA_TWO) * gradient * gradient
    first_hat = moment_one / (1.0 - BETA_ONE**STEP)
    second_hat = moment_two / (1.0 - BETA_TWO**STEP)
    weight = weight - step_rate * (
        first_hat / (jnp.sqrt(second_hat) + ADAM_EPS) + WEIGHT_DECAY * weight
    )
    return (weight, moment_one, moment_two)


def gelu_and_slope(hidden):
    root = math.sqrt(2.0 / math.pi)
    square = hidden * hidden
    bent = jnp.tanh(root * (hidden + 0.044715 * hidden * square))
    value = 0.5 * hidden * (1.0 + bent)
    slope = 0.5 * (1.0 + bent) + 0.5 * hidden * (1.0 - bent * bent) * root * (
        1.0 + 3.0 * 0.044715 * square
    )
    return (value, slope)


def dot(left, right, dims):
    return lax.dot_general(left, right, (dims, ((), ())), preferred_element_type=F32)


WHOLE = pl.BlockSpec(memory_space=pltpu.VMEM)
SCALAR = pl.BlockSpec(memory_space=pltpu.SMEM)
ROOM = pltpu.CompilerParams(vmem_limit_bytes=24 * 2**20)


class Near:
    def __init__(self, value):
        self.value = value


def loaded(kernel, out_shape, operands, scalars=(), scratch=(), flops=0, late=False, limit=36):
    near_ins = [isinstance(v, Near) for v in operands]
    lists = [
        [v.value] if isinstance(v, Near) else v if isinstance(v, list) else [v] for v in operands
    ]
    parts_at = [[(v[1], v[2]) if isinstance(v, tuple) else (0, v.shape[0]) for v in vs] for vs in lists]
    lists = [[v[0] if isinstance(v, tuple) else v for v in vs] for vs in lists]
    near_outs = [isinstance(v, Near) for v in out_shape]
    shapes = [v.value if isinstance(v, Near) else v for v in out_shape]
    arrays = [v for values in lists for v in values]
    far_ins = [i for i, near in enumerate(near_ins) if not near]
    far_outs = [k for k, near in enumerate(near_outs) if not near]
    cuts = []
    for i in far_ins:
        at = 0
        for part, value in enumerate(lists[i]):
            (start, rows), pieces = parts_at[i][part], 1
            nbytes = value.nbytes // value.shape[0] * rows
            while nbytes // pieces > 2**19 and rows % (pieces * 32) == 0:
                pieces = pieces * 2
            size = rows // pieces
            cuts = cuts + [(i, part, start + k * size, at + k * size, size) for k in range(pieces)]
            at = at + rows
    first = [sum(len(v) for v in lists[:i]) for i in range(len(lists))]
    counts = (len(scalars), len(arrays), len(shapes), len(far_ins), len(far_outs))

    def body(*refs):
        parts, at = [], 0
        for count in counts:
            parts.append(refs[at : at + count])
            at = at + count
        given, ins, outs, held, written = parts
        rest, in_sems, out_sems = refs[at:-2], refs[-2], refs[-1]
        ins_at = [ins[first[i]] for i in range(len(lists))]
        for i, ref in zip(far_ins, held):
            ins_at[i] = ref
        outs_at = list(outs)
        for k, ref in zip(far_outs, written):
            outs_at[k] = ref
        copies, waited, sent = [], set(), {}
        for n, (i, part, source, to, size) in enumerate(cuts):
            copies.append(
                pltpu.make_async_copy(
                    ins[first[i] + part].at[pl.ds(source, size)],
                    ins_at[i].at[pl.ds(to, size)],
                    in_sems.at[n],
                )
            )
            copies[-1].start()

        def ready(operand, array=None):
            for n, (i, part, _, _, _) in enumerate(cuts):
                if i == operand and array in (None, part) and n not in waited:
                    copies[n].wait()
                    waited.add(n)

        def done(k):
            if not near_outs[k]:
                sent[k] = pltpu.make_async_copy(outs_at[k], outs[k], out_sems.at[k])
                sent[k].start()

        if late:
            kernel(ready, done, *given, *ins_at, *outs_at, *rest)
        else:
            for i in range(len(lists)):
                ready(i)
            kernel(*given, *ins_at, *outs_at, *rest)
        for i in range(len(lists)):
            ready(i)
        for k in range(len(shapes)):
            if k not in sent:
                done(k)
        for copy in sent.values():
            copy.wait()

    moved = sum(v.nbytes for v in arrays) + sum(
        math.prod(v.shape) * jnp.dtype(v.dtype).itemsize for v in shapes
    )
    anywhere = pl.BlockSpec(memory_space=pl.ANY)
    in_specs, placed = [SCALAR] * len(scalars), []
    for near, values in zip(near_ins, lists):
        in_specs = in_specs + [WHOLE if near else anywhere] * len(values)
        space = pltpu.VMEM if near else pltpu.HBM
        placed = placed + [pltpu.with_memory_space_constraint(v, space) for v in values]
    return pl.pallas_call(
        body,
        out_shape=tuple(
            (pltpu.VMEM if near else pltpu.HBM)(v.shape, v.dtype)
            for near, v in zip(near_outs, shapes)
        ),
        in_specs=in_specs,
        out_specs=tuple(WHOLE if near else anywhere for near in near_outs),
        scratch_shapes=[
            pltpu.VMEM((sum(n for _, n in parts_at[i]),) + lists[i][0].shape[1:], lists[i][0].dtype)
            for i in far_ins
        ]
        + [pltpu.VMEM(shapes[k].shape, shapes[k].dtype) for k in far_outs]
        + list(scratch)
        + [
            pltpu.SemaphoreType.DMA((max(1, len(cuts)),)),
            pltpu.SemaphoreType.DMA((len(shapes),)),
        ],
        compiler_params=pltpu.CompilerParams(vmem_limit_bytes=limit * 2**20),
        cost_estimate=pl.CostEstimate(flops=flops, bytes_accessed=moved, transcendentals=0),
    )(*scalars, *placed)


TILES = D // 128
COLS = (QKV + HIDDEN) // 128
OUT_ROWS = FEAT // N_DP
COL_ROWS = N_CTX * COLS * (D // N_DP // N_CTX)
PIECE = COL_ROWS + TILES * (OUT_ROWS + UNITS)
THIRD = PIECE // 3


def pack_kernel(qkv_ref, fc1_ref, tok_ref, fc2_ref, columns_ref, fc2s_ref):
    for c in range(N_CTX):
        for part in range(3):
            columns_ref[c, part] = qkv_ref[part, :, c * FEAT : (c + 1) * FEAT].astype(BF)
        for pair in range(HIDDEN // 128):
            at = [(2 * pair + e) * N_CTX * UNITS + c * UNITS for e in range(2)]
            columns_ref[c, 3 + pair] = jnp.concatenate(
                [fc1_ref[:, i : i + UNITS] for i in at], axis=1
            ).astype(BF)
        columns_ref[c, COLS] = tok_ref[...].astype(BF)
    for tile in range(TILES):
        fc2s_ref[tile] = fc2_ref[:, tile * 128 : (tile + 1) * 128].astype(BF)


MASKS = (0, 4, 1, 3, 4 ^ 1, 4 ^ 3, 1 ^ 3, 4 ^ 1 ^ 3)


NT = ((1,), (1,))
NN = ((1,), (0,))
TN = ((0,), (0,))


def place(block, piece, qkv, fc1, out, fc2):
    own_d = D // N_DP // N_CTX
    for src in range(N_CTX):
        at = pl.ds(pl.multiple_of(block * (D // N_DP) + src * own_d, own_d), own_d)
        for j in range(COLS):
            start = (src * COLS + j) * own_d
            rows = piece[start : start + own_d, :]
            if j < 3:
                qkv[at, j * 128 : (j + 1) * 128] = rows
            else:
                fc1[at, (j - 3) * 128 : (j - 2) * 128] = rows
    for to, start, count in (
        (out, COL_ROWS, OUT_ROWS),
        (fc2, COL_ROWS + TILES * OUT_ROWS, UNITS),
    ):
        at = pl.ds(pl.multiple_of(block * count, count), count)
        for tile in range(TILES):
            to[at, tile * 128 : (tile + 1) * 128] = piece[
                start + tile * count : start + (tile + 1) * count, :
            ]


def fold(block, qkv, fc1, out, fc2, piece):
    own_d = D // N_DP // N_CTX
    for src in range(N_CTX):
        at = pl.ds(pl.multiple_of(block * (D // N_DP) + src * own_d, own_d), own_d)
        for j in range(COLS):
            to = (src * COLS + j) * own_d
            if j < 3:
                piece[to : to + own_d, :] = qkv[at, j * 128 : (j + 1) * 128]
            else:
                piece[to : to + own_d, :] = fc1[at, (j - 3) * 128 : (j - 2) * 128]
    for ref, start, count in (
        (out, COL_ROWS, OUT_ROWS),
        (fc2, COL_ROWS + TILES * OUT_ROWS, UNITS),
    ):
        at = pl.ds(pl.multiple_of(block * count, count), count)
        for tile in range(TILES):
            piece[start + tile * count : start + (tile + 1) * count, :] = ref[
                at, tile * 128 : (tile + 1) * 128
            ]


class Thirds:
    def __init__(self, refs):
        self.refs = refs

    def __setitem__(self, at, value):
        k = at[0].start // THIRD
        self.refs[k][at[0].start - k * THIRD : at[0].stop - k * THIRD, :] = value


def normal(value):
    value = value.astype(F32)
    centered = value - jnp.mean(value, axis=-1, keepdims=True)
    inv_std = lax.rsqrt(jnp.mean(centered * centered, axis=-1, keepdims=True) + NORM_EPS)
    return (centered * inv_std, inv_std)


def norm_kernel(ready, done, x, dy, gain, shift, normed, dy_out):
    ready(2)
    ready(3)
    for part in range(4):
        at = slice(part * 2 * HALF_ROWS, (part + 1) * 2 * HALF_ROWS)
        ready(0, part)
        normed[at, :] = (normal(x[at, :])[0] * gain[...] + shift[...]).astype(BF)
    done(0)
    ready(1)
    dy_out[...] = dy[...]


def half_branch(normed, dy, mats, biases, outs):
    qkv, fc1, out, fc2 = mats
    bias_fc1, bias_qkv = biases
    active, dhid, sums, pre, dattn = outs
    value, slope = gelu_and_slope(dot(normed[...], fc1[...], NN) + bias_fc1[...])
    active[...] = value.astype(BF)
    grad = (dot(dy[...], fc2[...], NT) * slope).astype(BF)
    dhid[...] = grad
    sums[...] = jnp.sum(grad.astype(F32), axis=0, keepdims=True)
    pre[...] = dot(normed[...], qkv[...], NN) + bias_qkv[...]
    dattn[...] = dot(dy[...], out[...], NT).astype(BF)


def place_kernel(ready, done, rank_ref, *refs):
    pieces, (normed, dy, *biases), outs = refs[:N_DP], refs[N_DP : N_DP + 4], refs[N_DP + 4 :]
    mats = outs[:4]
    for k, flip in enumerate(MASKS):
        ready(k)
        place(rank_ref[0] ^ flip, pieces[k], *mats)
    for k in range(4):
        done(k)
        ready(N_DP + k)
    half_branch(normed, dy, mats, biases, outs[4:])


def feed_forward_kernel(ready, done, *refs):
    normed_mine, dy_mine, active_mine, dhid_mine, normed, dy, *mats = refs[:10]
    biases, outs, (grad_fc1, grad_fc2) = refs[10:12], refs[12:17], refs[17:]
    for i in range(4, 12):
        ready(i)
    half_branch(normed, dy, mats, biases, outs)
    active, dhid = outs[:2]
    for k in range(5):
        done(k)
    for i in range(4):
        ready(i)
    for k in range(D // HIDDEN):
        at = slice(k * HIDDEN, (k + 1) * HIDDEN)
        grad_fc2[:, at] = (
            dot(active_mine[...], dy_mine[:, at], TN) + dot(active[...], dy[:, at], TN)
        ).astype(BF)
        grad_fc1[at, :] = (
            dot(normed_mine[:, at], dhid_mine[...], TN) + dot(normed[:, at], dhid[...], TN)
        ).astype(BF)


def attention_kernel(
    pre_mine,
    pre_theirs,
    dattn_mine,
    dattn_theirs,
    cos,
    sin,
    marks,
    key_tok,
    attended,
    dpre,
    sums,
    query_scr,
    key_scr,
    value_scr,
    dkey_scr,
    dvalue_scr,
    dattn_all,
):
    lane = lax.broadcasted_iota(jnp.int32, (1, FEAT), 1)
    early = (lane % HD) < (ROT // 2)
    first_head = lane < HD

    def partner(value):
        return jnp.where(
            early,
            pltpu.roll(value, FEAT - ROT // 2, axis=1),
            pltpu.roll(value, ROT // 2, axis=1),
        )

    half = GROUP // 2
    for i, (pre, dattn) in enumerate(((pre_mine, dattn_mine), (pre_theirs, dattn_theirs))):
        at = slice(i * half, (i + 1) * half)
        query = pre[:, :FEAT]
        query = (query * cos[at, :] + partner(query) * sin[at, :]).astype(BF)
        query_scr[at, :] = query * jnp.asarray(SCORE_SCALE, BF)
        key = pre[:, FEAT : 2 * FEAT]
        key_scr[at, :] = (key * cos[at, :] + partner(key) * sin[at, :]).astype(BF)
        value_scr[at, :] = pre[:, 2 * FEAT :].astype(BF)
        dattn_all[at, :] = dattn[...]
    dkey_scr[...] = jnp.zeros_like(dkey_scr)
    dvalue_scr[...] = jnp.zeros_like(dvalue_scr)

    @pl.loop(0, GROUP // Q_BLOCK)
    def _(step):
        rows = pl.ds(pl.multiple_of(step * Q_BLOCK, Q_BLOCK), Q_BLOCK)
        query = query_scr[rows, :]
        dattn = dattn_all[rows, :]
        key = key_scr[...]
        value = value_scr[...]
        token = key_tok[...]
        mask = (token <= marks[rows, 0:1]) & (token >= marks[rows, 1:2])
        zero = jnp.zeros((), BF)
        out_parts = []
        dquery_parts = []
        for head in range(2):
            inside = first_head if head == 0 else jnp.logical_not(first_head)
            query_h = jnp.where(inside, query, zero)
            dattn_h = jnp.where(inside, dattn, zero)
            scores = dot(query_h, key, NT)
            scores = jnp.where(mask, scores, MASKED)
            top = jnp.max(scores, axis=1, keepdims=True)
            probs = jnp.exp(scores - top)
            probs = probs * (1.0 / jnp.sum(probs, axis=1, keepdims=True))
            probs_b = probs.astype(BF)
            mixed = dot(probs_b, value, NN)
            delta = jnp.sum(
                jnp.where(inside, mixed, 0.0) * dattn_h.astype(F32), axis=1, keepdims=True
            )
            dprobs = dot(dattn_h, value, NT)
            dscore = (probs * (dprobs - delta)).astype(BF)
            dquery_parts.append(dot(dscore, key, NN))
            dkey_scr[...] += dot(dscore, query_h, TN)
            dvalue_scr[...] += dot(probs_b, dattn_h, TN)
            out_parts.append(mixed)
        attended[rows, :] = jnp.where(first_head, out_parts[0], out_parts[1]).astype(BF)
        dquery = jnp.where(first_head, dquery_parts[0], dquery_parts[1]) * SCORE_SCALE
        dpre[rows, :FEAT] = (dquery * cos[rows, :] - partner(dquery) * sin[rows, :]).astype(BF)

    dkey = dkey_scr[...]
    dpre[:, FEAT : 2 * FEAT] = (dkey * cos[...] - partner(dkey) * sin[...]).astype(BF)
    dpre[:, 2 * FEAT :] = dvalue_scr[...].astype(BF)
    sums[...] = jnp.sum(dpre[...].astype(F32), axis=0, keepdims=True)


def heads_kernel(ready, done, rank_ref, *refs):
    attended, dpre, qkv, fc1, out, fc2 = refs[:6]
    active, dhid, normed, dy = refs[6:8], refs[8:10], refs[10:12], refs[12:14]
    grad_fc1, grad_fc2, *sums = refs[14:20]
    grads, (grad_qkv, grad_out) = refs[20 : 20 + N_DP + 2], refs[20 + N_DP + 2 :]
    grads = list(grads[: N_DP - 1]) + [Thirds(grads[N_DP - 1 :])]
    halves = [slice(i * GROUP // 2, (i + 1) * GROUP // 2) for i in range(2)]
    for i in (1, 0):
        rows = halves[i]
        for k in range(D // HIDDEN):
            at = slice(k * HIDDEN, (k + 1) * HIDDEN)
            sums[2 * i][:, at] = (
                dot(dpre[rows, :], qkv[at, :], NT) + dot(dhid[i][...], fc1[at, :], NT)
            ).astype(BF)
            sums[2 * i + 1][:, at] = (
                dot(attended[rows, :], out[:, at], NN) + dot(active[i][...], fc2[:, at], NN)
            ).astype(BF)
        done(2 * i)
        done(2 * i + 1)
    for i in range(10, 14):
        ready(i)
    for k in range(D // HIDDEN):
        at = slice(k * HIDDEN, (k + 1) * HIDDEN)
        grad_qkv[at, :] = sum(
            dot(normed[i][:, at], dpre[halves[i], :], TN) for i in range(2)
        ).astype(BF)
        grad_out[:, at] = sum(
            dot(attended[halves[i], :], dy[i][:, at], TN) for i in range(2)
        ).astype(BF)
    for k in reversed(range(N_DP)):
        fold(rank_ref[0] ^ MASKS[k], grad_qkv, grad_fc1, grad_out, grad_fc2, grads[k])
        for third in range(3 if k == N_DP - 1 else 1):
            done(4 + k + third)


def rows_kernel(ready, done, normed_ref, normed_in, branch_ref, branch_in, x, *outs):
    normed_keep, normed_send, branch_keep, branch_send, gain_ref, shift_ref = outs
    block = 2 * HALF_ROWS
    ready(2)
    ready(3)
    for i in range(4):
        rows, to = slice(i * block, (i + 1) * block), branch_keep if i % 2 == 0 else branch_send
        total = branch_ref[rows, :].astype(F32) + branch_in[rows, :].astype(F32)
        to[(i // 2) * block : (i // 2 + 1) * block, :] = total.astype(BF)
    done(2)
    done(3)
    ready(0)
    ready(1)
    ready(4)
    gain = jnp.zeros((1, D), F32)
    shift = jnp.zeros((1, D), F32)
    for i in range(4):
        rows, to = slice(i * block, (i + 1) * block), normed_keep if i < 2 else normed_send
        total = normed_ref[rows, :].astype(F32) + normed_in[rows, :].astype(F32)
        gain = gain + jnp.sum(total * normal(x[rows, :])[0], axis=0, keepdims=True)
        shift = shift + jnp.sum(total, axis=0, keepdims=True)
        to[(i % 2) * block : (i % 2 + 1) * block, :] = total.astype(BF)
    gain_ref[...] = gain
    shift_ref[...] = shift


def combine(*jobs):
    operands = [value for values, _ in jobs for value in values]
    outs = [
        jax.ShapeDtypeStruct((stop - start, values[0].shape[1]), BF)
        for values, ranges in jobs
        for start, stop in ranges
    ]

    def kernel(*refs):
        ins, to = list(refs[: len(operands)]), list(refs[len(operands) :])
        for values, ranges in jobs:
            mine, ins = ins[: len(values)], ins[len(values) :]
            for start, stop in ranges:
                total = mine[0][start:stop, :].astype(F32)
                for ref in mine[1:]:
                    total = total + ref[start:stop, :].astype(F32)
                to.pop(0)[...] = total.astype(BF)

    return loaded(kernel, outs, operands)


def patched(pieces, others, starts):
    count = len(pieces)

    def kernel(*refs):
        for i in range(count):
            piece, other, to = refs[i], refs[count + i], refs[2 * count + i]
            start, stop = starts[i], starts[i] + other.shape[0]
            if start > 0:
                to[:start, :] = piece[:start, :]
            to[start:stop, :] = (piece[start:stop, :].astype(F32) + other[...].astype(F32)).astype(BF)
            if stop < piece.shape[0]:
                to[stop:, :] = piece[stop:, :]

    outs = [jax.ShapeDtypeStruct(v.shape, BF) for v in pieces]
    return loaded(kernel, outs, list(pieces) + list(others))


def finish_kernel(core_ref, gain_ref, bias_ref, x_ref, dy_ref, *refs):
    (normed_own, branch_own, normed_other, branch_other), (output_ref, grad_ref) = refs[:4], refs[4:]
    core = core_ref[0]
    for side, normed_in, branch_in in (
        (core, normed_own, branch_own),
        (1 - core, normed_other, branch_other),
    ):
        rows = pl.ds(pl.multiple_of(side * HALF_ROWS, HALF_ROWS), HALF_ROWS)
        value = x_ref[rows, :]
        normal_x, inv_std = normal(value)
        value = value.astype(F32)
        output_ref[rows, :] = (value + branch_in[...].astype(F32) + bias_ref[...]).astype(BF)
        scaled = normed_in[...].astype(F32) * gain_ref[...]
        grad_ref[rows, :] = dy_ref[rows, :].astype(F32) + inv_std * (
            scaled
            - jnp.mean(scaled, axis=-1, keepdims=True)
            - normal_x * jnp.mean(scaled * normal_x, axis=-1, keepdims=True)
        )


def vector_kernel(core_ref, own_ref, other_ref, *refs):
    (vectors_ref, first_ref, second_ref), outs, grad = refs[:3], refs[3:6], refs[6]
    first_core = core_ref[0] == 0
    units = FF // N_TP // D
    gain = jnp.zeros((TILES, 128), F32)
    shift = jnp.zeros((TILES, 128), F32)
    for side in range(N_TP):
        terms = jnp.where(first_core == (side == 0), own_ref[...], other_ref[...])
        for c in range(N_CTX):
            at = slice(side * (D // N_TP) + c * FEAT, side * (D // N_TP) + (c + 1) * FEAT)
            grad[0:3, at] = terms[c, 0:3, :]
            grad[7:8, at] = terms[c, 3:4, :]
            grad[8:9, at] = terms[c, 3:4, :]
            gain = gain + terms[c, 8 : 8 + TILES, :]
            shift = shift + terms[c, 8 + TILES : 8 + 2 * TILES, :]
        for e in range(N_DP):
            row = slice(3 + side * units + e // (N_DP // units), 4 + side * units + e // (N_DP // units))
            for c in range(0, N_CTX, 2):
                lanes = (e % (N_DP // units)) * N_CTX * UNITS + c * UNITS
                pair = [
                    terms[c + k, 4 + e // 2 : 5 + e // 2, (e % 2) * UNITS : (e % 2 + 1) * UNITS]
                    for k in range(2)
                ]
                grad[row, lanes : lanes + 2 * UNITS] = jnp.concatenate(pair, axis=1)
    for tile in range(TILES):
        grad[9:10, tile * 128 : (tile + 1) * 128] = gain[tile : tile + 1, :]
        grad[10:11, tile * 128 : (tile + 1) * 128] = shift[tile : tile + 1, :]
    new = adam_update(vectors_ref[...], grad[0:11, :], first_ref[...], second_ref[...], 0.2)
    for ref, value in zip(outs, new):
        ref[...] = value


RATE_IN = 2.0 / math.sqrt(D)
RATE_OUT = 16.0 / math.sqrt(D)
RATE_BACK = 2.0 / math.sqrt(FF)


def adam_kernel(ready, done, back, fc2_rows, *refs):
    ins, outs = refs[:9], refs[9:]

    def update(group, at, gradient, rate):
        weight, first, second = [ins[group * 3 + i][at] for i in range(3)]
        for i, value in enumerate(adam_update(weight, gradient, first, second, rate)):
            outs[group * 3 + i][at] = value

    for i in range(1, 11):
        ready(i)
    for tile in range(TILES):
        lanes = slice(tile * 128, (tile + 1) * 128)
        rows = fc2_rows[tile * UNITS : (tile + 1) * UNITS, :].astype(F32)
        update(2, (slice(None), lanes), rows, RATE_BACK)
    for k in range(6, 9):
        done(k)
    ready(0)
    for c in range(N_CTX):
        for part in range(3):
            at = (part, slice(None), slice(c * FEAT, (c + 1) * FEAT))
            update(0, at, back[c, part].astype(F32), RATE_IN)
    for e in range(N_DP):
        pair, side = divmod(e, 2)
        for c in range(0, N_CTX, 2):
            gradient = jnp.concatenate(
                [
                    back[c + k, 3 + pair].astype(F32)[:, side * UNITS : (side + 1) * UNITS]
                    for k in range(2)
                ],
                axis=1,
            )
            to = e * N_CTX * UNITS + c * UNITS
            update(1, (slice(None), slice(to, to + 2 * UNITS)), gradient, RATE_IN)


def swap(value):
    return lax.ppermute(value, "tp", [(0, 1), (1, 0)])


DP_Y, DP_A, DP_B = 4, 1, 3
CTX_Y, CTX_A, CTX_B = 1, 2, 6
BLOCKS = (0, 1, 2, 3, 6, 7, 4, 5)


def exchange(value, flip):
    return lax.ppermute(value, "dp", [(d, d ^ flip) for d in range(N_DP)])


def exchange_ctx(value, flip):
    return lax.ppermute(value, "ctx", [(c, c ^ flip) for c in range(N_CTX)])


def stage(*values):
    return lax.optimization_barrier(values)


def added(left, right):
    return (left.astype(F32) + right.astype(F32)).astype(BF)


def rows_to_team(value):
    pairs = [
        (d * N_CTX + c, c * N_CTX + d) for d in range(N_DP) for c in range(N_CTX)
    ]
    return lax.ppermute(value, ("dp", "ctx"), pairs)


def rows_to_owner(value):
    pairs = [
        (c * N_CTX + d, d * N_CTX + c) for d in range(N_DP) for c in range(N_CTX)
    ]
    return lax.ppermute(value, ("dp", "ctx"), pairs)


def shards(
    block_input,
    out_cotangent,
    token_order,
    seq_lengths,
    w_qkv,
    w_out,
    w_fc1,
    w_fc2,
    vectors,
    mom1_qkv,
    mom1_out,
    mom1_fc1,
    mom1_fc2,
    mom1_vec,
    mom2_qkv,
    mom2_out,
    mom2_fc1,
    mom2_fc2,
    mom2_vec,
):
    ctx_rank = lax.axis_index("ctx")
    tp_rank = lax.axis_index("tp")
    team_rank = tp_rank * N_CTX + ctx_rank
    own_d = D // (N_DP * N_CTX)
    half_rows = N_CTX * HALF_ROWS
    two = 2 * HALF_ROWS
    lanes = QKV + HIDDEN

    def half(value):
        return lax.dynamic_slice_in_dim(value, tp_rank * HALF_ROWS, HALF_ROWS, 0)

    tok_pair = jnp.concatenate([token_order // 32, token_order % 32], axis=0)
    columns, fc2 = loaded(
        pack_kernel,
        [
            jax.ShapeDtypeStruct((N_CTX, COLS + 1, own_d, 128), BF),
            jax.ShapeDtypeStruct((TILES, UNITS, 128), BF),
        ],
        [
            w_qkv.transpose(1, 0, 2),
            w_fc1,
            jnp.pad(tok_pair.astype(F32), ((0, own_d - 2), (0, 0))),
            w_fc2[0],
        ],
    )
    x_own = half(block_input)
    dy_own = half(out_cotangent)
    out = w_out[0].astype(BF).reshape(OUT_ROWS, TILES, 128).transpose(1, 0, 2)
    x_own, dy_own, out, columns, fc2 = stage(x_own, dy_own, out, columns, fc2)

    columns = lax.all_to_all(columns, "ctx", 0, 0, tiled=True)
    columns, out, x_other, dy_other = stage(
        columns, rows_to_team(out), exchange_ctx(x_own, CTX_Y), exchange_ctx(dy_own, CTX_Y)
    )
    piece = jnp.concatenate(
        [
            columns[:, :COLS].reshape(COL_ROWS, 128),
            out.reshape(TILES * OUT_ROWS, 128),
            fc2.reshape(TILES * UNITS, 128),
        ],
        axis=0,
    )
    x_two = jnp.concatenate([x_own, x_other], axis=0)
    dy_two = jnp.concatenate([dy_own, dy_other], axis=0)
    piece, x_two, dy_two, columns = stage(piece, x_two, dy_two, columns)

    by_y, by_a, by_b = [exchange(piece, flip) for flip in (DP_Y, DP_A, DP_B)]
    x_a, dy_b = stage(exchange_ctx(x_two, CTX_A), exchange_ctx(dy_two, CTX_B))
    tok = columns[:, COLS, :2].astype(jnp.int32)
    tok = (tok[:, 0] * 32 + tok[:, 1]).reshape(N_CTX * N_TP, HALF_ROWS)
    blocks = jnp.bitwise_xor(ctx_rank, jnp.asarray(BLOCKS, jnp.int32)) * N_TP + tp_rank
    tok = tok[jnp.concatenate([blocks, jnp.bitwise_xor(blocks, 1)])].reshape(GROUP)
    first = jnp.zeros_like(tok)
    end = jnp.zeros((), jnp.int32)
    for i in range(seq_lengths.shape[1]):
        first = jnp.where(tok >= end, end, first)
        end = end + seq_lengths[0, i]
    position = (tok - first).astype(F32)
    lane = jnp.arange(FEAT) % HD
    inverse = ROPE_BASE ** (-(2.0 * (lane % (ROT // 2)).astype(F32)) / ROT)
    inverse = jnp.where(lane < ROT, inverse, 0.0)
    rotation = position[:, None] * inverse[None, :]
    cos_table = jnp.cos(rotation)
    sin_table = jnp.sin(rotation) * jnp.where(lane < ROT // 2, -1.0, 1.0)
    tok = tok.astype(F32)
    first = first.astype(F32)
    marks = jnp.where(jnp.arange(FEAT)[None, :] == 0, tok[:, None], first[:, None])
    norm_gain = vectors[9]
    norm_shift = vectors[10]
    bias_qkv = lax.dynamic_slice(vectors, (0, team_rank * FEAT), (3, FEAT))
    bias_fc1 = vectors[3:7].reshape(N_TP, N_DP, N_CTX, UNITS)
    bias_fc1 = lax.dynamic_slice(bias_fc1, (tp_rank, 0, ctx_rank, 0), (1, N_DP, 1, UNITS))
    bias_fc1 = bias_fc1.reshape(HIDDEN)

    x_four = jnp.concatenate([x_two, x_a], axis=0)
    dy_four = jnp.concatenate([dy_two, dy_b], axis=0)
    by_ya = exchange(by_y, DP_A)
    by_yb = exchange(by_b, DP_Y)
    by_ab = exchange(by_a, DP_B)
    x_b, dy_a, tok, marks, cos_table, sin_table, bias_qkv, bias_fc1 = stage(
        exchange_ctx(x_four, CTX_B),
        exchange_ctx(dy_four, CTX_A),
        tok,
        marks,
        cos_table,
        sin_table,
        bias_qkv,
        bias_fc1,
    )
    x_mine = [x_two, x_a, (x_b, 0, two), (x_b, two, two)]
    dy_parts = [dy_two, (dy_a, 0, two), dy_b, (dy_a, two, two)]

    def shaped(rows, columns, kind=BF):
        return jax.ShapeDtypeStruct((rows, columns), kind)

    dp_rank = lax.axis_index("dp").astype(jnp.int32).reshape(1)
    normed_mine, dy_mine = loaded(
        norm_kernel,
        [Near(shaped(half_rows, D))] * 2,
        [x_mine, dy_parts, norm_gain[None], norm_shift[None]],
        late=True,
    )
    normed_mine, dy_mine, far1, far2, far3 = stage(
        normed_mine,
        dy_mine,
        exchange(by_ya[:THIRD], DP_B),
        exchange(by_yb[THIRD : 2 * THIRD], DP_A),
        exchange(by_ab[2 * THIRD :], DP_Y),
    )
    half_shapes = [
        Near(shaped(half_rows, HIDDEN)),
        Near(shaped(half_rows, HIDDEN)),
        shaped(1, HIDDEN, F32),
        Near(shaped(half_rows, QKV, F32)),
        Near(shaped(half_rows, FEAT)),
    ]
    biases = [bias_fc1[None], bias_qkv.reshape(1, QKV)]
    mat_qkv, mat_fc1, mat_out, mat_fc2, active_mine, dhid_mine, sums_mine, pre_mine, dattn_mine = (
        loaded(
            place_kernel,
            [
                Near(shaped(D, QKV)),
                Near(shaped(D, HIDDEN)),
                Near(shaped(FEAT, D)),
                Near(shaped(HIDDEN, D)),
            ]
            + half_shapes,
            [piece, by_y, by_a, by_b, by_ya, by_yb, by_ab, [far1, far2, far3]]
            + [Near(normed_mine), Near(dy_mine)]
            + biases,
            [dp_rank],
            flops=2 * half_rows * D * (2 * HIDDEN + QKV + FEAT),
            late=True,
        )
    )
    mats = [mat_qkv, mat_fc1, mat_out, mat_fc2]
    normed_theirs, dy_theirs, mats, active_mine, dhid_mine, pre_mine, dattn_mine = stage(
        swap(normed_mine), swap(dy_mine), mats, active_mine, dhid_mine, pre_mine, dattn_mine
    )
    active_theirs, dhid_theirs, sums_theirs, pre_theirs, dattn_theirs, grad_fc1, grad_fc2 = loaded(
        feed_forward_kernel,
        half_shapes + [Near(shaped(D, HIDDEN)), Near(shaped(HIDDEN, D))],
        [Near(v) for v in (normed_mine, dy_mine, active_mine, dhid_mine)]
        + [normed_theirs, dy_theirs]
        + [Near(v) for v in mats]
        + biases,
        flops=12 * half_rows * D * HIDDEN,
        late=True,
    )

    def far_sent(pieces):
        return exchange(pieces[7], DP_B), exchange(pieces[8], DP_A), exchange(pieces[9], DP_Y)

    def far_added(pieces, others):
        return pieces[:4] + tuple(patched(pieces[4:7], others, (0, THIRD, 2 * THIRD)))

    def middle_sent(pieces):
        return exchange(pieces[4], DP_A), exchange(pieces[5], DP_Y), exchange(pieces[6], DP_B)

    def middle_jobs(pieces, others):
        whole = [(0, pieces[0].shape[0])]
        return (
            ((pieces[1], others[0]), whole),
            ((pieces[2], others[2]), whole),
            ((pieces[3], others[1]), whole),
        )

    def near_sent(pieces):
        return exchange(pieces[1], DP_Y), exchange(pieces[2], DP_A), exchange(pieces[3], DP_B)

    attended, dpre, dpre_sums = loaded(
        attention_kernel,
        [Near(shaped(GROUP, FEAT)), Near(shaped(GROUP, QKV)), shaped(1, QKV, F32)],
        [
            Near(pre_mine),
            Near(pre_theirs),
            Near(dattn_mine),
            Near(dattn_theirs),
            cos_table,
            sin_table,
            marks,
            tok[None, :],
        ],
        scratch=[
            pltpu.VMEM((GROUP, FEAT), BF),
            pltpu.VMEM((GROUP, FEAT), BF),
            pltpu.VMEM((GROUP, FEAT), BF),
            pltpu.VMEM((GROUP, FEAT), F32),
            pltpu.VMEM((GROUP, FEAT), F32),
            pltpu.VMEM((GROUP, FEAT), BF),
        ],
        flops=28 * GROUP * GROUP * HD,
        limit=26,
    )
    normed_part, branch_part, normed_out, branch_out, *pieces = loaded(
        heads_kernel,
        [shaped(half_rows, D)] * 4
        + [shaped(PIECE, 128)] * (N_DP - 1)
        + [shaped(THIRD, 128)] * 3,
        [Near(attended), Near(dpre)]
        + [Near(v) for v in mats]
        + [Near(v) for v in (active_mine, active_theirs, dhid_mine, dhid_theirs)]
        + [Near(normed_mine), normed_theirs, Near(dy_mine), dy_theirs]
        + [Near(grad_fc1), Near(grad_fc2)],
        [dp_rank],
        [pltpu.VMEM((D, QKV), BF), pltpu.VMEM((FEAT, D), BF)],
        flops=4 * GROUP * D * (QKV + FEAT + HIDDEN),
        late=True,
    )
    pieces = tuple(pieces)
    dy_sum = sum(
        jnp.sum(lax.dynamic_slice_in_dim(value, team_rank * FEAT, FEAT, 1).astype(F32), axis=0)
        for value in (dy_mine, dy_theirs)
    )
    others, normed_in, branch_in, dy_sum = stage(
        far_sent(pieces), swap(normed_out), swap(branch_out), dy_sum
    )
    pieces = far_added(pieces, others)
    pieces, normed_in, branch_in = stage(pieces, normed_in, branch_in)
    others = middle_sent(pieces)
    part_shape = jax.ShapeDtypeStruct((half_rows // 2, D), BF)
    term_shape = jax.ShapeDtypeStruct((1, D), F32)
    normed_keep, normed_send, branch_keep, branch_send, gain_term, shift_term = loaded(
        rows_kernel,
        [part_shape] * 4 + [term_shape] * 2,
        [normed_part, normed_in, branch_part, branch_in, x_mine],
        late=True,
    )
    terms = jnp.concatenate(
        [dpre_sums[0], dy_sum, (sums_mine + sums_theirs)[0], gain_term[0], shift_term[0]]
    ).reshape(1, 40, 128)
    normed_send, branch_send, terms = stage(normed_send, branch_send, terms)

    quarter = half_rows // 4
    halves = [(0, quarter), (quarter, 2 * quarter)]
    terms = lax.all_to_all(
        jnp.broadcast_to(terms, (N_DP,) + terms.shape[1:]), "dp", 0, 0, tiled=True
    )
    others, normed_other, branch_other, terms = stage(
        others, exchange_ctx(normed_send, CTX_B), exchange_ctx(branch_send, CTX_A), terms
    )
    normed_keep, normed_send, branch_keep, branch_send, *near = combine(
        ((normed_keep, normed_other), halves),
        ((branch_keep, branch_other), halves),
        *middle_jobs(pieces, others),
    )
    pieces = pieces[:1] + tuple(near)
    normed_keep, normed_send, branch_keep, branch_send, pieces = stage(
        normed_keep, normed_send, branch_keep, branch_send, pieces
    )
    terms = jnp.sum(terms, axis=0, keepdims=True)
    terms = lax.all_to_all(
        jnp.broadcast_to(terms, (N_CTX,) + terms.shape[1:]), "ctx", 0, 0, tiled=True
    )

    others = near_sent(pieces)
    normed_other, branch_other = stage(
        exchange_ctx(normed_send, CTX_A), exchange_ctx(branch_send, CTX_B)
    )
    eighth = [(0, HALF_ROWS), (HALF_ROWS, 2 * HALF_ROWS)]
    normed_keep, normed_send, branch_keep, branch_send = combine(
        ((normed_keep, normed_other), eighth), ((branch_keep, branch_other), eighth)
    )
    normed_keep, normed_send, branch_keep, branch_send = stage(
        normed_keep, normed_send, branch_keep, branch_send
    )
    cut = COL_ROWS + TILES * OUT_ROWS
    back, head_rows, ff_rows = combine(
        ((pieces[0],) + others, [(0, COL_ROWS), (COL_ROWS, cut), (cut, PIECE)])
    )
    back = back.reshape(N_CTX, COLS, own_d, 128)
    normed_other, branch_other, back, head_rows, ff_rows, terms = stage(
        exchange_ctx(normed_send, CTX_Y),
        exchange_ctx(branch_send, CTX_Y),
        back,
        head_rows,
        ff_rows,
        terms,
    )
    back = lax.all_to_all(back, "ctx", 0, 0, tiled=True)
    head_rows = rows_to_owner(head_rows)
    normed_rows, branch_rows = combine(
        ((normed_keep, normed_other), [(0, HALF_ROWS)]),
        ((branch_keep, branch_other), [(0, HALF_ROWS)]),
    )
    normed_theirs, branch_theirs, terms_other = stage(
        swap(normed_rows), swap(branch_rows), swap(terms)
    )
    state = [
        [value.transpose(1, 0, 2) for value in (w_qkv, mom1_qkv, mom2_qkv)],
        [w_fc1, mom1_fc1, mom2_fc1],
        [value[0] for value in (w_fc2, mom1_fc2, mom2_fc2)],
    ]
    state = [value for values in state for value in values]
    new_state = loaded(
        adam_kernel,
        [jax.ShapeDtypeStruct(value.shape, F32) for value in state],
        [back, ff_rows] + state,
        late=True,
    )
    new_qkv = [value.transpose(1, 0, 2) for value in new_state[:3]]
    new_fc1 = new_state[3:6]
    new_fc2 = [value[None] for value in new_state[6:]]
    sum_out = head_rows.reshape(TILES, OUT_ROWS, 128).transpose(1, 0, 2).reshape(1, OUT_ROWS, D)
    new_out = adam_update(w_out, sum_out.astype(F32), mom1_out, mom2_out, RATE_OUT)
    new_vec = pl.pallas_call(
        vector_kernel,
        out_shape=(jax.ShapeDtypeStruct(vectors.shape, F32),) * 3,
        in_specs=[SCALAR] + [WHOLE] * 5,
        out_specs=(WHOLE,) * 3,
        scratch_shapes=[pltpu.VMEM((16, D), F32)],
        compiler_params=ROOM,
    )(
        tp_rank.astype(jnp.int32).reshape(1),
        terms,
        terms_other,
        vectors,
        mom1_vec,
        mom2_vec,
    )
    block_output, input_grad = pl.pallas_call(
        finish_kernel,
        out_shape=(
            jax.ShapeDtypeStruct(block_input.shape, BF),
            jax.ShapeDtypeStruct(block_input.shape, F32),
        ),
        in_specs=[SCALAR] + [WHOLE] * 8,
        out_specs=(WHOLE,) * 2,
        compiler_params=ROOM,
    )(
        tp_rank.astype(jnp.int32).reshape(1),
        norm_gain[None],
        (vectors[7] + vectors[8])[None],
        block_input,
        out_cotangent,
        normed_rows,
        branch_rows,
        normed_theirs,
        branch_theirs,
    )
    return (
        block_output,
        input_grad,
        new_qkv[0],
        new_out[0],
        new_fc1[0],
        new_fc2[0],
        new_vec[0],
        new_qkv[1],
        new_out[1],
        new_fc1[1],
        new_fc2[1],
        new_vec[1],
        new_qkv[2],
        new_out[2],
        new_fc1[2],
        new_fc2[2],
        new_vec[2],
    )


def solution(mesh):
    in_specs = (
        P(("dp", "ctx"), None),
        P(("dp", "ctx"), None),
        P("dp", "ctx"),
        P("dp", None),
        P(("dp", "ctx"), None, "tp"),
        P("tp", ("dp", "ctx"), None),
        P(("dp", "ctx"), "tp"),
        P("tp", ("dp", "ctx"), None),
        P(),
        P(("dp", "ctx"), None, "tp"),
        P("tp", ("dp", "ctx"), None),
        P(("dp", "ctx"), "tp"),
        P("tp", ("dp", "ctx"), None),
        P(),
        P(("dp", "ctx"), None, "tp"),
        P("tp", ("dp", "ctx"), None),
        P(("dp", "ctx"), "tp"),
        P("tp", ("dp", "ctx"), None),
        P(),
    )
    out_specs = (
        P(("dp", "ctx"), None),
        P(("dp", "ctx"), None),
        P(("dp", "ctx"), None, "tp"),
        P("tp", ("dp", "ctx"), None),
        P(("dp", "ctx"), "tp"),
        P("tp", ("dp", "ctx"), None),
        P(),
        P(("dp", "ctx"), None, "tp"),
        P("tp", ("dp", "ctx"), None),
        P(("dp", "ctx"), "tp"),
        P("tp", ("dp", "ctx"), None),
        P(),
        P(("dp", "ctx"), None, "tp"),
        P("tp", ("dp", "ctx"), None),
        P(("dp", "ctx"), "tp"),
        P("tp", ("dp", "ctx"), None),
        P(),
    )
    return jax.shard_map(shards, mesh=mesh, in_specs=in_specs, out_specs=out_specs, check_vma=False)
```

```python
import math

import jax
import jax.numpy as jnp
from jax import lax
from jax.experimental import pallas as pl
from jax.experimental.pallas import tpu as pltpu
from jax.sharding import PartitionSpec as P

D = 2048
FF = 8192
HD = 64
ROT = 32
STEP = 10

NORM_EPS = 1e-05
SCORE_SCALE = 0.125
MASKED = -1e30
ROPE_BASE = 10000.0
BETA_ONE = 0.9
BETA_TWO = 0.95
ADAM_EPS = 1e-08
WEIGHT_DECAY = 0.1

N_DP = 8
N_CTX = 8
N_TP = 2
TEAM = N_CTX * N_TP
GROUP = 1024
HALF_ROWS = 64
FEAT = D // TEAM
HIDDEN = FF // TEAM
QKV = 3 * FEAT
Q_BLOCK = 256
UNITS = HIDDEN // N_DP

BF = jnp.bfloat16
F32 = jnp.float32


def adam_update(weight, gradient, moment_one, moment_two, step_rate):
    moment_one = BETA_ONE * moment_one + (1.0 - BETA_ONE) * gradient
    moment_two = BETA_TWO * moment_two + (1.0 - BETA_TWO) * gradient * gradient
    first_hat = moment_one / (1.0 - BETA_ONE**STEP)
    second_hat = moment_two / (1.0 - BETA_TWO**STEP)
    weight = weight - step_rate * (
        first_hat / (jnp.sqrt(second_hat) + ADAM_EPS) + WEIGHT_DECAY * weight
    )
    return (weight, moment_one, moment_two)


def gelu_and_slope(hidden):
    root = math.sqrt(2.0 / math.pi)
    square = hidden * hidden
    bent = jnp.tanh(root * (hidden + 0.044715 * hidden * square))
    value = 0.5 * hidden * (1.0 + bent)
    slope = 0.5 * (1.0 + bent) + 0.5 * hidden * (1.0 - bent * bent) * root * (
        1.0 + 3.0 * 0.044715 * square
    )
    return (value, slope)


def dot(left, right, dims):
    return lax.dot_general(left, right, (dims, ((), ())), preferred_element_type=F32)


WHOLE = pl.BlockSpec(memory_space=pltpu.VMEM)
SCALAR = pl.BlockSpec(memory_space=pltpu.SMEM)
ROOM = pltpu.CompilerParams(vmem_limit_bytes=24 * 2**20)


class Near:
    def __init__(self, value):
        self.value = value


def loaded(kernel, out_shape, operands, scalars=(), scratch=(), flops=0, late=False, limit=36):
    near_ins = [isinstance(v, Near) for v in operands]
    lists = [
        [v.value] if isinstance(v, Near) else v if isinstance(v, list) else [v] for v in operands
    ]
    parts_at = [[(v[1], v[2]) if isinstance(v, tuple) else (0, v.shape[0]) for v in vs] for vs in lists]
    lists = [[v[0] if isinstance(v, tuple) else v for v in vs] for vs in lists]
    near_outs = [isinstance(v, Near) for v in out_shape]
    shapes = [v.value if isinstance(v, Near) else v for v in out_shape]
    arrays = [v for values in lists for v in values]
    far_ins = [i for i, near in enumerate(near_ins) if not near]
    far_outs = [k for k, near in enumerate(near_outs) if not near]
    cuts = []
    for i in far_ins:
        at = 0
        for part, value in enumerate(lists[i]):
            (start, rows), pieces = parts_at[i][part], 1
            nbytes = value.nbytes // value.shape[0] * rows
            while nbytes // pieces > 2**19 and rows % (pieces * 32) == 0:
                pieces = pieces * 2
            size = rows // pieces
            cuts = cuts + [(i, part, start + k * size, at + k * size, size) for k in range(pieces)]
            at = at + rows
    first = [sum(len(v) for v in lists[:i]) for i in range(len(lists))]
    counts = (len(scalars), len(arrays), len(shapes), len(far_ins), len(far_outs))

    def body(*refs):
        parts, at = [], 0
        for count in counts:
            parts.append(refs[at : at + count])
            at = at + count
        given, ins, outs, held, written = parts
        rest, in_sems, out_sems = refs[at:-2], refs[-2], refs[-1]
        ins_at = [ins[first[i]] for i in range(len(lists))]
        for i, ref in zip(far_ins, held):
            ins_at[i] = ref
        outs_at = list(outs)
        for k, ref in zip(far_outs, written):
            outs_at[k] = ref
        copies, waited, sent = [], set(), {}
        for n, (i, part, source, to, size) in enumerate(cuts):
            copies.append(
                pltpu.make_async_copy(
                    ins[first[i] + part].at[pl.ds(source, size)],
                    ins_at[i].at[pl.ds(to, size)],
                    in_sems.at[n],
                )
            )
            copies[-1].start()

        def ready(operand, array=None):
            for n, (i, part, _, _, _) in enumerate(cuts):
                if i == operand and array in (None, part) and n not in waited:
                    copies[n].wait()
                    waited.add(n)

        def done(k):
            if not near_outs[k]:
                sent[k] = pltpu.make_async_copy(outs_at[k], outs[k], out_sems.at[k])
                sent[k].start()

        if late:
            kernel(ready, done, *given, *ins_at, *outs_at, *rest)
        else:
            for i in range(len(lists)):
                ready(i)
            kernel(*given, *ins_at, *outs_at, *rest)
        for i in range(len(lists)):
            ready(i)
        for k in range(len(shapes)):
            if k not in sent:
                done(k)
        for copy in sent.values():
            copy.wait()

    moved = sum(v.nbytes for v in arrays) + sum(
        math.prod(v.shape) * jnp.dtype(v.dtype).itemsize for v in shapes
    )
    anywhere = pl.BlockSpec(memory_space=pl.ANY)
    in_specs, placed = [SCALAR] * len(scalars), []
    for near, values in zip(near_ins, lists):
        in_specs = in_specs + [WHOLE if near else anywhere] * len(values)
        space = pltpu.VMEM if near else pltpu.HBM
        placed = placed + [pltpu.with_memory_space_constraint(v, space) for v in values]
    return pl.pallas_call(
        body,
        out_shape=tuple(
            (pltpu.VMEM if near else pltpu.HBM)(v.shape, v.dtype)
            for near, v in zip(near_outs, shapes)
        ),
        in_specs=in_specs,
        out_specs=tuple(WHOLE if near else anywhere for near in near_outs),
        scratch_shapes=[
            pltpu.VMEM((sum(n for _, n in parts_at[i]),) + lists[i][0].shape[1:], lists[i][0].dtype)
            for i in far_ins
        ]
        + [pltpu.VMEM(shapes[k].shape, shapes[k].dtype) for k in far_outs]
        + list(scratch)
        + [
            pltpu.SemaphoreType.DMA((max(1, len(cuts)),)),
            pltpu.SemaphoreType.DMA((len(shapes),)),
        ],
        compiler_params=pltpu.CompilerParams(vmem_limit_bytes=limit * 2**20),
        cost_estimate=pl.CostEstimate(flops=flops, bytes_accessed=moved, transcendentals=0),
    )(*scalars, *placed)


TILES = D // 128
COLS = (QKV + HIDDEN) // 128
OUT_ROWS = FEAT // N_DP
COL_ROWS = N_CTX * COLS * (D // N_DP // N_CTX)
PIECE = COL_ROWS + TILES * (OUT_ROWS + UNITS)
THIRD = PIECE // 3


def pack_kernel(qkv_ref, fc1_ref, tok_ref, fc2_ref, columns_ref, fc2s_ref):
    for c in range(N_CTX):
        for part in range(3):
            columns_ref[c, part] = qkv_ref[part, :, c * FEAT : (c + 1) * FEAT].astype(BF)
        for pair in range(HIDDEN // 128):
            at = [(2 * pair + e) * N_CTX * UNITS + c * UNITS for e in range(2)]
            columns_ref[c, 3 + pair] = jnp.concatenate(
                [fc1_ref[:, i : i + UNITS] for i in at], axis=1
            ).astype(BF)
        columns_ref[c, COLS] = tok_ref[...].astype(BF)
    for tile in range(TILES):
        fc2s_ref[tile] = fc2_ref[:, tile * 128 : (tile + 1) * 128].astype(BF)


MASKS = (0, 4, 1, 3, 4 ^ 1, 4 ^ 3, 1 ^ 3, 4 ^ 1 ^ 3)


NT = ((1,), (1,))
NN = ((1,), (0,))
TN = ((0,), (0,))


def place(block, piece, qkv, fc1, out, fc2):
    own_d = D // N_DP // N_CTX
    for src in range(N_CTX):
        at = pl.ds(pl.multiple_of(block * (D // N_DP) + src * own_d, own_d), own_d)
        for j in range(COLS):
            start = (src * COLS + j) * own_d
            rows = piece[start : start + own_d, :]
            if j < 3:
                qkv[at, j * 128 : (j + 1) * 128] = rows
            else:
                fc1[at, (j - 3) * 128 : (j - 2) * 128] = rows
    for to, start, count in (
        (out, COL_ROWS, OUT_ROWS),
        (fc2, COL_ROWS + TILES * OUT_ROWS, UNITS),
    ):
        at = pl.ds(pl.multiple_of(block * count, count), count)
        for tile in range(TILES):
            to[at, tile * 128 : (tile + 1) * 128] = piece[
                start + tile * count : start + (tile + 1) * count, :
            ]


def fold(block, qkv, fc1, out, fc2, piece):
    own_d = D // N_DP // N_CTX
    for src in range(N_CTX):
        at = pl.ds(pl.multiple_of(block * (D // N_DP) + src * own_d, own_d), own_d)
        for j in range(COLS):
            to = (src * COLS + j) * own_d
            if j < 3:
                piece[to : to + own_d, :] = qkv[at, j * 128 : (j + 1) * 128]
            else:
                piece[to : to + own_d, :] = fc1[at, (j - 3) * 128 : (j - 2) * 128]
    for ref, start, count in (
        (out, COL_ROWS, OUT_ROWS),
        (fc2, COL_ROWS + TILES * OUT_ROWS, UNITS),
    ):
        at = pl.ds(pl.multiple_of(block * count, count), count)
        for tile in range(TILES):
            piece[start + tile * count : start + (tile + 1) * count, :] = ref[
                at, tile * 128 : (tile + 1) * 128
            ]


class Thirds:
    def __init__(self, refs):
        self.refs = refs

    def __setitem__(self, at, value):
        k = at[0].start // THIRD
        self.refs[k][at[0].start - k * THIRD : at[0].stop - k * THIRD, :] = value


def normal(value):
    value = value.astype(F32)
    centered = value - jnp.mean(value, axis=-1, keepdims=True)
    inv_std = lax.rsqrt(jnp.mean(centered * centered, axis=-1, keepdims=True) + NORM_EPS)
    return (centered * inv_std, inv_std)


def norm_kernel(ready, done, x, dy, gain, shift, normed, dy_out):
    ready(2)
    ready(3)
    for part in range(4):
        at = slice(part * 2 * HALF_ROWS, (part + 1) * 2 * HALF_ROWS)
        ready(0, part)
        normed[at, :] = (normal(x[at, :])[0] * gain[...] + shift[...]).astype(BF)
    done(0)
    ready(1)
    dy_out[...] = dy[...]


def half_branch(normed, dy, mats, biases, outs):
    qkv, fc1, out, fc2 = mats
    bias_fc1, bias_qkv = biases
    active, dhid, sums, pre, dattn = outs
    value, slope = gelu_and_slope(dot(normed[...], fc1[...], NN) + bias_fc1[...])
    active[...] = value.astype(BF)
    grad = (dot(dy[...], fc2[...], NT) * slope).astype(BF)
    dhid[...] = grad
    sums[...] = jnp.sum(grad.astype(F32), axis=0, keepdims=True)
    pre[...] = dot(normed[...], qkv[...], NN) + bias_qkv[...]
    dattn[...] = dot(dy[...], out[...], NT).astype(BF)


def place_kernel(ready, done, rank_ref, *refs):
    pieces, (normed, dy, *biases), outs = refs[:N_DP], refs[N_DP : N_DP + 4], refs[N_DP + 4 :]
    mats = outs[:4]
    for k, flip in enumerate(MASKS):
        ready(k)
        place(rank_ref[0] ^ flip, pieces[k], *mats)
    for k in range(4):
        done(k)
        ready(N_DP + k)
    half_branch(normed, dy, mats, biases, outs[4:])


def feed_forward_kernel(ready, done, *refs):
    normed_mine, dy_mine, active_mine, dhid_mine, normed, dy, *mats = refs[:10]
    biases, outs, (grad_fc1, grad_fc2) = refs[10:12], refs[12:17], refs[17:]
    for i in range(4, 12):
        ready(i)
    half_branch(normed, dy, mats, biases, outs)
    active, dhid = outs[:2]
    for k in range(5):
        done(k)
    for i in range(4):
        ready(i)
    for k in range(D // HIDDEN):
        at = slice(k * HIDDEN, (k + 1) * HIDDEN)
        grad_fc2[:, at] = (
            dot(active_mine[...], dy_mine[:, at], TN) + dot(active[...], dy[:, at], TN)
        ).astype(BF)
        grad_fc1[at, :] = (
            dot(normed_mine[:, at], dhid_mine[...], TN) + dot(normed[:, at], dhid[...], TN)
        ).astype(BF)


def attention_kernel(
    pre_mine,
    pre_theirs,
    dattn_mine,
    dattn_theirs,
    cos,
    sin,
    marks,
    key_tok,
    attended,
    dpre,
    sums,
    query_scr,
    key_scr,
    value_scr,
    dkey_scr,
    dvalue_scr,
    dattn_all,
):
    lane = lax.broadcasted_iota(jnp.int32, (1, FEAT), 1)
    early = (lane % HD) < (ROT // 2)
    first_head = lane < HD

    def partner(value):
        return jnp.where(
            early,
            pltpu.roll(value, FEAT - ROT // 2, axis=1),
            pltpu.roll(value, ROT // 2, axis=1),
        )

    half = GROUP // 2
    for i, (pre, dattn) in enumerate(((pre_mine, dattn_mine), (pre_theirs, dattn_theirs))):
        at = slice(i * half, (i + 1) * half)
        query = pre[:, :FEAT]
        query = (query * cos[at, :] + partner(query) * sin[at, :]).astype(BF)
        query_scr[at, :] = query * jnp.asarray(SCORE_SCALE, BF)
        key = pre[:, FEAT : 2 * FEAT]
        key_scr[at, :] = (key * cos[at, :] + partner(key) * sin[at, :]).astype(BF)
        value_scr[at, :] = pre[:, 2 * FEAT :].astype(BF)
        dattn_all[at, :] = dattn[...]
    dkey_scr[...] = jnp.zeros_like(dkey_scr)
    dvalue_scr[...] = jnp.zeros_like(dvalue_scr)

    @pl.loop(0, GROUP // Q_BLOCK)
    def _(step):
        rows = pl.ds(pl.multiple_of(step * Q_BLOCK, Q_BLOCK), Q_BLOCK)
        query = query_scr[rows, :]
        dattn = dattn_all[rows, :]
        key = key_scr[...]
        value = value_scr[...]
        token = key_tok[...]
        mask = (token <= marks[rows, 0:1]) & (token >= marks[rows, 1:2])
        zero = jnp.zeros((), BF)
        out_parts = []
        dquery_parts = []
        for head in range(2):
            inside = first_head if head == 0 else jnp.logical_not(first_head)
            query_h = jnp.where(inside, query, zero)
            dattn_h = jnp.where(inside, dattn, zero)
            scores = dot(query_h, key, NT)
            scores = jnp.where(mask, scores, MASKED)
            top = jnp.max(scores, axis=1, keepdims=True)
            probs = jnp.exp(scores - top)
            probs = probs * (1.0 / jnp.sum(probs, axis=1, keepdims=True))
            probs_b = probs.astype(BF)
            mixed = dot(probs_b, value, NN)
            delta = jnp.sum(
                jnp.where(inside, mixed, 0.0) * dattn_h.astype(F32), axis=1, keepdims=True
            )
            dprobs = dot(dattn_h, value, NT)
            dscore = (probs * (dprobs - delta)).astype(BF)
            dquery_parts.append(dot(dscore, key, NN))
            dkey_scr[...] += dot(dscore, query_h, TN)
            dvalue_scr[...] += dot(probs_b, dattn_h, TN)
            out_parts.append(mixed)
        attended[rows, :] = jnp.where(first_head, out_parts[0], out_parts[1]).astype(BF)
        dquery = jnp.where(first_head, dquery_parts[0], dquery_parts[1]) * SCORE_SCALE
        dpre[rows, :FEAT] = (dquery * cos[rows, :] - partner(dquery) * sin[rows, :]).astype(BF)

    dkey = dkey_scr[...]
    dpre[:, FEAT : 2 * FEAT] = (dkey * cos[...] - partner(dkey) * sin[...]).astype(BF)
    dpre[:, 2 * FEAT :] = dvalue_scr[...].astype(BF)
    sums[...] = jnp.sum(dpre[...].astype(F32), axis=0, keepdims=True)


def heads_kernel(ready, done, rank_ref, *refs):
    attended, dpre, qkv, fc1, out, fc2 = refs[:6]
    active, dhid, normed, dy = refs[6:8], refs[8:10], refs[10:12], refs[12:14]
    grad_fc1, grad_fc2, *sums = refs[14:20]
    grads, (grad_qkv, grad_out) = refs[20 : 20 + N_DP + 2], refs[20 + N_DP + 2 :]
    grads = list(grads[: N_DP - 1]) + [Thirds(grads[N_DP - 1 :])]
    halves = [slice(i * GROUP // 2, (i + 1) * GROUP // 2) for i in range(2)]
    for i in (1, 0):
        rows = halves[i]
        for k in range(D // HIDDEN):
            at = slice(k * HIDDEN, (k + 1) * HIDDEN)
            sums[2 * i][:, at] = (
                dot(dpre[rows, :], qkv[at, :], NT) + dot(dhid[i][...], fc1[at, :], NT)
            ).astype(BF)
            sums[2 * i + 1][:, at] = (
                dot(attended[rows, :], out[:, at], NN) + dot(active[i][...], fc2[:, at], NN)
            ).astype(BF)
        done(2 * i)
        done(2 * i + 1)
    for i in range(10, 14):
        ready(i)
    for k in range(D // HIDDEN):
        at = slice(k * HIDDEN, (k + 1) * HIDDEN)
        grad_qkv[at, :] = sum(
            dot(normed[i][:, at], dpre[halves[i], :], TN) for i in range(2)
        ).astype(BF)
        grad_out[:, at] = sum(
            dot(attended[halves[i], :], dy[i][:, at], TN) for i in range(2)
        ).astype(BF)
    for k in reversed(range(N_DP)):
        fold(rank_ref[0] ^ MASKS[k], grad_qkv, grad_fc1, grad_out, grad_fc2, grads[k])
        for third in range(3 if k == N_DP - 1 else 1):
            done(4 + k + third)


def rows_kernel(ready, done, normed_ref, normed_in, branch_ref, branch_in, x, *outs):
    normed_keep, normed_send, branch_keep, branch_send, gain_ref, shift_ref = outs
    block = 2 * HALF_ROWS
    ready(2)
    ready(3)
    for i in range(4):
        rows, to = slice(i * block, (i + 1) * block), branch_keep if i % 2 == 0 else branch_send
        total = branch_ref[rows, :].astype(F32) + branch_in[rows, :].astype(F32)
        to[(i // 2) * block : (i // 2 + 1) * block, :] = total.astype(BF)
    done(2)
    done(3)
    ready(0)
    ready(1)
    ready(4)
    gain = jnp.zeros((1, D), F32)
    shift = jnp.zeros((1, D), F32)
    for i in range(4):
        rows, to = slice(i * block, (i + 1) * block), normed_keep if i < 2 else normed_send
        total = normed_ref[rows, :].astype(F32) + normed_in[rows, :].astype(F32)
        gain = gain + jnp.sum(total * normal(x[rows, :])[0], axis=0, keepdims=True)
        shift = shift + jnp.sum(total, axis=0, keepdims=True)
        to[(i % 2) * block : (i % 2 + 1) * block, :] = total.astype(BF)
    gain_ref[...] = gain
    shift_ref[...] = shift


def combine(*jobs):
    operands = [value for values, _ in jobs for value in values]
    outs = [
        jax.ShapeDtypeStruct((stop - start, values[0].shape[1]), BF)
        for values, ranges in jobs
        for start, stop in ranges
    ]

    def kernel(*refs):
        ins, to = list(refs[: len(operands)]), list(refs[len(operands) :])
        for values, ranges in jobs:
            mine, ins = ins[: len(values)], ins[len(values) :]
            for start, stop in ranges:
                total = mine[0][start:stop, :].astype(F32)
                for ref in mine[1:]:
                    total = total + ref[start:stop, :].astype(F32)
                to.pop(0)[...] = total.astype(BF)

    return loaded(kernel, outs, operands)


def patched(pieces, others, starts):
    count = len(pieces)

    def kernel(*refs):
        for i in range(count):
            piece, other, to = refs[i], refs[count + i], refs[2 * count + i]
            start, stop = starts[i], starts[i] + other.shape[0]
            if start > 0:
                to[:start, :] = piece[:start, :]
            to[start:stop, :] = (piece[start:stop, :].astype(F32) + other[...].astype(F32)).astype(BF)
            if stop < piece.shape[0]:
                to[stop:, :] = piece[stop:, :]

    outs = [jax.ShapeDtypeStruct(v.shape, BF) for v in pieces]
    return loaded(kernel, outs, list(pieces) + list(others))


def finish_kernel(core_ref, gain_ref, bias_ref, x_ref, dy_ref, *refs):
    (normed_own, branch_own, normed_other, branch_other), (output_ref, grad_ref) = refs[:4], refs[4:]
    core = core_ref[0]
    for side, normed_in, branch_in in (
        (core, normed_own, branch_own),
        (1 - core, normed_other, branch_other),
    ):
        rows = pl.ds(pl.multiple_of(side * HALF_ROWS, HALF_ROWS), HALF_ROWS)
        value = x_ref[rows, :]
        normal_x, inv_std = normal(value)
        value = value.astype(F32)
        output_ref[rows, :] = (value + branch_in[...].astype(F32) + bias_ref[...]).astype(BF)
        scaled = normed_in[...].astype(F32) * gain_ref[...]
        grad_ref[rows, :] = dy_ref[rows, :].astype(F32) + inv_std * (
            scaled
            - jnp.mean(scaled, axis=-1, keepdims=True)
            - normal_x * jnp.mean(scaled * normal_x, axis=-1, keepdims=True)
        )


def vector_kernel(core_ref, own_ref, other_ref, *refs):
    (vectors_ref, first_ref, second_ref), outs, grad = refs[:3], refs[3:6], refs[6]
    first_core = core_ref[0] == 0
    units = FF // N_TP // D
    gain = jnp.zeros((TILES, 128), F32)
    shift = jnp.zeros((TILES, 128), F32)
    for side in range(N_TP):
        terms = jnp.where(first_core == (side == 0), own_ref[...], other_ref[...])
        for c in range(N_CTX):
            at = slice(side * (D // N_TP) + c * FEAT, side * (D // N_TP) + (c + 1) * FEAT)
            grad[0:3, at] = terms[c, 0:3, :]
            grad[7:8, at] = terms[c, 3:4, :]
            grad[8:9, at] = terms[c, 3:4, :]
            gain = gain + terms[c, 8 : 8 + TILES, :]
            shift = shift + terms[c, 8 + TILES : 8 + 2 * TILES, :]
        for e in range(N_DP):
            row = slice(3 + side * units + e // (N_DP // units), 4 + side * units + e // (N_DP // units))
            for c in range(0, N_CTX, 2):
                lanes = (e % (N_DP // units)) * N_CTX * UNITS + c * UNITS
                pair = [
                    terms[c + k, 4 + e // 2 : 5 + e // 2, (e % 2) * UNITS : (e % 2 + 1) * UNITS]
                    for k in range(2)
                ]
                grad[row, lanes : lanes + 2 * UNITS] = jnp.concatenate(pair, axis=1)
    for tile in range(TILES):
        grad[9:10, tile * 128 : (tile + 1) * 128] = gain[tile : tile + 1, :]
        grad[10:11, tile * 128 : (tile + 1) * 128] = shift[tile : tile + 1, :]
    new = adam_update(vectors_ref[...], grad[0:11, :], first_ref[...], second_ref[...], 0.2)
    for ref, value in zip(outs, new):
        ref[...] = value


RATE_IN = 2.0 / math.sqrt(D)
RATE_OUT = 16.0 / math.sqrt(D)
RATE_BACK = 2.0 / math.sqrt(FF)


def adam_kernel(ready, done, back, fc2_rows, *refs):
    ins, outs = refs[:9], refs[9:]

    def update(group, at, gradient, rate):
        weight, first, second = [ins[group * 3 + i][at] for i in range(3)]
        for i, value in enumerate(adam_update(weight, gradient, first, second, rate)):
            outs[group * 3 + i][at] = value

    for i in range(1, 11):
        ready(i)
    for tile in range(TILES):
        lanes = slice(tile * 128, (tile + 1) * 128)
        rows = fc2_rows[tile * UNITS : (tile + 1) * UNITS, :].astype(F32)
        update(2, (slice(None), lanes), rows, RATE_BACK)
    for k in range(6, 9):
        done(k)
    ready(0)
    for c in range(N_CTX):
        for part in range(3):
            at = (part, slice(None), slice(c * FEAT, (c + 1) * FEAT))
            update(0, at, back[c, part].astype(F32), RATE_IN)
    for e in range(N_DP):
        pair, side = divmod(e, 2)
        for c in range(0, N_CTX, 2):
            gradient = jnp.concatenate(
                [
                    back[c + k, 3 + pair].astype(F32)[:, side * UNITS : (side + 1) * UNITS]
                    for k in range(2)
                ],
                axis=1,
            )
            to = e * N_CTX * UNITS + c * UNITS
            update(1, (slice(None), slice(to, to + 2 * UNITS)), gradient, RATE_IN)


def swap(value):
    return lax.ppermute(value, "tp", [(0, 1), (1, 0)])


DP_Y, DP_A, DP_B = 4, 1, 3
CTX_Y, CTX_A, CTX_B = 1, 2, 6
BLOCKS = (0, 1, 2, 3, 6, 7, 4, 5)


def exchange(value, flip):
    return lax.ppermute(value, "dp", [(d, d ^ flip) for d in range(N_DP)])


def exchange_ctx(value, flip):
    return lax.ppermute(value, "ctx", [(c, c ^ flip) for c in range(N_CTX)])


def stage(*values):
    return lax.optimization_barrier(values)


def added(left, right):
    return (left.astype(F32) + right.astype(F32)).astype(BF)


def rows_to_team(value):
    pairs = [
        (d * N_CTX + c, c * N_CTX + d) for d in range(N_DP) for c in range(N_CTX)
    ]
    return lax.ppermute(value, ("dp", "ctx"), pairs)


def rows_to_owner(value):
    pairs = [
        (c * N_CTX + d, d * N_CTX + c) for d in range(N_DP) for c in range(N_CTX)
    ]
    return lax.ppermute(value, ("dp", "ctx"), pairs)


def shards(
    block_input,
    out_cotangent,
    token_order,
    seq_lengths,
    w_qkv,
    w_out,
    w_fc1,
    w_fc2,
    vectors,
    mom1_qkv,
    mom1_out,
    mom1_fc1,
    mom1_fc2,
    mom1_vec,
    mom2_qkv,
    mom2_out,
    mom2_fc1,
    mom2_fc2,
    mom2_vec,
):
    ctx_rank = lax.axis_index("ctx")
    tp_rank = lax.axis_index("tp")
    team_rank = tp_rank * N_CTX + ctx_rank
    own_d = D // (N_DP * N_CTX)
    half_rows = N_CTX * HALF_ROWS
    two = 2 * HALF_ROWS
    lanes = QKV + HIDDEN

    def half(value):
        return lax.dynamic_slice_in_dim(value, tp_rank * HALF_ROWS, HALF_ROWS, 0)

    tok_pair = jnp.concatenate([token_order // 32, token_order % 32], axis=0)
    columns, fc2 = loaded(
        pack_kernel,
        [
            jax.ShapeDtypeStruct((N_CTX, COLS + 1, own_d, 128), BF),
            jax.ShapeDtypeStruct((TILES, UNITS, 128), BF),
        ],
        [
            w_qkv.transpose(1, 0, 2),
            w_fc1,
            jnp.pad(tok_pair.astype(F32), ((0, own_d - 2), (0, 0))),
            w_fc2[0],
        ],
    )
    x_own = half(block_input)
    dy_own = half(out_cotangent)
    out = w_out[0].astype(BF).reshape(OUT_ROWS, TILES, 128).transpose(1, 0, 2)
    x_own, dy_own, out, columns, fc2 = stage(x_own, dy_own, out, columns, fc2)

    columns = lax.all_to_all(columns, "ctx", 0, 0, tiled=True)
    columns, out, x_other, dy_other = stage(
        columns, rows_to_team(out), exchange_ctx(x_own, CTX_Y), exchange_ctx(dy_own, CTX_Y)
    )
    piece = jnp.concatenate(
        [
            columns[:, :COLS].reshape(COL_ROWS, 128),
            out.reshape(TILES * OUT_ROWS, 128),
            fc2.reshape(TILES * UNITS, 128),
        ],
        axis=0,
    )
    x_two = jnp.concatenate([x_own, x_other], axis=0)
    dy_two = jnp.concatenate([dy_own, dy_other], axis=0)
    piece, x_two, dy_two, columns = stage(piece, x_two, dy_two, columns)

    by_y, by_a, by_b = [exchange(piece, flip) for flip in (DP_Y, DP_A, DP_B)]
    x_a, dy_b = stage(exchange_ctx(x_two, CTX_A), exchange_ctx(dy_two, CTX_B))
    tok = columns[:, COLS, :2].astype(jnp.int32)
    tok = (tok[:, 0] * 32 + tok[:, 1]).reshape(N_CTX * N_TP, HALF_ROWS)
    blocks = jnp.bitwise_xor(ctx_rank, jnp.asarray(BLOCKS, jnp.int32)) * N_TP + tp_rank
    tok = tok[jnp.concatenate([blocks, jnp.bitwise_xor(blocks, 1)])].reshape(GROUP)
    first = jnp.zeros_like(tok)
    end = jnp.zeros((), jnp.int32)
    for i in range(seq_lengths.shape[1]):
        first = jnp.where(tok >= end, end, first)
        end = end + seq_lengths[0, i]
    position = (tok - first).astype(F32)
    lane = jnp.arange(FEAT) % HD
    inverse = ROPE_BASE ** (-(2.0 * (lane % (ROT // 2)).astype(F32)) / ROT)
    inverse = jnp.where(lane < ROT, inverse, 0.0)
    rotation = position[:, None] * inverse[None, :]
    cos_table = jnp.cos(rotation)
    sin_table = jnp.sin(rotation) * jnp.where(lane < ROT // 2, -1.0, 1.0)
    tok = tok.astype(F32)
    first = first.astype(F32)
    marks = jnp.where(jnp.arange(FEAT)[None, :] == 0, tok[:, None], first[:, None])
    norm_gain = vectors[9]
    norm_shift = vectors[10]
    bias_qkv = lax.dynamic_slice(vectors, (0, team_rank * FEAT), (3, FEAT))
    bias_fc1 = vectors[3:7].reshape(N_TP, N_DP, N_CTX, UNITS)
    bias_fc1 = lax.dynamic_slice(bias_fc1, (tp_rank, 0, ctx_rank, 0), (1, N_DP, 1, UNITS))
    bias_fc1 = bias_fc1.reshape(HIDDEN)

    x_four = jnp.concatenate([x_two, x_a], axis=0)
    dy_four = jnp.concatenate([dy_two, dy_b], axis=0)
    by_ya = exchange(by_y, DP_A)
    by_yb = exchange(by_b, DP_Y)
    by_ab = exchange(by_a, DP_B)
    x_b, dy_a, tok, marks, cos_table, sin_table, bias_qkv, bias_fc1 = stage(
        exchange_ctx(x_four, CTX_B),
        exchange_ctx(dy_four, CTX_A),
        tok,
        marks,
        cos_table,
        sin_table,
        bias_qkv,
        bias_fc1,
    )
    x_mine = [x_two, x_a, (x_b, 0, two), (x_b, two, two)]
    dy_parts = [dy_two, (dy_a, 0, two), dy_b, (dy_a, two, two)]

    def shaped(rows, columns, kind=BF):
        return jax.ShapeDtypeStruct((rows, columns), kind)

    dp_rank = lax.axis_index("dp").astype(jnp.int32).reshape(1)
    normed_mine, dy_mine = loaded(
        norm_kernel,
        [Near(shaped(half_rows, D))] * 2,
        [x_mine, dy_parts, norm_gain[None], norm_shift[None]],
        late=True,
    )
    normed_mine, dy_mine, far1, far2, far3 = stage(
        normed_mine,
        dy_mine,
        exchange(by_ya[:THIRD], DP_B),
        exchange(by_yb[THIRD : 2 * THIRD], DP_A),
        exchange(by_ab[2 * THIRD :], DP_Y),
    )
    half_shapes = [
        Near(shaped(half_rows, HIDDEN)),
        Near(shaped(half_rows, HIDDEN)),
        shaped(1, HIDDEN, F32),
        Near(shaped(half_rows, QKV, F32)),
        Near(shaped(half_rows, FEAT)),
    ]
    biases = [bias_fc1[None], bias_qkv.reshape(1, QKV)]
    mat_qkv, mat_fc1, mat_out, mat_fc2, active_mine, dhid_mine, sums_mine, pre_mine, dattn_mine = (
        loaded(
            place_kernel,
            [
                Near(shaped(D, QKV)),
                Near(shaped(D, HIDDEN)),
                Near(shaped(FEAT, D)),
                Near(shaped(HIDDEN, D)),
            ]
            + half_shapes,
            [piece, by_y, by_a, by_b, by_ya, by_yb, by_ab, [far1, far2, far3]]
            + [Near(normed_mine), Near(dy_mine)]
            + biases,
            [dp_rank],
            flops=2 * half_rows * D * (2 * HIDDEN + QKV + FEAT),
            late=True,
        )
    )
    mats = [mat_qkv, mat_fc1, mat_out, mat_fc2]
    normed_theirs, dy_theirs, mats, active_mine, dhid_mine, pre_mine, dattn_mine = stage(
        swap(normed_mine), swap(dy_mine), mats, active_mine, dhid_mine, pre_mine, dattn_mine
    )
    active_theirs, dhid_theirs, sums_theirs, pre_theirs, dattn_theirs, grad_fc1, grad_fc2 = loaded(
        feed_forward_kernel,
        half_shapes + [Near(shaped(D, HIDDEN)), Near(shaped(HIDDEN, D))],
        [Near(v) for v in (normed_mine, dy_mine, active_mine, dhid_mine)]
        + [normed_theirs, dy_theirs]
        + [Near(v) for v in mats]
        + biases,
        flops=12 * half_rows * D * HIDDEN,
        late=True,
    )

    def far_sent(pieces):
        return exchange(pieces[7], DP_B), exchange(pieces[8], DP_A), exchange(pieces[9], DP_Y)

    def far_added(pieces, others):
        return pieces[:4] + tuple(patched(pieces[4:7], others, (0, THIRD, 2 * THIRD)))

    def middle_sent(pieces):
        return exchange(pieces[4], DP_A), exchange(pieces[5], DP_Y), exchange(pieces[6], DP_B)

    def middle_jobs(pieces, others):
        whole = [(0, pieces[0].shape[0])]
        return (
            ((pieces[1], others[0]), whole),
            ((pieces[2], others[2]), whole),
            ((pieces[3], others[1]), whole),
        )

    def near_sent(pieces):
        return exchange(pieces[1], DP_Y), exchange(pieces[2], DP_A), exchange(pieces[3], DP_B)

    attended, dpre, dpre_sums = loaded(
        attention_kernel,
        [Near(shaped(GROUP, FEAT)), Near(shaped(GROUP, QKV)), shaped(1, QKV, F32)],
        [
            Near(pre_mine),
            Near(pre_theirs),
            Near(dattn_mine),
            Near(dattn_theirs),
            cos_table,
            sin_table,
            marks,
            tok[None, :],
        ],
        scratch=[
            pltpu.VMEM((GROUP, FEAT), BF),
            pltpu.VMEM((GROUP, FEAT), BF),
            pltpu.VMEM((GROUP, FEAT), BF),
            pltpu.VMEM((GROUP, FEAT), F32),
            pltpu.VMEM((GROUP, FEAT), F32),
            pltpu.VMEM((GROUP, FEAT), BF),
        ],
        flops=28 * GROUP * GROUP * HD,
        limit=26,
    )
    normed_part, branch_part, normed_out, branch_out, *pieces = loaded(
        heads_kernel,
        [shaped(half_rows, D)] * 4
        + [shaped(PIECE, 128)] * (N_DP - 1)
        + [shaped(THIRD, 128)] * 3,
        [Near(attended), Near(dpre)]
        + [Near(v) for v in mats]
        + [Near(v) for v in (active_mine, active_theirs, dhid_mine, dhid_theirs)]
        + [Near(normed_mine), normed_theirs, Near(dy_mine), dy_theirs]
        + [Near(grad_fc1), Near(grad_fc2)],
        [dp_rank],
        [pltpu.VMEM((D, QKV), BF), pltpu.VMEM((FEAT, D), BF)],
        flops=4 * GROUP * D * (QKV + FEAT + HIDDEN),
        late=True,
    )
    pieces = tuple(pieces)
    dy_sum = sum(
        jnp.sum(lax.dynamic_slice_in_dim(value, team_rank * FEAT, FEAT, 1).astype(F32), axis=0)
        for value in (dy_mine, dy_theirs)
    )
    others = far_sent(pieces)
    normed_in, branch_in, dy_sum = stage(swap(normed_out), swap(branch_out), dy_sum)
    pieces = far_added(pieces, others)
    others = middle_sent(pieces)
    part_shape = jax.ShapeDtypeStruct((half_rows // 2, D), BF)
    term_shape = jax.ShapeDtypeStruct((1, D), F32)
    normed_keep, normed_send, branch_keep, branch_send, gain_term, shift_term = loaded(
        rows_kernel,
        [part_shape] * 4 + [term_shape] * 2,
        [normed_part, normed_in, branch_part, branch_in, x_mine],
        late=True,
    )
    terms = jnp.concatenate(
        [dpre_sums[0], dy_sum, (sums_mine + sums_theirs)[0], gain_term[0], shift_term[0]]
    ).reshape(1, 40, 128)
    normed_send, branch_send, terms = stage(normed_send, branch_send, terms)

    quarter = half_rows // 4
    halves = [(0, quarter), (quarter, 2 * quarter)]
    terms = lax.all_to_all(
        jnp.broadcast_to(terms, (N_DP,) + terms.shape[1:]), "dp", 0, 0, tiled=True
    )
    others, normed_other, branch_other, terms = stage(
        others, exchange_ctx(normed_send, CTX_B), exchange_ctx(branch_send, CTX_A), terms
    )
    normed_keep, normed_send, branch_keep, branch_send, *near = combine(
        ((normed_keep, normed_other), halves),
        ((branch_keep, branch_other), halves),
        *middle_jobs(pieces, others),
    )
    pieces = pieces[:1] + tuple(near)
    normed_keep, normed_send, branch_keep, branch_send, pieces = stage(
        normed_keep, normed_send, branch_keep, branch_send, pieces
    )
    terms = jnp.sum(terms, axis=0, keepdims=True)
    terms = lax.all_to_all(
        jnp.broadcast_to(terms, (N_CTX,) + terms.shape[1:]), "ctx", 0, 0, tiled=True
    )

    others = near_sent(pieces)
    normed_other, branch_other = stage(
        exchange_ctx(normed_send, CTX_A), exchange_ctx(branch_send, CTX_B)
    )
    eighth = [(0, HALF_ROWS), (HALF_ROWS, 2 * HALF_ROWS)]
    normed_keep, normed_send, branch_keep, branch_send = combine(
        ((normed_keep, normed_other), eighth), ((branch_keep, branch_other), eighth)
    )
    normed_keep, normed_send, branch_keep, branch_send = stage(
        normed_keep, normed_send, branch_keep, branch_send
    )
    cut = COL_ROWS + TILES * OUT_ROWS
    back, head_rows, ff_rows = combine(
        ((pieces[0],) + others, [(0, COL_ROWS), (COL_ROWS, cut), (cut, PIECE)])
    )
    back = back.reshape(N_CTX, COLS, own_d, 128)
    normed_other, branch_other, back, head_rows, ff_rows, terms = stage(
        exchange_ctx(normed_send, CTX_Y),
        exchange_ctx(branch_send, CTX_Y),
        lax.all_to_all(back, "ctx", 0, 0, tiled=True),
        rows_to_owner(head_rows),
        ff_rows,
        terms,
    )
    normed_rows, branch_rows = combine(
        ((normed_keep, normed_other), [(0, HALF_ROWS)]),
        ((branch_keep, branch_other), [(0, HALF_ROWS)]),
    )
    normed_theirs, branch_theirs, terms_other = stage(
        swap(normed_rows), swap(branch_rows), swap(terms)
    )
    state = [
        [value.transpose(1, 0, 2) for value in (w_qkv, mom1_qkv, mom2_qkv)],
        [w_fc1, mom1_fc1, mom2_fc1],
        [value[0] for value in (w_fc2, mom1_fc2, mom2_fc2)],
    ]
    state = [value for values in state for value in values]
    new_state = loaded(
        adam_kernel,
        [jax.ShapeDtypeStruct(value.shape, F32) for value in state],
        [back, ff_rows] + state,
        late=True,
    )
    new_qkv = [value.transpose(1, 0, 2) for value in new_state[:3]]
    new_fc1 = new_state[3:6]
    new_fc2 = [value[None] for value in new_state[6:]]
    sum_out = head_rows.reshape(TILES, OUT_ROWS, 128).transpose(1, 0, 2).reshape(1, OUT_ROWS, D)
    new_out = adam_update(w_out, sum_out.astype(F32), mom1_out, mom2_out, RATE_OUT)
    new_vec = pl.pallas_call(
        vector_kernel,
        out_shape=(jax.ShapeDtypeStruct(vectors.shape, F32),) * 3,
        in_specs=[SCALAR] + [WHOLE] * 5,
        out_specs=(WHOLE,) * 3,
        scratch_shapes=[pltpu.VMEM((16, D), F32)],
        compiler_params=ROOM,
    )(
        tp_rank.astype(jnp.int32).reshape(1),
        terms,
        terms_other,
        vectors,
        mom1_vec,
        mom2_vec,
    )
    block_output, input_grad = pl.pallas_call(
        finish_kernel,
        out_shape=(
            jax.ShapeDtypeStruct(block_input.shape, BF),
            jax.ShapeDtypeStruct(block_input.shape, F32),
        ),
        in_specs=[SCALAR] + [WHOLE] * 8,
        out_specs=(WHOLE,) * 2,
        compiler_params=ROOM,
    )(
        tp_rank.astype(jnp.int32).reshape(1),
        norm_gain[None],
        (vectors[7] + vectors[8])[None],
        block_input,
        out_cotangent,
        normed_rows,
        branch_rows,
        normed_theirs,
        branch_theirs,
    )
    return (
        block_output,
        input_grad,
        new_qkv[0],
        new_out[0],
        new_fc1[0],
        new_fc2[0],
        new_vec[0],
        new_qkv[1],
        new_out[1],
        new_fc1[1],
        new_fc2[1],
        new_vec[1],
        new_qkv[2],
        new_out[2],
        new_fc1[2],
        new_fc2[2],
        new_vec[2],
    )


def solution(mesh):
    in_specs = (
        P(("dp", "ctx"), None),
        P(("dp", "ctx"), None),
        P("dp", "ctx"),
        P("dp", None),
        P(("dp", "ctx"), None, "tp"),
        P("tp", ("dp", "ctx"), None),
        P(("dp", "ctx"), "tp"),
        P("tp", ("dp", "ctx"), None),
        P(),
        P(("dp", "ctx"), None, "tp"),
        P("tp", ("dp", "ctx"), None),
        P(("dp", "ctx"), "tp"),
        P("tp", ("dp", "ctx"), None),
        P(),
        P(("dp", "ctx"), None, "tp"),
        P("tp", ("dp", "ctx"), None),
        P(("dp", "ctx"), "tp"),
        P("tp", ("dp", "ctx"), None),
        P(),
    )
    out_specs = (
        P(("dp", "ctx"), None),
        P(("dp", "ctx"), None),
        P(("dp", "ctx"), None, "tp"),
        P("tp", ("dp", "ctx"), None),
        P(("dp", "ctx"), "tp"),
        P("tp", ("dp", "ctx"), None),
        P(),
        P(("dp", "ctx"), None, "tp"),
        P("tp", ("dp", "ctx"), None),
        P(("dp", "ctx"), "tp"),
        P("tp", ("dp", "ctx"), None),
        P(),
        P(("dp", "ctx"), None, "tp"),
        P("tp", ("dp", "ctx"), None),
        P(("dp", "ctx"), "tp"),
        P("tp", ("dp", "ctx"), None),
        P(),
    )
    return jax.shard_map(shards, mesh=mesh, in_specs=in_specs, out_specs=out_specs, check_vma=False)
```
